512 devices in a mesh: mem: 16 (over y, core), space: 32 (over z, x).
Axes of the slice: x: 4, y: 8, z: 8, core: 2. Of those that a mesh axis runs over, the one named last changes fastest.
Arguments:
- ensemble: bfloat16 [16, 896, 2048], P('mem', 'space'), may hold values from -4 to 4
- decay_rate: float32 [896, 2048], P('space'), may hold values from 0 to 1, as said below
- innovation: float32 [896, 2048], P('space'), may hold values from -6 to 6
- obs_weight: float32 [896, 2048], P('space'), may hold values from 0.25 to 4
Outputs:
- control: float32 [16, 896, 2048], P('mem', 'space')
- increment: float32 [896, 2048], P('space')
The draws below stay inside these ranges and needn't reach their ends.
Inputs may be any that keep to these rules, and one draw needn't show every extreme that they name: `decay_rate`: every entry lies strictly between 0 and 1.
All inputs are finite; a program needn't handle non-finite values.
Results may differ from the reference program's by a relative error of at most 0.0003.
Values sent between devices are 32-bit elements; how exact they have to be, the bound alone decides.
No kernel may reach another device: no remote copies, remote signals or barrier semaphores. Data moves between devices by JAX's collectives and lax.ppermute only.
A program may use at most 64 MiB of HBM per device.

```python
import math
import jax
import jax.numpy as jnp
from jax import lax

YW = 256
LEVELS = 8
ITERS = 2
MEMBERS = 16
FILTER_COLUMNS = 896
LINES = 2048


def draw_decay_rate(key, part):
    key = jax.random.fold_in(key, 7)
    segment_parts = jax.random.split(key, 4)
    length = jax.random.uniform(segment_parts[0], (1, LEVELS * YW), minval=math.log(0.03), maxval=math.log(8.0))
    length_cells = jnp.exp(length) * FILTER_COLUMNS
    roughness = jnp.exp(jax.random.uniform(segment_parts[1], (FILTER_COLUMNS, LEVELS * YW), minval=-0.5, maxval=0.5))
    steady = jnp.exp(-1.0 / (length_cells * roughness))
    spike_position = jax.random.randint(segment_parts[2], (4,), 0, FILTER_COLUMNS)
    spike_retained = jax.random.uniform(segment_parts[3], (4,), minval=0.5, maxval=0.8)
    index_of_row = jnp.arange(FILTER_COLUMNS)[:, None]
    multiplier_value = jnp.prod(jnp.where(index_of_row == spike_position[None, :], spike_retained[None, :], 1.0), axis=1)
    return (steady * multiplier_value[:, None]).astype(jnp.float32)


def level_of(own_key, extent, shards, least, largest):
    loudness, own = 1.0, jax.random.fold_in(own_key, 6)
    for dim, parts in shards:
        steps = jnp.exp(jax.random.uniform(jax.random.fold_in(own, dim), (parts,), jnp.float32, least / len(shards), largest / len(shards)))
        loudness = loudness * jnp.repeat(steps, extent[dim] // parts).reshape([-1 if axis == dim else 1 for axis in range(len(extent))])
    return loudness


def noise(stream_key, dims, width, most, pieces=(), kind=jnp.bfloat16):
    drawn = width * jax.random.normal(stream_key, dims, jnp.float32)
    if pieces:
        drawn = drawn * level_of(stream_key, dims, pieces, -0.22, 0.18)
    return jnp.clip(drawn, -most, most).astype(kind)


def setup_inputs(seed: int = 0) -> dict:
    arg_keys = jax.random.split(jax.random.key(seed), 5)
    ensemble = noise(arg_keys[0], (MEMBERS, FILTER_COLUMNS, LINES), (1.0 / MEMBERS ** 0.5), 4.0, ((0, 16), (1, 32)))
    decay_rate = draw_decay_rate(jax.random.fold_in(arg_keys[4], 71), 0)
    innovation = noise(arg_keys[2], (FILTER_COLUMNS, LINES), 1.0, 6.0, ((0, 32),), jnp.float32)
    obs_weight = jnp.clip(jnp.exp(math.log(4.0) - 2.7725887 * jax.random.uniform(arg_keys[3], (FILTER_COLUMNS, LINES), jnp.float32) ** level_of(arg_keys[3], (FILTER_COLUMNS, LINES), ((0, 32),), -0.2, 0.2)), 0.25, 4.0)
    return {"ensemble": ensemble, "decay_rate": decay_rate, "innovation": innovation, "obs_weight": obs_weight}


def advance(values, decay_rate, signal_amplitude):

    def recur(state, inputs):
        rate, scale, column = inputs
        state = rate * state + scale * column
        return (state, state)
    start = jnp.zeros((values.shape[0], values.shape[2]), jnp.float32)
    _, output = lax.scan(recur, start, (decay_rate, signal_amplitude, jnp.moveaxis(values, 1, 0)))
    return jnp.moveaxis(output, 0, 1)

def retreat(values, decay_rate, signal_amplitude):

    def recur(carry_in, inputs):
        rate, scale, column = inputs
        summed = column + carry_in
        return (rate * summed, scale * summed)
    start = jnp.zeros((values.shape[0], values.shape[2]), jnp.float32)
    _, output = lax.scan(recur, start, (decay_rate, signal_amplitude, jnp.moveaxis(values, 1, 0)), reverse=True)
    return jnp.moveaxis(output, 0, 1)

def hessian(direction, members, decay_rate, signal_amplitude, obs_weight):
    filtered = advance(direction, decay_rate, signal_amplitude)
    field_part = lax.optimization_barrier(jnp.sum(members * filtered, axis=0))
    weighted = obs_weight * field_part
    return (field_part, direction + retreat(members * weighted[None], decay_rate, signal_amplitude))

def reference(ensemble, decay_rate, innovation, obs_weight):
    signal_amplitude = jnp.sqrt((1.0 - decay_rate) * (1.0 + decay_rate))
    members = ensemble.astype(jnp.float32)
    rhs = retreat(members * (obs_weight * innovation)[None], decay_rate, signal_amplitude)
    control = jnp.zeros_like(rhs)
    increment = jnp.zeros_like(innovation)
    residual = rhs
    direction = rhs
    norm_now = jnp.sum(residual * residual)
    for repeat in range(ITERS):
        field_part, hessian_times_direction = hessian(direction, members, decay_rate, signal_amplitude, obs_weight)
        step_size = norm_now / jnp.sum(direction * hessian_times_direction)
        control = control + step_size * direction
        increment = increment + step_size * field_part
        residual = residual - step_size * hessian_times_direction
        norm_next = jnp.sum(residual * residual)
        direction = residual + norm_next / norm_now * direction
        norm_now = norm_next
    return (control, increment)
```

```python
import jax
import jax.numpy as jnp
from jax import lax
from jax.experimental import pallas as pl
from jax.experimental.pallas import tpu as pltpu
from jax.sharding import PartitionSpec as P

MEMBERS, TILES, COLS, LINES = 16, 32, 28, 4
DEVICES = MEMBERS * TILES
ROWS = 32
LANES = 128
BLOCKS = DEVICES // LANES
VMEM = pl.BlockSpec(memory_space=pltpu.VMEM)


def lane_block(line, block):
    start = line * DEVICES + block * LANES
    return slice(start, start + LANES)


def pack(place, ensemble_ref, decay_ref, innovation_ref, weight_ref, out_ref, rows_ref):
    rows_ref[:COLS, :] = ensemble_ref[0].astype(jnp.float32) * jnp.sqrt(weight_ref[...])
    quarter = lax.rem(place, 8)
    start = pl.multiple_of(8 * jnp.minimum(lax.div(quarter, 2), 2), 8)

    def four(ref):
        eight = ref[pl.ds(start, 8), :]
        inner = jnp.where(lax.rem(quarter, 2) == 0, eight[:4], eight[4:])
        return jnp.where(quarter >= 6, ref[COLS - 4 :, :], inner)

    scaled = jnp.sqrt(four(weight_ref)) * four(innovation_ref)
    rows_ref[COLS:, :] = jnp.where(place < 8, four(decay_ref), scaled)
    for block in range(BLOCKS):
        piece = jnp.concatenate([rows_ref[:, lane_block(line, block)] for line in range(LINES)], axis=0)
        out_ref[block * LANES : (block + 1) * LANES, :] = piece.T


def spread(piece, lane_group):
    turned = [piece] + [pltpu.roll(piece, 32 * k, 1) for k in (1, 2, 3)]
    out = []
    for source in range(4):
        value = turned[(3 - source) % 4]
        for group in (2, 1, 0):
            value = jnp.where(lane_group == group, turned[(group - source) % 4], value)
        out.append(value)
    return out


def own_lines(in_ref, out_ref, rows_ref, fields_ref, state_ref, first_ref, sums_ref):
    for block in range(BLOCKS):
        piece = slice(block * LANES, (block + 1) * LANES)
        rows_ref[piece, :] = in_ref[piece, :].T

    lane = lax.broadcasted_iota(jnp.int32, (8, LANES), 1)
    sub = lax.broadcasted_iota(jnp.int32, (8, LANES), 0)
    tile, lane_group = lane % TILES, lane // TILES
    low = sub < 4

    def column(c):
        value = rows_ref[pl.ds(c, 16, stride=ROWS), :]
        return value[:8], value[8:]

    RATE, SQUARED, AFTER, UPTO, INNOV, Z0, Z1 = range(7)

    def field(kind, c):
        return fields_ref[kind, c]

    for j in range(4):
        for kind, value in zip((RATE, INNOV), column(COLS + j)):
            other = pltpu.roll(value, 4, 0)
            for half, both in enumerate((jnp.where(low, value, other), jnp.where(low, other, value))):
                for source, copied in enumerate(spread(both, lane_group)):
                    c = 16 * half + 4 * source + j
                    if c < COLS:
                        fields_ref[kind, c] = copied

    one = jnp.ones((8, LANES), jnp.float32)
    upto, after = one, one
    for c in range(COLS):
        rate = field(RATE, c)
        fields_ref[SQUARED, c] = (1.0 - rate) * (1.0 + rate)
        upto = upto * rate
        fields_ref[UPTO, c] = upto
        fields_ref[AFTER, COLS - 1 - c] = after
        after = after * field(RATE, COLS - 1 - c)

    steps = (1, 2, 4, 8, 16)
    back, forth = [], []
    to_left, to_right = upto, upto
    for k in steps:
        back.append(jnp.where(tile < TILES - k, to_left, 0.0))
        to_left = back[-1] * pltpu.roll(to_left, LANES - k, 1)
        forth.append(jnp.where(tile >= k, to_right, 0.0))
        to_right = forth[-1] * pltpu.roll(to_right, k, 1)

    def entering(values, backward):
        out = []
        for value in values:
            for k, factor in zip(steps, back if backward else forth):
                value = value + factor * pltpu.roll(value, LANES - k if backward else k, 1)
            if backward:
                out.append(jnp.where(tile < TILES - 1, pltpu.roll(value, LANES - 1, 1), 0.0))
            else:
                out.append(jnp.where(tile >= 1, pltpu.roll(value, 1, 1), 0.0))
        return out

    def apply(source, target, on_state):
        zero = jnp.zeros((8, LANES), jnp.float32)
        carry = [zero, zero]
        for c in reversed(range(COLS)):
            rate, weight = field(RATE, c), field(source, c)
            for i, member in enumerate(column(c)):
                summed = member * weight + carry[i]
                state_ref[c, i] = summed
                carry[i] = rate * summed
        from_right = entering(carry, True)
        state = [zero, zero]
        for c in range(COLS):
            rate, squared, after = field(RATE, c), field(SQUARED, c), field(AFTER, c)
            for i in range(2):
                summed = state_ref[c, i] + after * from_right[i]
                driven = squared * summed
                on_state(c, i, summed, driven)
                state[i] = rate * state[i] + driven
                state_ref[c, i] = state[i]
        from_left = entering(state, False)
        for c in range(COLS):
            upto, members = field(UPTO, c), column(c)
            total = sum(members[i] * (state_ref[c, i] + upto * from_left[i]) for i in range(2))
            total = total + pltpu.roll(total, 4, 0)
            total = total + pltpu.roll(total, 64, 1)
            total = total + pltpu.roll(total, 32, 1)
            fields_ref[target, c] = total
        return from_right

    def whole(value):
        return jnp.sum(jnp.sum(value, axis=0, keepdims=True), axis=1, keepdims=True)

    squares = [jnp.zeros((8, LANES), jnp.float32)] * 2

    def keep(c, i, summed, driven):
        first_ref[c, i] = summed
        squares[i] = squares[i] + summed * driven

    right0 = apply(INNOV, Z0, keep)
    alpha = whole(squares[0] + squares[1])
    beta = jnp.zeros((8, LANES), jnp.float32)
    for c in range(COLS):
        beta = beta + field(Z0, c) * field(Z0, c)
    beta = 0.125 * whole(beta)
    ratio = jnp.where(alpha > 0.0, beta / jnp.where(alpha > 0.0, alpha, 1.0), 0.0)
    ratio = jnp.broadcast_to(ratio, (8, LANES))

    rest = [jnp.zeros((8, LANES), jnp.float32)] * 2

    def orthogonal(c, i, summed, driven):
        part = summed - ratio * first_ref[c, i]
        rest[i] = rest[i] + field(SQUARED, c) * part * part

    right1 = apply(Z0, Z1, orthogonal)
    kappa = whole(rest[0] + rest[1])
    energy = jnp.zeros((8, LANES), jnp.float32)
    cross = energy
    for c in range(COLS):
        part = field(Z1, c) - ratio * field(Z0, c)
        energy = energy + part * part
        cross = cross + part * field(Z0, c)
    energy, cross = 0.125 * whole(energy), 0.125 * whole(cross)

    def put(row, values):
        rows_ref[pl.ds(row, 16, stride=ROWS), :] = jnp.concatenate(values, axis=0)

    line = sub % 4
    scalars = jnp.where(line == 0, alpha, jnp.where(line == 1, beta, jnp.where(line == 2, kappa, energy)))
    others = jnp.where(line == 0, cross, 0.0)
    for c in range(COLS):
        put(c, [field(Z0, c)] * 2)
    put(COLS, right0)
    put(COLS + 1, right1)
    put(COLS + 2, [scalars] * 2)
    put(COLS + 3, [others] * 2)
    for c in range(COLS):
        sums_ref[pl.ds(c, 4, stride=ROWS), :] = field(Z1, c)[:4]
    for r in range(COLS, ROWS):
        sums_ref[pl.ds(r, 4, stride=ROWS), :] = jnp.zeros((4, LANES), jnp.float32)
    second = sums_ref[...].T
    for block in range(BLOCKS):
        first = rows_ref[block * LANES : (block + 1) * LANES, :].T
        out_ref[pl.ds(2 * block * LANES, LANES, stride=2), :] = first
        out_ref[pl.ds(2 * block * LANES + 1, LANES, stride=2), :] = second


def finish(in_ref, ensemble_ref, decay_ref, innovation_ref, weight_ref, control_ref, increment_ref,
           first_ref, second_ref, driven_ref, rate_ref):
    for block in range(BLOCKS):
        for half, ref in enumerate((first_ref, second_ref)):
            piece = in_ref[pl.ds(2 * block * LANES + half, LANES, stride=2), :].T
            for line in range(LINES):
                ref[:, lane_block(line, block)] = piece[line * ROWS : (line + 1) * ROWS]

    def scalar(row, line):
        return first_ref[row : row + 1, line * DEVICES : (line + 1) * DEVICES]

    def whole(value):
        return jnp.sum(value, axis=1, keepdims=True)

    alphas, betas, kappas, energies = (scalar(COLS + 2, line) for line in range(LINES))
    crosses = scalar(COLS + 3, 0)
    alpha, beta = whole(alphas), whole(betas)
    ratio = beta / alpha
    shift = jnp.where(alphas > 0.0, betas / jnp.where(alphas > 0.0, alphas, 1.0), 0.0) - ratio
    kappa = whole(kappas + alphas * shift * shift)
    energy = whole(energies + shift * (2.0 * crosses + shift * betas))
    step = alpha / (alpha + beta)
    curvature = kappa + energy - step * kappa * (kappa / alpha)
    back = jnp.where(curvature > 0.0, step * kappa / jnp.where(curvature > 0.0, curvature, 1.0), 0.0)
    ahead = step + back * (ratio + step * (kappa / alpha))

    root = jnp.sqrt(weight_ref[...])
    z0 = first_ref[:COLS, :]
    increment_ref[...] = (ahead * z0 - back * second_ref[:COLS, :]) / root
    scaled = root * (ahead * (root * innovation_ref[...]) - back * z0)
    driven = ensemble_ref[0].astype(jnp.float32) * scaled
    groups = LINES * DEVICES // LANES
    carry = []
    for g in range(groups):
        part = slice(g * LANES, (g + 1) * LANES)
        driven_ref[pl.ds(g, COLS, stride=groups), :] = driven[:, part]
        rate_ref[pl.ds(g, COLS, stride=groups), :] = decay_ref[:, part]
        carry.append(ahead * first_ref[COLS : COLS + 1, part] - back * first_ref[COLS + 1 : COLS + 2, part])
    carry = jnp.concatenate(carry, axis=0)
    for c in reversed(range(COLS)):
        part = slice(c * groups, (c + 1) * groups)
        rate = rate_ref[part, :]
        summed = driven_ref[part, :] + carry
        carry = rate * summed
        driven_ref[part, :] = jnp.sqrt((1.0 - rate) * (1.0 + rate)) * summed
    for g in range(groups):
        control_ref[0, :, g * LANES : (g + 1) * LANES] = driven_ref[pl.ds(g, COLS, stride=groups), :]


def shape(*dims):
    return jax.ShapeDtypeStruct(dims, jnp.float32)


def scratch(*dims):
    return pltpu.VMEM(dims, jnp.float32)


def call(kernel, out_shape, scratch_shapes, inputs):
    one = not isinstance(out_shape, tuple)
    return pl.pallas_call(
        kernel,
        out_shape=out_shape,
        in_specs=[VMEM] * inputs,
        out_specs=VMEM if one else (VMEM,) * len(out_shape),
        scratch_shapes=scratch_shapes,
        compiler_params=pltpu.CompilerParams(vmem_limit_bytes=32 * 1024 * 1024),
    )


def pack_here(*refs):
    pack(lax.axis_index("mem"), *refs)


def own_call(received):
    return call(
        own_lines,
        shape(2 * DEVICES, LANES),
        [
            scratch(DEVICES, LANES),
            scratch(7, COLS, 8, LANES),
            scratch(COLS, 2, 8, LANES),
            scratch(COLS, 2, 8, LANES),
            scratch(LANES, LANES),
        ],
        1,
    )(received)


def finish_call(received, *args):
    width = LINES * DEVICES
    return call(
        finish,
        (shape(1, COLS, width), shape(COLS, width)),
        [scratch(ROWS, width), scratch(ROWS, width)] + [scratch(COLS * width // LANES, LANES)] * 2,
        5,
    )(received, *args)


def on_device(ensemble, decay_rate, innovation, obs_weight):
    args = (ensemble, decay_rate, innovation, obs_weight)
    axes = ("mem", "space")
    sent = call(pack_here, shape(DEVICES, LANES), [scratch(ROWS, LINES * DEVICES)], 4)(*args)
    received = lax.all_to_all(sent, axes, 0, 0, tiled=True)
    results = own_call(received).reshape(DEVICES, 2, LANES)
    returned = lax.all_to_all(results, axes, 0, 0, tiled=True)
    return finish_call(returned.reshape(2 * DEVICES, LANES), *args)


def solution(mesh):
    in_specs = (P("mem", "space", None), P("space", None), P("space", None), P("space", None))
    out_specs = (P("mem", "space", None), P("space", None))
    return jax.shard_map(
        on_device, mesh=mesh, in_specs=in_specs, out_specs=out_specs, check_vma=False
    )
```

```python
import jax
import jax.numpy as jnp
from jax import lax
from jax.experimental import pallas as pl
from jax.experimental.pallas import tpu as pltpu
from jax.sharding import PartitionSpec as P

MEMBERS, TILES, COLS, LINES = 16, 32, 28, 4
DEVICES = MEMBERS * TILES
ROWS = 32
LANES = 128
BLOCKS = DEVICES // LANES
VMEM = pl.BlockSpec(memory_space=pltpu.VMEM)


def lane_block(line, block):
    start = line * DEVICES + block * LANES
    return slice(start, start + LANES)


def pack(place, ensemble_hbm, decay_hbm, innovation_hbm, weight_hbm, out_ref,
         ensemble_ref, decay_ref, innovation_ref, weight_ref, rows_ref, sems):
    pairs = (
        (ensemble_hbm, ensemble_ref), (weight_hbm, weight_ref), (decay_hbm, decay_ref), (innovation_hbm, innovation_ref)
    )
    copies = [pltpu.make_async_copy(*pair, sems.at[i]) for i, pair in enumerate(pairs)]
    for copy in copies:
        copy.start()
    for copy in copies:
        copy.wait()
    rows_ref[:COLS, :] = ensemble_ref[0].astype(jnp.float32) * jnp.sqrt(weight_ref[...])
    quarter = lax.rem(place, 8)
    start = pl.multiple_of(8 * jnp.minimum(lax.div(quarter, 2), 2), 8)

    def four(ref):
        eight = ref[pl.ds(start, 8), :]
        inner = jnp.where(lax.rem(quarter, 2) == 0, eight[:4], eight[4:])
        return jnp.where(quarter >= 6, ref[COLS - 4 :, :], inner)

    scaled = jnp.sqrt(four(weight_ref)) * four(innovation_ref)
    rows_ref[COLS:, :] = jnp.where(place < 8, four(decay_ref), scaled)
    for block in range(BLOCKS):
        piece = jnp.concatenate([rows_ref[:, lane_block(line, block)] for line in range(LINES)], axis=0)
        out_ref[block * LANES : (block + 1) * LANES, :] = piece.T


def spread(piece, lane_group):
    turned = [piece] + [pltpu.roll(piece, 32 * k, 1) for k in (1, 2, 3)]
    out = []
    for source in range(4):
        value = turned[(3 - source) % 4]
        for group in (2, 1, 0):
            value = jnp.where(lane_group == group, turned[(group - source) % 4], value)
        out.append(value)
    return out


def own_lines(in_ref, out_ref, rows_ref, fields_ref, state_ref, first_ref):
    for block in range(BLOCKS):
        piece = slice(block * LANES, (block + 1) * LANES)
        rows_ref[piece, :] = in_ref[piece, :].T

    lane = lax.broadcasted_iota(jnp.int32, (8, LANES), 1)
    sub = lax.broadcasted_iota(jnp.int32, (8, LANES), 0)
    tile, lane_group = lane % TILES, lane // TILES
    low = sub < 4

    def column(c):
        value = rows_ref[pl.ds(c, 16, stride=ROWS), :]
        return value[:8], value[8:]

    RATE, SQUARED, AFTER, UPTO, INNOV, Z0, Z1 = range(7)

    def field(kind, c):
        return fields_ref[kind, c]

    for j in range(4):
        for kind, value in zip((RATE, INNOV), column(COLS + j)):
            other = pltpu.roll(value, 4, 0)
            for half, both in enumerate((jnp.where(low, value, other), jnp.where(low, other, value))):
                for source, copied in enumerate(spread(both, lane_group)):
                    c = 16 * half + 4 * source + j
                    if c < COLS:
                        fields_ref[kind, c] = copied

    one = jnp.ones((8, LANES), jnp.float32)
    upto, after = one, one
    for c in range(COLS):
        rate = field(RATE, c)
        fields_ref[SQUARED, c] = (1.0 - rate) * (1.0 + rate)
        upto = upto * rate
        fields_ref[UPTO, c] = upto
        fields_ref[AFTER, COLS - 1 - c] = after
        after = after * field(RATE, COLS - 1 - c)

    steps = (1, 2, 4, 8, 16)
    back, forth = [], []
    to_left, to_right = upto, upto
    for k in steps:
        back.append(jnp.where(tile < TILES - k, to_left, 0.0))
        to_left = back[-1] * pltpu.roll(to_left, LANES - k, 1)
        forth.append(jnp.where(tile >= k, to_right, 0.0))
        to_right = forth[-1] * pltpu.roll(to_right, k, 1)

    def entering(values, backward):
        out = []
        for value in values:
            for k, factor in zip(steps, back if backward else forth):
                value = value + factor * pltpu.roll(value, LANES - k if backward else k, 1)
            if backward:
                out.append(jnp.where(tile < TILES - 1, pltpu.roll(value, LANES - 1, 1), 0.0))
            else:
                out.append(jnp.where(tile >= 1, pltpu.roll(value, 1, 1), 0.0))
        return out

    def apply(source, target, on_state):
        zero = jnp.zeros((8, LANES), jnp.float32)
        carry = [zero, zero]
        for c in reversed(range(COLS)):
            rate, weight = field(RATE, c), field(source, c)
            for i, member in enumerate(column(c)):
                summed = member * weight + carry[i]
                state_ref[c, i] = summed
                carry[i] = rate * summed
        from_right = entering(carry, True)
        state = [zero, zero]
        for c in range(COLS):
            rate, squared, after = field(RATE, c), field(SQUARED, c), field(AFTER, c)
            for i in range(2):
                summed = state_ref[c, i] + after * from_right[i]
                driven = squared * summed
                on_state(c, i, summed, driven)
                state[i] = rate * state[i] + driven
                state_ref[c, i] = state[i]
        from_left = entering(state, False)
        for c in range(COLS):
            upto, members = field(UPTO, c), column(c)
            total = sum(members[i] * (state_ref[c, i] + upto * from_left[i]) for i in range(2))
            total = total + pltpu.roll(total, 4, 0)
            total = total + pltpu.roll(total, 64, 1)
            total = total + pltpu.roll(total, 32, 1)
            fields_ref[target, c] = total
        return from_right

    def whole(value):
        return jnp.sum(jnp.sum(value, axis=0, keepdims=True), axis=1, keepdims=True)

    squares = [jnp.zeros((8, LANES), jnp.float32)] * 2

    def keep(c, i, summed, driven):
        first_ref[c, i] = summed
        squares[i] = squares[i] + summed * driven

    right0 = apply(INNOV, Z0, keep)
    alpha = whole(squares[0] + squares[1])
    beta = jnp.zeros((8, LANES), jnp.float32)
    for c in range(COLS):
        beta = beta + field(Z0, c) * field(Z0, c)
    beta = 0.125 * whole(beta)
    ratio = jnp.where(alpha > 0.0, beta / jnp.where(alpha > 0.0, alpha, 1.0), 0.0)
    ratio = jnp.broadcast_to(ratio, (8, LANES))

    rest = [jnp.zeros((8, LANES), jnp.float32)] * 2

    def orthogonal(c, i, summed, driven):
        part = summed - ratio * first_ref[c, i]
        rest[i] = rest[i] + field(SQUARED, c) * part * part

    right1 = apply(Z0, Z1, orthogonal)
    kappa = whole(rest[0] + rest[1])
    energy = jnp.zeros((8, LANES), jnp.float32)
    cross = energy
    for c in range(COLS):
        part = field(Z1, c) - ratio * field(Z0, c)
        energy = energy + part * part
        cross = cross + part * field(Z0, c)
    energy, cross = 0.125 * whole(energy), 0.125 * whole(cross)

    def put(row, values):
        rows_ref[pl.ds(row, 16, stride=ROWS), :] = jnp.concatenate(values, axis=0)

    line = sub % 4
    scalars = jnp.where(line == 0, alpha, jnp.where(line == 1, beta, jnp.where(line == 2, kappa, energy)))
    others = jnp.where(line == 0, cross, 0.0)
    even = lane_group % 2 == 0
    for c in range(COLS):
        put(c, [jnp.where(even, field(Z0, c), field(Z1, c))] * 2)
    put(COLS, right0)
    put(COLS + 1, right1)
    put(COLS + 2, [scalars] * 2)
    put(COLS + 3, [others] * 2)
    for block in range(BLOCKS):
        piece = slice(block * LANES, (block + 1) * LANES)
        out_ref[piece, :] = rows_ref[piece, :].T


def unpack(in_ref, out_ref):
    for block in range(BLOCKS):
        piece = in_ref[block * LANES : (block + 1) * LANES, :].T
        for line in range(LINES):
            out_ref[:, lane_block(line, block)] = piece[line * ROWS : (line + 1) * ROWS]


def finish(place, own_ref, in_ref, ensemble_ref, decay_ref, innovation_ref, weight_ref, control_ref, increment_ref,
           other_ref, rate_ref):
    unpack(in_ref, other_ref)
    even = lax.rem(place, 2) == 0

    def scalar(row, line):
        return own_ref[row : row + 1, line * DEVICES : (line + 1) * DEVICES]

    def whole(value):
        return jnp.sum(value, axis=1, keepdims=True)

    alphas, betas, kappas, energies = (scalar(COLS + 2, line) for line in range(LINES))
    crosses = scalar(COLS + 3, 0)
    alpha, beta = whole(alphas), whole(betas)
    ratio = beta / alpha
    shift = jnp.where(alphas > 0.0, betas / jnp.where(alphas > 0.0, alphas, 1.0), 0.0) - ratio
    kappa = whole(kappas + alphas * shift * shift)
    energy = whole(energies + shift * (2.0 * crosses + shift * betas))
    step = alpha / (alpha + beta)
    curvature = kappa + energy - step * kappa * (kappa / alpha)
    back = jnp.where(curvature > 0.0, step * kappa / jnp.where(curvature > 0.0, curvature, 1.0), 0.0)
    ahead = step + back * (ratio + step * (kappa / alpha))

    root = jnp.sqrt(weight_ref[...])
    own, other = own_ref[:COLS, :], other_ref[:COLS, :]
    z0, z1 = jnp.where(even, own, other), jnp.where(even, other, own)
    increment_ref[...] = (ahead * z0 - back * z1) / root
    scaled = root * (ahead * (root * innovation_ref[...]) - back * z0)
    driven = ensemble_ref[0].astype(jnp.float32) * scaled
    groups = LINES * DEVICES // LANES
    carry = []
    for g in range(groups):
        part = slice(g * LANES, (g + 1) * LANES)
        control_ref[pl.ds(g, COLS, stride=groups), :] = driven[:, part]
        rate_ref[pl.ds(g, COLS, stride=groups), :] = decay_ref[:, part]
        carry.append(ahead * own_ref[COLS : COLS + 1, part] - back * own_ref[COLS + 1 : COLS + 2, part])
    carry = jnp.concatenate(carry, axis=0)
    for c in reversed(range(COLS)):
        part = slice(c * groups, (c + 1) * groups)
        rate = rate_ref[part, :]
        summed = control_ref[part, :] + carry
        carry = rate * summed
        control_ref[part, :] = jnp.sqrt((1.0 - rate) * (1.0 + rate)) * summed


def shape(*dims):
    return jax.ShapeDtypeStruct(dims, jnp.float32)


def scratch(*dims):
    return pltpu.VMEM(dims, jnp.float32)


def call(kernel, out_shape, scratch_shapes, in_specs, limit=32 * 1024 * 1024):
    one = not isinstance(out_shape, tuple)
    return pl.pallas_call(
        kernel,
        out_shape=out_shape,
        in_specs=in_specs,
        out_specs=VMEM if one else (VMEM,) * len(out_shape),
        scratch_shapes=scratch_shapes,
        compiler_params=pltpu.CompilerParams(vmem_limit_bytes=limit),
    )


WIDTH = LINES * DEVICES


def pack_call(place, *args):
    return call(
        lambda *refs: pack(place(), *refs),
        shape(DEVICES, LANES),
        [pltpu.VMEM((1, COLS, WIDTH), jnp.bfloat16)]
        + [scratch(COLS, WIDTH)] * 3
        + [scratch(ROWS, WIDTH), pltpu.SemaphoreType.DMA((4,))],
        [pl.BlockSpec(memory_space=pltpu.HBM)] * 4,
        limit=32 * 1024 * 1024,
    )(*(pltpu.with_memory_space_constraint(a, pltpu.HBM) for a in args))


def own_call(received):
    return call(
        own_lines,
        shape(DEVICES, LANES),
        [
            scratch(DEVICES, LANES),
            scratch(7, COLS, 8, LANES),
            scratch(COLS, 2, 8, LANES),
            scratch(COLS, 2, 8, LANES),
        ],
        [VMEM],
    )(received)


def unpack_call(received):
    return call(unpack, shape(ROWS, WIDTH), [], [VMEM])(received)


def finish_call(place, own, received, *args):
    return call(
        lambda *refs: finish(place(), *refs),
        (shape(COLS * WIDTH // LANES, LANES), shape(COLS, WIDTH)),
        [scratch(ROWS, WIDTH), scratch(COLS * WIDTH // LANES, LANES)],
        [VMEM] * 6,
    )(own, received, *args)


def on_device(ensemble, decay_rate, innovation, obs_weight):
    args = (ensemble, decay_rate, innovation, obs_weight)
    axes = ("mem", "space")
    place = lambda: lax.axis_index("mem")
    sent = pack_call(place, *args)
    received = lax.all_to_all(sent, axes, 0, 0, tiled=True)
    returned = lax.all_to_all(own_call(received), axes, 0, 0, tiled=True)
    other = lax.ppermute(returned, "mem", [(k, k ^ 1) for k in range(MEMBERS)])
    control, increment = finish_call(place, unpack_call(returned), other, *args)
    return control.reshape(1, COLS, WIDTH), increment


def solution(mesh):
    in_specs = (P("mem", "space", None), P("space", None), P("space", None), P("space", None))
    out_specs = (P("mem", "space", None), P("space", None))
    return jax.shard_map(
        on_device, mesh=mesh, in_specs=in_specs, out_specs=out_specs, check_vma=False
    )
```

```python
import jax
import jax.numpy as jnp
from jax import lax
from jax.experimental import pallas as pl
from jax.experimental.pallas import tpu as pltpu
from jax.sharding import PartitionSpec as P

MEMBERS, TILES, COLS, LINES = 16, 32, 28, 4
DEVICES = MEMBERS * TILES
ROWS = 32
LANES = 128
BLOCKS = DEVICES // LANES
GROUPS = LINES * BLOCKS
WIDTH = LINES * DEVICES
NEAR = 8
SCALARS = tuple(line * ROWS + COLS + 2 for line in range(LINES)) + (COLS + 3,)
VMEM = pl.BlockSpec(memory_space=pltpu.VMEM)
HBM = pl.BlockSpec(memory_space=pltpu.HBM)


def lane_block(line, block):
    start = line * DEVICES + block * LANES
    return slice(start, start + LANES)


def pack(place, ensemble_hbm, decay_hbm, innovation_hbm, weight_hbm, out_ref,
         ensemble_ref, decay_ref, innovation_ref, weight_ref, rows_ref, sems):
    pairs = (
        (ensemble_hbm, ensemble_ref), (weight_hbm, weight_ref), (decay_hbm, decay_ref), (innovation_hbm, innovation_ref)
    )
    copies = [pltpu.make_async_copy(*pair, sems.at[i]) for i, pair in enumerate(pairs)]
    for copy in copies:
        copy.start()
    for copy in copies:
        copy.wait()
    rows_ref[:COLS, :] = ensemble_ref[0].astype(jnp.float32) * jnp.sqrt(weight_ref[...])
    quarter = lax.rem(place, 8)
    start = pl.multiple_of(8 * jnp.minimum(lax.div(quarter, 2), 2), 8)

    def four(ref):
        eight = ref[pl.ds(start, 8), :]
        inner = jnp.where(lax.rem(quarter, 2) == 0, eight[:4], eight[4:])
        return jnp.where(quarter >= 6, ref[COLS - 4 :, :], inner)

    scaled = jnp.sqrt(four(weight_ref)) * four(innovation_ref)
    rows_ref[COLS:, :] = jnp.where(place < 8, four(decay_ref), scaled)
    for block in range(BLOCKS):
        piece = jnp.concatenate([rows_ref[:, lane_block(line, block)] for line in range(LINES)], axis=0)
        out_ref[block * LANES : (block + 1) * LANES, :] = piece.T


def spread(piece, lane_group):
    turned = [piece] + [pltpu.roll(piece, 32 * k, 1) for k in (1, 2, 3)]
    out = []
    for source in range(4):
        value = turned[(3 - source) % 4]
        for group in (2, 1, 0):
            value = jnp.where(lane_group == group, turned[(group - source) % 4], value)
        out.append(value)
    return out


def own_lines(in_ref, out_ref, rows_ref, members_ref, fields_ref, state_ref, first_ref):
    for block in range(BLOCKS):
        piece = slice(block * LANES, (block + 1) * LANES)
        rows_ref[piece, :] = in_ref[piece, :].T

    lane = lax.broadcasted_iota(jnp.int32, (8, LANES), 1)
    sub = lax.broadcasted_iota(jnp.int32, (8, LANES), 0)
    tile, lane_group = lane % TILES, lane // TILES
    low = sub < 4
    zero = jnp.zeros((8, LANES), jnp.float32)

    for c in range(COLS):
        value = rows_ref[pl.ds(c, 16, stride=ROWS), :]
        members_ref[c, 0], members_ref[c, 1] = value[:8], value[8:]

    RATE, SQUARED, AFTER, UPTO, INNOV, Z0, Z1 = range(7)

    def field(kind, c):
        return fields_ref[kind, c]

    for j in range(4):
        given = rows_ref[pl.ds(COLS + j, 16, stride=ROWS), :]
        for kind, value in ((RATE, given[:8]), (INNOV, given[8:])):
            other = pltpu.roll(value, 4, 0)
            for half, both in enumerate((jnp.where(low, value, other), jnp.where(low, other, value))):
                for source, copied in enumerate(spread(both, lane_group)):
                    c = 16 * half + 4 * source + j
                    if c < COLS:
                        fields_ref[kind, c] = copied

    upto, after = zero + 1.0, zero + 1.0
    for c in range(COLS):
        rate = field(RATE, c)
        fields_ref[SQUARED, c] = (1.0 - rate) * (1.0 + rate)
        upto = upto * rate
        fields_ref[UPTO, c] = upto
        fields_ref[AFTER, COLS - 1 - c] = after
        after = after * field(RATE, COLS - 1 - c)

    def turn(value, k, backward):
        return pltpu.roll(value, LANES - k if backward else k, 1)

    def inside(k, backward):
        return tile < TILES - k if backward else tile >= k

    def factors(backward):
        near, product = [], zero + 1.0
        for k in range(1, NEAR + 1):
            near.append((k, jnp.where(inside(k, backward), product, 0.0)))
            product = product * turn(upto, k, backward)
        stride = jnp.where(inside(NEAR, backward), product, 0.0)
        far, product = [(NEAR, stride)], stride
        for k in range(2 * NEAR, TILES, NEAR):
            product = stride * turn(product, NEAR, backward)
            far.append((k, jnp.where(inside(k, backward), product, 0.0)))
        return near, far

    chains = {backward: factors(backward) for backward in (True, False)}

    def entering(values, backward):
        near, far = chains[backward]
        out = []
        for value in values:
            value = sum(factor * turn(value, k, backward) for k, factor in near)
            out.append(value + sum(factor * turn(value, k, backward) for k, factor in far))
        return out

    def apply(source, target, on_state, on_field):
        carry = [zero, zero]
        for c in reversed(range(COLS)):
            rate, weight = field(RATE, c), field(source, c)
            for i in range(2):
                summed = members_ref[c, i] * weight + carry[i]
                state_ref[c, i] = summed
                carry[i] = rate * summed
        from_right = entering(carry, True)
        state = [zero, zero]
        for c in range(COLS):
            rate, squared, after = field(RATE, c), field(SQUARED, c), field(AFTER, c)
            for i in range(2):
                summed = state_ref[c, i] + after * from_right[i]
                driven = squared * summed
                on_state(c, i, summed, driven)
                state[i] = rate * state[i] + driven
                state_ref[c, i] = state[i]
        from_left = entering(state, False)
        for c in reversed(range(COLS)):
            upto = field(UPTO, c)
            total = sum(members_ref[c, i] * (state_ref[c, i] + upto * from_left[i]) for i in range(2))
            total = total + pltpu.roll(total, 4, 0)
            total = total + pltpu.roll(total, 64, 1)
            total = total + pltpu.roll(total, 32, 1)
            fields_ref[target, c] = total
            on_field(c, total)
        return from_right

    def whole(value):
        return jnp.sum(jnp.sum(value, axis=0, keepdims=True), axis=1, keepdims=True)

    sums = {name: zero for name in ("alpha", "beta", "kappa", "energy", "cross")}

    def keep(c, i, summed, driven):
        first_ref[c, i] = summed
        sums["alpha"] += summed * driven

    def square(c, total):
        sums["beta"] += total * total

    right0 = apply(INNOV, Z0, keep, square)
    alpha = whole(sums["alpha"])
    beta = 0.125 * whole(sums["beta"])
    ratio = jnp.where(alpha > 0.0, beta / jnp.where(alpha > 0.0, alpha, 1.0), 0.0)
    ratio = jnp.broadcast_to(ratio, (8, LANES))

    def orthogonal(c, i, summed, driven):
        part = summed - ratio * first_ref[c, i]
        sums["kappa"] += field(SQUARED, c) * part * part

    even = lane_group % 2 == 0

    def put(row, values):
        rows_ref[pl.ds(row, 16, stride=ROWS), :] = jnp.concatenate(values, axis=0)

    def compare(c, total):
        part = total - ratio * field(Z0, c)
        sums["energy"] += part * part
        sums["cross"] += part * field(Z0, c)
        put(c, [jnp.where(even, field(Z0, c), total)] * 2)

    put(COLS, right0)
    put(COLS + 1, apply(Z0, Z1, orthogonal, compare))
    scalars = (alpha, beta, whole(sums["kappa"]), 0.125 * whole(sums["energy"]), 0.125 * whole(sums["cross"]))
    row = lax.broadcasted_iota(jnp.int32, (1, LANES), 1)
    last = jnp.zeros((1, LANES), jnp.float32)
    for place, value in zip(SCALARS, scalars):
        last = jnp.where(row == place, value, last)
    last = jnp.broadcast_to(last, (LANES, LANES))
    ours = lax.broadcasted_iota(jnp.int32, (LANES, LANES), 1) % ROWS >= COLS + 2
    for block in range(BLOCKS):
        piece = slice(block * LANES, (block + 1) * LANES)
        out_ref[piece, :] = jnp.where(ours, last, rows_ref[piece, :].T)


def prepare(place, in_ref, ensemble_ref, decay_ref, innovation_ref, weight_ref,
            add_ref, scale_ref, add_control_ref, scale_control_ref, rate_ref, amplitude_ref, carry_ref, own_ref):
    for block in range(BLOCKS):
        piece = in_ref[block * LANES : (block + 1) * LANES, :].T
        for line in range(LINES):
            own_ref[:, lane_block(line, block)] = piece[line * ROWS : (line + 1) * ROWS]

    def scalar(at):
        line, row = at // ROWS, at % ROWS
        return own_ref[row : row + 1, line * DEVICES : (line + 1) * DEVICES]

    def whole(value):
        return jnp.sum(value, axis=1, keepdims=True)

    alphas, betas, kappas, energies, crosses = (scalar(at) for at in SCALARS)
    alpha, beta = whole(alphas), whole(betas)
    ratio = beta / alpha
    shift = jnp.where(alphas > 0.0, betas / jnp.where(alphas > 0.0, alphas, 1.0), 0.0) - ratio
    kappa = whole(kappas + alphas * shift * shift)
    energy = whole(energies + shift * (2.0 * crosses + shift * betas))
    step = alpha / (alpha + beta)
    curvature = kappa + energy - step * kappa * (kappa / alpha)
    back = jnp.where(curvature > 0.0, step * kappa / jnp.where(curvature > 0.0, curvature, 1.0), 0.0)
    ahead = step + back * (ratio + step * (kappa / alpha))

    even = lax.rem(place, 2) == 0
    to_own, to_other = jnp.where(even, ahead, -back), jnp.where(even, -back, ahead)
    z0_own, z0_other = jnp.where(even, -back, 0.0), jnp.where(even, 0.0, -back)
    for g in range(GROUPS):
        part = slice(g * LANES, (g + 1) * LANES)
        rows = pl.ds(g, COLS, stride=GROUPS)
        root = jnp.sqrt(weight_ref[:, part])
        own, inverse = own_ref[:COLS, part], 1.0 / root
        add_ref[:, part] = to_own * inverse * own
        scale_ref[:, part] = to_other * inverse
        factor = ensemble_ref[0, :, part].astype(jnp.float32) * root
        add_control_ref[rows, :] = factor * (ahead * (root * innovation_ref[:, part]) + z0_own * own)
        scale_control_ref[rows, :] = z0_other * factor
        rate = decay_ref[:, part]
        rate_ref[rows, :] = rate
        amplitude_ref[rows, :] = jnp.sqrt((1.0 - rate) * (1.0 + rate))
        carry_ref[g : g + 1, :] = ahead * own_ref[COLS : COLS + 1, part] - back * own_ref[COLS + 1 : COLS + 2, part]


def finish(in_ref, add_ref, scale_ref, add_control_ref, scale_control_ref, rate_ref, amplitude_ref, carry_ref,
           control_hbm, increment_hbm, control_ref, increment_ref, sems):
    for block in range(BLOCKS):
        piece = in_ref[block * LANES : (block + 1) * LANES, :].T
        for line in range(LINES):
            part, other = lane_block(line, block), piece[line * ROWS : line * ROWS + COLS]
            increment_ref[:, part] = add_ref[:, part] + scale_ref[:, part] * other
            control_ref[pl.ds(line * BLOCKS + block, COLS, stride=GROUPS), :] = other
    copies = [pltpu.make_async_copy(increment_ref, increment_hbm, sems.at[0])]
    copies[0].start()
    carry = carry_ref[...]
    for c in reversed(range(COLS)):
        part = slice(c * GROUPS, (c + 1) * GROUPS)
        summed = add_control_ref[part, :] + scale_control_ref[part, :] * control_ref[part, :] + carry
        carry = rate_ref[part, :] * summed
        control_ref[part, :] = amplitude_ref[part, :] * summed
        if c % 7 == 0:
            part = slice(c * GROUPS, (c + 7) * GROUPS)
            copies.append(
                pltpu.make_async_copy(control_ref.at[part, :], control_hbm.at[part, :], sems.at[len(copies)])
            )
            copies[-1].start()
    for copy in copies:
        copy.wait()


def shape(*dims):
    return jax.ShapeDtypeStruct(dims, jnp.float32)


def scratch(*dims):
    return pltpu.VMEM(dims, jnp.float32)


def call(kernel, out_shape, scratch_shapes, in_specs, out_specs):
    return pl.pallas_call(
        kernel,
        out_shape=out_shape,
        in_specs=in_specs,
        out_specs=out_specs,
        scratch_shapes=scratch_shapes,
        compiler_params=pltpu.CompilerParams(vmem_limit_bytes=32 * 1024 * 1024),
    )


def pack_call(place, *args):
    return call(
        lambda *refs: pack(place(), *refs),
        shape(DEVICES, LANES),
        [pltpu.VMEM((1, COLS, WIDTH), jnp.bfloat16)]
        + [scratch(COLS, WIDTH)] * 3
        + [scratch(ROWS, WIDTH), pltpu.SemaphoreType.DMA((4,))],
        [HBM] * 4,
        VMEM,
    )(*(pltpu.with_memory_space_constraint(value, pltpu.HBM) for value in args))


def own_call(received):
    return call(
        own_lines,
        shape(DEVICES, LANES),
        [
            scratch(DEVICES, LANES),
            scratch(COLS, 2, 8, LANES),
            scratch(7, COLS, 8, LANES),
            scratch(COLS, 2, 8, LANES),
            scratch(COLS, 2, 8, LANES),
        ],
        [VMEM],
        VMEM,
    )(received)


def prepare_call(place, returned, *args):
    plain, by_column = shape(COLS, WIDTH), shape(COLS * GROUPS, LANES)
    return call(
        lambda *refs: prepare(place(), *refs),
        (plain, plain, by_column, by_column, by_column, by_column, shape(GROUPS, LANES)),
        [scratch(ROWS, WIDTH)],
        [VMEM] * 5,
        (VMEM,) * 7,
    )(returned, *args)


def finish_call(other, *prepared):
    return call(
        finish,
        (shape(COLS * GROUPS, LANES), shape(COLS, WIDTH)),
        [scratch(COLS * GROUPS, LANES), scratch(COLS, WIDTH), pltpu.SemaphoreType.DMA((5,))],
        [VMEM] * 8,
        (HBM, HBM),
    )(other, *prepared)


def on_device(ensemble, decay_rate, innovation, obs_weight):
    args = (ensemble, decay_rate, innovation, obs_weight)
    axes = ("mem", "space")
    place = lambda: lax.axis_index("mem")
    sent = pack_call(place, *args)
    received = lax.all_to_all(sent, axes, 0, 0, tiled=True)
    returned = lax.all_to_all(own_call(received), axes, 0, 0, tiled=True)
    other = lax.ppermute(returned, "mem", [(k, k ^ 1) for k in range(MEMBERS)])
    control, increment = finish_call(other, *prepare_call(place, returned, *args))
    return control.reshape(1, COLS, WIDTH), increment


def solution(mesh):
    in_specs = (P("mem", "space", None), P("space", None), P("space", None), P("space", None))
    out_specs = (P("mem", "space", None), P("space", None))
    return jax.shard_map(
        on_device, mesh=mesh, in_specs=in_specs, out_specs=out_specs, check_vma=False
    )
```

```python
import jax
import jax.numpy as jnp
from jax import lax
from jax.experimental import pallas as pl
from jax.experimental.pallas import tpu as pltpu
from jax.sharding import PartitionSpec as P

MEMBERS, TILES, COLS, LINES = 16, 32, 28, 4
DEVICES = MEMBERS * TILES
ROWS = 32
LANES = 128
BLOCKS = DEVICES // LANES
GROUPS = LINES * BLOCKS
WIDTH = LINES * DEVICES
CHIPS, HALF = DEVICES // 2, WIDTH // 2
NEAR = 8
SCALARS = tuple(line * ROWS + COLS + 2 for line in range(LINES)) + (COLS + 3,)
VMEM = pl.BlockSpec(memory_space=pltpu.VMEM)
HBM = pl.BlockSpec(memory_space=pltpu.HBM)


def lane_block(line, block):
    start = (block // 2) * HALF + line * CHIPS + (block % 2) * LANES
    return slice(start, start + LANES)


def pack(place, ensemble_hbm, decay_hbm, innovation_hbm, weight_hbm, out_ref,
         ensemble_ref, decay_ref, innovation_ref, weight_ref, rows_ref, sems):
    pairs = (
        (ensemble_hbm, ensemble_ref), (weight_hbm, weight_ref), (decay_hbm, decay_ref), (innovation_hbm, innovation_ref)
    )
    copies = [pltpu.make_async_copy(*pair, sems.at[i]) for i, pair in enumerate(pairs)]
    for copy in copies:
        copy.start()
    for copy in copies:
        copy.wait()
    rows_ref[:COLS, :] = ensemble_ref[0].astype(jnp.float32) * jnp.sqrt(weight_ref[...])
    quarter = lax.rem(place, 8)
    start = pl.multiple_of(8 * jnp.minimum(lax.div(quarter, 2), 2), 8)

    def four(ref):
        eight = ref[pl.ds(start, 8), :]
        inner = jnp.where(lax.rem(quarter, 2) == 0, eight[:4], eight[4:])
        return jnp.where(quarter >= 6, ref[COLS - 4 :, :], inner)

    scaled = jnp.sqrt(four(weight_ref)) * four(innovation_ref)
    rows_ref[COLS:, :] = jnp.where(place < 8, four(decay_ref), scaled)
    for block in range(BLOCKS):
        piece = jnp.concatenate([rows_ref[:, lane_block(line, block)] for line in range(LINES)], axis=0)
        out_ref[block * LANES : (block + 1) * LANES, :] = piece.T


def spread(piece, lane_group):
    turned = [piece] + [pltpu.roll(piece, 32 * k, 1) for k in (1, 2, 3)]
    out = []
    for source in range(4):
        value = turned[(3 - source) % 4]
        for group in (2, 1, 0):
            value = jnp.where(lane_group == group, turned[(group - source) % 4], value)
        out.append(value)
    return out


def own_lines(in_ref, out_ref, rows_ref, members_ref, fields_ref, state_ref, first_ref):
    for block in range(BLOCKS):
        piece = slice(block * LANES, (block + 1) * LANES)
        rows_ref[piece, :] = in_ref[piece, :].T

    lane = lax.broadcasted_iota(jnp.int32, (8, LANES), 1)
    sub = lax.broadcasted_iota(jnp.int32, (8, LANES), 0)
    tile, lane_group = lane % TILES, lane // TILES
    low = sub < 4
    zero = jnp.zeros((8, LANES), jnp.float32)

    for c in range(COLS):
        value = rows_ref[pl.ds(c, 16, stride=ROWS), :]
        members_ref[c, 0], members_ref[c, 1] = value[:8], value[8:]

    RATE, SQUARED, AFTER, UPTO, INNOV, Z0, Z1 = range(7)

    def field(kind, c):
        return fields_ref[kind, c]

    for j in range(4):
        given = rows_ref[pl.ds(COLS + j, 16, stride=ROWS), :]
        for kind, value in ((RATE, given[:8]), (INNOV, given[8:])):
            other = pltpu.roll(value, 4, 0)
            for half, both in enumerate((jnp.where(low, value, other), jnp.where(low, other, value))):
                for source, copied in enumerate(spread(both, lane_group)):
                    c = 16 * half + 4 * source + j
                    if c < COLS:
                        fields_ref[kind, c] = copied

    upto, after = zero + 1.0, zero + 1.0
    for c in range(COLS):
        rate = field(RATE, c)
        fields_ref[SQUARED, c] = (1.0 - rate) * (1.0 + rate)
        upto = upto * rate
        fields_ref[UPTO, c] = upto
        fields_ref[AFTER, COLS - 1 - c] = after
        after = after * field(RATE, COLS - 1 - c)

    def turn(value, k, backward):
        return pltpu.roll(value, LANES - k if backward else k, 1)

    def inside(k, backward):
        return tile < TILES - k if backward else tile >= k

    def factors(backward):
        near, product = [], zero + 1.0
        for k in range(1, NEAR + 1):
            near.append((k, jnp.where(inside(k, backward), product, 0.0)))
            product = product * turn(upto, k, backward)
        stride = jnp.where(inside(NEAR, backward), product, 0.0)
        far, product = [(NEAR, stride)], stride
        for k in range(2 * NEAR, TILES, NEAR):
            product = stride * turn(product, NEAR, backward)
            far.append((k, jnp.where(inside(k, backward), product, 0.0)))
        return near, far

    chains = {backward: factors(backward) for backward in (True, False)}

    def entering(values, backward):
        near, far = chains[backward]
        out = []
        for value in values:
            value = sum(factor * turn(value, k, backward) for k, factor in near)
            out.append(value + sum(factor * turn(value, k, backward) for k, factor in far))
        return out

    def apply(source, target, on_state, on_field):
        carry = [zero, zero]
        for c in reversed(range(COLS)):
            rate, weight = field(RATE, c), field(source, c)
            for i in range(2):
                summed = members_ref[c, i] * weight + carry[i]
                state_ref[c, i] = summed
                carry[i] = rate * summed
        from_right = entering(carry, True)
        state = [zero, zero]
        for c in range(COLS):
            rate, squared, after = field(RATE, c), field(SQUARED, c), field(AFTER, c)
            for i in range(2):
                summed = state_ref[c, i] + after * from_right[i]
                driven = squared * summed
                on_state(c, i, summed, driven)
                state[i] = rate * state[i] + driven
                state_ref[c, i] = state[i]
        from_left = entering(state, False)
        for c in reversed(range(COLS)):
            upto = field(UPTO, c)
            total = sum(members_ref[c, i] * (state_ref[c, i] + upto * from_left[i]) for i in range(2))
            total = total + pltpu.roll(total, 4, 0)
            total = total + pltpu.roll(total, 64, 1)
            total = total + pltpu.roll(total, 32, 1)
            fields_ref[target, c] = total
            on_field(c, total)
        return from_right

    def whole(value):
        return jnp.sum(jnp.sum(value, axis=0, keepdims=True), axis=1, keepdims=True)

    sums = {name: zero for name in ("alpha", "beta", "kappa", "energy", "cross")}

    def keep(c, i, summed, driven):
        first_ref[c, i] = summed
        sums["alpha"] += summed * driven

    def square(c, total):
        sums["beta"] += total * total

    right0 = apply(INNOV, Z0, keep, square)
    alpha = whole(sums["alpha"])
    beta = 0.125 * whole(sums["beta"])
    ratio = jnp.where(alpha > 0.0, beta / jnp.where(alpha > 0.0, alpha, 1.0), 0.0)
    ratio = jnp.broadcast_to(ratio, (8, LANES))

    def orthogonal(c, i, summed, driven):
        part = summed - ratio * first_ref[c, i]
        sums["kappa"] += field(SQUARED, c) * part * part

    def put(row, values):
        rows_ref[pl.ds(row, 16, stride=ROWS), :] = jnp.concatenate(values, axis=0)

    def compare(c, total):
        part = total - ratio * field(Z0, c)
        sums["energy"] += part * part
        sums["cross"] += part * field(Z0, c)
        put(c, [field(Z0, c), total])

    put(COLS, right0)
    put(COLS + 1, apply(Z0, Z1, orthogonal, compare))
    scalars = (alpha, beta, whole(sums["kappa"]), 0.125 * whole(sums["energy"]), 0.125 * whole(sums["cross"]))
    row = lax.broadcasted_iota(jnp.int32, (1, LANES), 1)
    last = jnp.zeros((1, LANES), jnp.float32)
    for place, value in zip(SCALARS, scalars):
        last = jnp.where(row == place, value, last)
    last = jnp.broadcast_to(last, (LANES, LANES))
    ours = lax.broadcasted_iota(jnp.int32, (LANES, LANES), 1) % ROWS >= COLS + 2
    for block in range(BLOCKS):
        piece = rows_ref[block * LANES : (block + 1) * LANES, :].T
        to = pl.ds((block % 2) * 2 * LANES + block // 2, LANES, stride=2)
        out_ref[to, :] = jnp.where(ours, last, piece)


def one_half(at, first, in_ref, ensemble_ref, decay_ref, innovation_ref, weight_ref,
             field0_ref, field1_ref, vector0_ref, vector1_ref, scalars_ref, rate_ref, amplitude_ref):
    rows = []
    for j in range(2):
        pieces = [in_ref[pl.ds(2 * j * LANES + h, LANES, stride=2), :].T for h in range(2)]
        state = jnp.where(first, pieces[0], pieces[1])
        for line in range(LINES):
            start = line * CHIPS + j * LANES
            here = pl.ds(pl.multiple_of(at + start, LANES), LANES)
            part = slice(start, start + LANES)
            group = pl.ds(2 * line + j, COLS, stride=8)
            root = jnp.sqrt(weight_ref[:, here])
            inverse = 1.0 / root
            z0, z1 = (piece[line * ROWS : line * ROWS + COLS] for piece in pieces)
            field0_ref[:, part] = inverse * z0
            field1_ref[:, part] = inverse * z1
            factor = ensemble_ref[0, :, here].astype(jnp.float32) * root
            vector0_ref[group, :] = factor * (root * innovation_ref[:, here])
            vector1_ref[group, :] = factor * z0
            rate = decay_ref[:, here]
            rate_ref[group, :] = rate
            amplitude_ref[group, :] = jnp.sqrt((1.0 - rate) * (1.0 + rate))
            rows.append((2 * line + j, state[line * ROWS + COLS : line * ROWS + COLS + 2]))
        for i, place in enumerate(SCALARS):
            scalars_ref[i : i + 1, j * LANES : (j + 1) * LANES] = pieces[0][place : place + 1]
    rows = [row for _, row in sorted(rows, key=lambda pair: pair[0])]
    refs = (vector0_ref, vector1_ref)
    carry = [jnp.concatenate([row[i : i + 1] for row in rows], axis=0) for i in range(2)]
    for c in reversed(range(COLS)):
        part = slice(8 * c, 8 * c + 8)
        rate, amplitude = rate_ref[part, :], amplitude_ref[part, :]
        for i, ref in enumerate(refs):
            summed = ref[part, :] + carry[i]
            carry[i] = rate * summed
            ref[part, :] = amplitude * summed


def prepare(core, *refs):
    one_half(core * HALF, core == 0, *refs)


def finish(core, in_ref, ensemble_ref, decay_ref, innovation_ref, weight_ref, *refs):
    own = refs[:5]
    control_hbm, increment_hbm = refs[5:7]
    other = refs[7:12]
    rate_ref, amplitude_ref, control_ref, increment_ref, sems = refs[12:]
    inputs = (in_ref, ensemble_ref, decay_ref, innovation_ref, weight_ref)
    one_half((1 - core) * HALF, core == 0, *inputs, *other, rate_ref, amplitude_ref)

    def whole(value):
        return jnp.sum(value, axis=1, keepdims=True)

    def both(i):
        return jnp.concatenate([ref[i : i + 1, :] for ref in (own[4], other[4])], axis=1)

    alphas, betas, kappas, energies, crosses = (both(i) for i in range(5))
    alpha, beta = whole(alphas), whole(betas)
    ratio = beta / alpha
    shift = jnp.where(alphas > 0.0, betas / jnp.where(alphas > 0.0, alphas, 1.0), 0.0) - ratio
    kappa = whole(kappas + alphas * shift * shift)
    energy = whole(energies + shift * (2.0 * crosses + shift * betas))
    step = alpha / (alpha + beta)
    curvature = kappa + energy - step * kappa * (kappa / alpha)
    back = jnp.where(curvature > 0.0, step * kappa / jnp.where(curvature > 0.0, curvature, 1.0), 0.0)
    ahead = step + back * (ratio + step * (kappa / alpha))

    copies = []

    def send(source, target):
        copies.append(pltpu.make_async_copy(source, target, sems.at[len(copies)]))
        copies[-1].start()

    for at, (field0_ref, field1_ref, *_) in ((core, own), (1 - core, other)):
        here = pl.ds(pl.multiple_of(at * HALF, HALF), HALF)
        increment_ref[:, here] = ahead * field0_ref[...] - back * field1_ref[...]
    send(increment_ref, increment_hbm)
    for quarter in range(4):
        for c in range(7 * quarter, 7 * quarter + 7):
            for at, (_, _, vector0_ref, vector1_ref, _) in ((core, own), (1 - core, other)):
                part = slice(8 * c, 8 * c + 8)
                here = pl.ds(pl.multiple_of(c * GROUPS + 8 * at, 8), 8)
                control_ref[here, :] = ahead * vector0_ref[part, :] - back * vector1_ref[part, :]
        part = slice(7 * quarter * GROUPS, (7 * quarter + 7) * GROUPS)
        send(control_ref.at[part, :], control_hbm.at[part, :])
    for copy in copies:
        copy.wait()


def shape(*dims):
    return jax.ShapeDtypeStruct(dims, jnp.float32)


def scratch(*dims):
    return pltpu.VMEM(dims, jnp.float32)


def call(kernel, out_shape, scratch_shapes, in_specs, out_specs):
    return pl.pallas_call(
        kernel,
        out_shape=out_shape,
        in_specs=in_specs,
        out_specs=out_specs,
        scratch_shapes=scratch_shapes,
        compiler_params=pltpu.CompilerParams(vmem_limit_bytes=32 * 1024 * 1024),
    )


def pack_call(place, *args):
    return call(
        lambda *refs: pack(place(), *refs),
        shape(DEVICES, LANES),
        [pltpu.VMEM((1, COLS, WIDTH), jnp.bfloat16)]
        + [scratch(COLS, WIDTH)] * 3
        + [scratch(ROWS, WIDTH), pltpu.SemaphoreType.DMA((4,))],
        [HBM] * 4,
        VMEM,
    )(*(pltpu.with_memory_space_constraint(value, pltpu.HBM) for value in args))


def own_call(received):
    return call(
        own_lines,
        shape(DEVICES, LANES),
        [
            scratch(DEVICES, LANES),
            scratch(COLS, 2, 8, LANES),
            scratch(7, COLS, 8, LANES),
            scratch(COLS, 2, 8, LANES),
            scratch(COLS, 2, 8, LANES),
        ],
        [VMEM],
        VMEM,
    )(received)


HALVES = ((COLS, HALF), (COLS, HALF), (COLS * 8, LANES), (COLS * 8, LANES), (8, CHIPS))


def prepare_call(core, returned, *args):
    return call(
        lambda *refs: prepare(core(), *refs),
        tuple(shape(*dims) for dims in HALVES),
        [scratch(COLS * 8, LANES)] * 2,
        [VMEM] * 5,
        (VMEM,) * 5,
    )(returned, *args)


def finish_call(core, other, args, prepared):
    return call(
        lambda *refs: finish(core(), *refs),
        (shape(COLS * GROUPS, LANES), shape(COLS, WIDTH)),
        [scratch(*dims) for dims in HALVES]
        + [scratch(COLS * 8, LANES)] * 2
        + [scratch(COLS * GROUPS, LANES), scratch(COLS, WIDTH), pltpu.SemaphoreType.DMA((5,))],
        [VMEM] * 10,
        (HBM, HBM),
    )(other, *args, *prepared)


def on_device(ensemble, decay_rate, innovation, obs_weight):
    args = (ensemble, decay_rate, innovation, obs_weight)
    core = lambda: lax.axis_index("core")
    sent = pack_call(lambda: 8 * lax.axis_index("core") + lax.axis_index("y"), *args)
    received = lax.all_to_all(sent, ("core", "y", "space"), 0, 0, tiled=True)
    results = own_call(received).reshape(CHIPS, 2, LANES)
    returned = lax.all_to_all(results, ("y", "space"), 0, 0, tiled=True).reshape(DEVICES, LANES)
    other = lax.ppermute(returned, "core", [(0, 1), (1, 0)])
    control, increment = finish_call(core, other, args, prepare_call(core, returned, *args))
    return control.reshape(1, COLS, WIDTH), increment


def solution(mesh):
    chips = jax.sharding.Mesh(mesh.devices.reshape(MEMBERS // 2, 2, TILES), ("y", "core", "space"))
    split = P(("y", "core"), "space", None)
    in_specs = (split, P("space", None), P("space", None), P("space", None))
    return jax.shard_map(
        on_device, mesh=chips, in_specs=in_specs, out_specs=(split, P("space", None)), check_vma=False
    )
```

```python
import jax
import jax.numpy as jnp
from jax import lax
from jax.experimental import pallas as pl
from jax.experimental.pallas import tpu as pltpu
from jax.sharding import PartitionSpec as P

MEMBERS, TILES, COLS, LINES = 16, 32, 28, 4
DEVICES = MEMBERS * TILES
ROWS = 32
LANES = 128
BLOCKS = DEVICES // LANES
GROUPS = LINES * BLOCKS
WIDTH = LINES * DEVICES
CHIPS, HALF = DEVICES // 2, WIDTH // 2
NEAR = 8
SCALARS = tuple(line * ROWS + COLS + 2 for line in range(LINES)) + (COLS + 3,)
VMEM = pl.BlockSpec(memory_space=pltpu.VMEM)
HBM = pl.BlockSpec(memory_space=pltpu.HBM)


def lane_block(line, block):
    start = (block // 2) * HALF + line * CHIPS + (block % 2) * LANES
    return slice(start, start + LANES)


def pack(core, y, ensemble_hbm, decay_hbm, innovation_hbm, weight_hbm, out_ref,
         ensemble_ref, decay_ref, innovation_ref, weight_ref, rows_ref, sems):
    pairs = (
        (ensemble_hbm, ensemble_ref), (weight_hbm, weight_ref), (decay_hbm, decay_ref), (innovation_hbm, innovation_ref)
    )
    copies = [pltpu.make_async_copy(*pair, sems.at[i]) for i, pair in enumerate(pairs)]
    for copy in copies:
        copy.start()
    for copy in copies:
        copy.wait()
    rows_ref[:COLS, :] = ensemble_ref[0].astype(jnp.float32) * jnp.sqrt(weight_ref[...])
    start = pl.multiple_of(8 * jnp.minimum(lax.div(y, 2), 2), 8)

    def four(ref):
        eight = ref[pl.ds(start, 8), :]
        inner = jnp.where(lax.rem(y, 2) == 0, eight[:4], eight[4:])
        return jnp.where(y >= 6, ref[COLS - 4 :, :], inner)

    scaled = jnp.sqrt(four(weight_ref)) * four(innovation_ref)
    rates = four(decay_ref)
    for owner in range(2):
        part = slice(owner * HALF, (owner + 1) * HALF)
        rows_ref[COLS:, part] = jnp.where(core == owner, rates[:, part], scaled[:, part])
    for block in range(BLOCKS):
        piece = jnp.concatenate([rows_ref[:, lane_block(line, block)] for line in range(LINES)], axis=0)
        to = pl.ds((block % 2) * 2 * LANES + block // 2, LANES, stride=2)
        out_ref[to, :] = piece.T


def spread(piece, lane_group):
    turned = [piece] + [pltpu.roll(piece, 32 * k, 1) for k in (1, 2, 3)]
    out = []
    for source in range(4):
        value = turned[(3 - source) % 4]
        for group in (2, 1, 0):
            value = jnp.where(lane_group == group, turned[(group - source) % 4], value)
        out.append(value)
    return out


RATE, SQUARED, AFTER, UPTO, INNOV, Z0, Z1 = range(7)
FAR = TILES // NEAR - 1


def places():
    lane = lax.broadcasted_iota(jnp.int32, (8, LANES), 1)
    sub = lax.broadcasted_iota(jnp.int32, (8, LANES), 0)
    return lane % TILES, lane // TILES, sub < 4


def arrived(core, in_ref, rows_ref, members_ref, keep_field):
    for j in range(2):
        pieces = [in_ref[pl.ds(2 * j * LANES + owner, LANES, stride=2), :] for owner in range(2)]
        rows_ref[j * LANES : (j + 1) * LANES, :] = jnp.where(core == 0, *pieces).T
    for c in range(COLS):
        members_ref[c] = rows_ref[pl.ds(c, 8, stride=ROWS), :]
    _, lane_group, low = places()
    for j in range(4):
        value = rows_ref[pl.ds(COLS + j, 8, stride=ROWS), :]
        other = pltpu.roll(value, 4, 0)
        for half, both in enumerate((jnp.where(low, value, other), jnp.where(low, other, value))):
            for source, copied in enumerate(spread(both, lane_group)):
                c = 16 * half + 4 * source + j
                if c < COLS:
                    keep_field(c, copied)


def turn(value, k, backward):
    return pltpu.roll(value, LANES - k if backward else k, 1)


def own_first(core, in_ref, members_ref, rates_ref, factors_ref, rows_ref):
    def keep_rate(c, value):
        rates_ref[RATE, c] = value

    arrived(core, in_ref, rows_ref, members_ref, keep_rate)
    tile, _, _ = places()
    one = jnp.ones((8, LANES), jnp.float32)
    upto, after = one, one
    for c in range(COLS):
        rate = rates_ref[RATE, c]
        rates_ref[SQUARED, c] = (1.0 - rate) * (1.0 + rate)
        upto = upto * rate
        rates_ref[UPTO, c] = upto
        rates_ref[AFTER, COLS - 1 - c] = after
        after = after * rates_ref[RATE, COLS - 1 - c]

    for backward in (True, False):

        def inside(k):
            return tile < TILES - k if backward else tile >= k

        product = one
        for k in range(1, NEAR + 1):
            factors_ref[int(backward), k - 1] = jnp.where(inside(k), product, 0.0)
            product = product * turn(upto, k, backward)
        stride = jnp.where(inside(NEAR), product, 0.0)
        product = stride
        for i in range(FAR):
            factors_ref[int(backward), NEAR + i] = jnp.where(inside(NEAR * (i + 1)), product, 0.0)
            product = stride * turn(product, NEAR, backward)


def own_lines(core, in_ref, own_members_ref, rates_ref, factors_ref, out_ref,
              rows_ref, other_members_ref, fields_ref, state_ref, first_ref):
    def keep_innovation(c, value):
        fields_ref[INNOV - INNOV, c] = value

    arrived(core, in_ref, rows_ref, other_members_ref, keep_innovation)
    members = (own_members_ref, other_members_ref)
    zero = jnp.zeros((8, LANES), jnp.float32)

    def field(kind, c):
        return rates_ref[kind, c] if kind < INNOV else fields_ref[kind - INNOV, c]

    def entering(values, backward):
        out = []
        for value in values:
            for steps in (range(1, NEAR + 1), range(NEAR, TILES, NEAR)):
                at = 0 if steps.step == 1 else NEAR
                terms = [factors_ref[int(backward), at + i] * turn(value, k, backward) for i, k in enumerate(steps)]
                if steps.step > 1:
                    terms.append(value)
                while len(terms) > 1:
                    terms = [sum(terms[i : i + 2]) for i in range(0, len(terms), 2)]
                value = terms[0]
            out.append(value)
        return out

    def apply(source, target, on_state, on_field):
        carry = [zero, zero]
        for c in reversed(range(COLS)):
            rate, weight = field(RATE, c), field(source, c)
            for i in range(2):
                summed = members[i][c] * weight + carry[i]
                state_ref[c, i] = summed
                carry[i] = rate * summed
        from_right = entering(carry, True)
        state = [zero, zero]
        for c in range(COLS):
            rate, squared, after = field(RATE, c), field(SQUARED, c), field(AFTER, c)
            for i in range(2):
                summed = state_ref[c, i] + after * from_right[i]
                driven = squared * summed
                on_state(c, i, summed, driven)
                state[i] = rate * state[i] + driven
                state_ref[c, i] = state[i]
        from_left = entering(state, False)
        for c in reversed(range(COLS)):
            upto = field(UPTO, c)
            total = sum(members[i][c] * (state_ref[c, i] + upto * from_left[i]) for i in range(2))
            total = total + pltpu.roll(total, 4, 0)
            total = total + pltpu.roll(total, 64, 1)
            total = total + pltpu.roll(total, 32, 1)
            fields_ref[target - INNOV, c] = total
            on_field(c, total)
        return from_right

    def whole(value):
        return jnp.sum(jnp.sum(value, axis=0, keepdims=True), axis=1, keepdims=True)

    sums = {name: zero for name in ("alpha", "beta", "kappa", "energy", "cross")}

    def keep(c, i, summed, driven):
        first_ref[c, i] = summed
        sums["alpha"] += summed * driven

    def square(c, total):
        sums["beta"] += total * total

    right0 = apply(INNOV, Z0, keep, square)
    alpha = whole(sums["alpha"])
    beta = 0.125 * whole(sums["beta"])
    ratio = jnp.where(alpha > 0.0, beta / jnp.where(alpha > 0.0, alpha, 1.0), 0.0)
    ratio = jnp.broadcast_to(ratio, (8, LANES))

    def orthogonal(c, i, summed, driven):
        part = summed - ratio * first_ref[c, i]
        sums["kappa"] += field(SQUARED, c) * part * part

    def put(row, values):
        rows_ref[pl.ds(row, 16, stride=ROWS), :] = jnp.concatenate(values, axis=0)

    def compare(c, total):
        part = total - ratio * field(Z0, c)
        sums["energy"] += part * part
        sums["cross"] += part * field(Z0, c)
        put(c, [field(Z0, c), total])

    put(COLS, right0)
    put(COLS + 1, apply(Z0, Z1, orthogonal, compare))
    scalars = (alpha, beta, whole(sums["kappa"]), 0.125 * whole(sums["energy"]), 0.125 * whole(sums["cross"]))
    row = lax.broadcasted_iota(jnp.int32, (1, LANES), 1)
    last = jnp.zeros((1, LANES), jnp.float32)
    for place, value in zip(SCALARS, scalars):
        last = jnp.where(row == place, value, last)
    last = jnp.broadcast_to(last, (LANES, LANES))
    ours = lax.broadcasted_iota(jnp.int32, (LANES, LANES), 1) % ROWS >= COLS + 2
    for block in range(BLOCKS):
        piece = rows_ref[block * LANES : (block + 1) * LANES, :].T
        to = pl.ds((block % 2) * 2 * LANES + block // 2, LANES, stride=2)
        out_ref[to, :] = jnp.where(ours, last, piece)


def factors_of(at, ensemble_ref, decay_ref, innovation_ref, weight_ref, refs):
    inverse_ref, vector_ref, factor_ref, rate_ref, amplitude_ref = refs
    for g in range(8):
        here = pl.ds(pl.multiple_of(at + g * LANES, LANES), LANES)
        group = pl.ds(g, COLS, stride=8)
        root = jnp.sqrt(weight_ref[:, here])
        inverse_ref[:, g * LANES : (g + 1) * LANES] = 1.0 / root
        factor = ensemble_ref[0, :, here].astype(jnp.float32) * root
        vector_ref[group, :] = factor * (root * innovation_ref[:, here])
        factor_ref[group, :] = factor
        rate = decay_ref[:, here]
        rate_ref[group, :] = rate
        amplitude_ref[group, :] = jnp.sqrt((1.0 - rate) * (1.0 + rate))


def one_half(mine, in_ref, field0_ref, field1_ref, vector0_ref, vector1_ref, scalars_ref,
             inverse_ref, vector_ref, factor_ref, rate_ref, amplitude_ref):
    rows = [None] * 8
    for j in range(2):
        pieces = [in_ref[pl.ds(2 * j * LANES + h, LANES, stride=2), :].T for h in range(2)]
        for line in range(LINES):
            g = 2 * line + j
            part = slice(g * LANES, (g + 1) * LANES)
            z0, z1 = (piece[line * ROWS : line * ROWS + COLS] for piece in pieces)
            inverse = inverse_ref[:, part]
            field0_ref[:, part] = inverse * z0
            field1_ref[:, part] = inverse * z1
            vector1_ref[pl.ds(g, COLS, stride=8), :] = z0
            rows[g] = pieces[mine][line * ROWS + COLS : line * ROWS + COLS + 2]
        for i, place in enumerate(SCALARS):
            scalars_ref[i : i + 1, j * LANES : (j + 1) * LANES] = pieces[0][place : place + 1]
    carry = [jnp.concatenate([row[i : i + 1] for row in rows], axis=0) for i in range(2)]
    for c in reversed(range(COLS)):
        part = slice(8 * c, 8 * c + 8)
        rate, amplitude = rate_ref[part, :], amplitude_ref[part, :]
        for i, value in enumerate((vector_ref[part, :], factor_ref[part, :] * vector1_ref[part, :])):
            summed = value + carry[i]
            carry[i] = rate * summed
            (vector0_ref, vector1_ref)[i][part, :] = amplitude * summed


def prepare(core, in_ref, *refs):
    args, half, other, own = refs[:4], refs[4:9], refs[9:14], refs[14:]
    factors_of(core * HALF, *args, own)
    one_half(0, in_ref, *half, *own)
    factors_of((1 - core) * HALF, *args, other)


def finish(core, in_ref, *refs):
    own, factors = refs[:5], refs[5:10]
    control_hbm, increment_hbm = refs[10:12]
    other = refs[12:17]
    control_ref, increment_ref, sems = refs[17:]
    one_half(1, in_ref, *other, *factors)

    def whole(value):
        return jnp.sum(value, axis=1, keepdims=True)

    def both(i):
        return jnp.concatenate([ref[i : i + 1, :] for ref in (own[4], other[4])], axis=1)

    alphas, betas, kappas, energies, crosses = (both(i) for i in range(5))
    alpha, beta = whole(alphas), whole(betas)
    ratio = beta / alpha
    shift = jnp.where(alphas > 0.0, betas / jnp.where(alphas > 0.0, alphas, 1.0), 0.0) - ratio
    kappa = whole(kappas + alphas * shift * shift)
    energy = whole(energies + shift * (2.0 * crosses + shift * betas))
    step = alpha / (alpha + beta)
    curvature = kappa + energy - step * kappa * (kappa / alpha)
    back = jnp.where(curvature > 0.0, step * kappa / jnp.where(curvature > 0.0, curvature, 1.0), 0.0)
    ahead = step + back * (ratio + step * (kappa / alpha))

    copies = []

    def send(source, target):
        copies.append(pltpu.make_async_copy(source, target, sems.at[len(copies)]))
        copies[-1].start()

    for at, (field0_ref, field1_ref, *_) in ((core, own), (1 - core, other)):
        here = pl.ds(pl.multiple_of(at * HALF, HALF), HALF)
        increment_ref[:, here] = ahead * field0_ref[...] - back * field1_ref[...]
    send(increment_ref, increment_hbm)
    for quarter in range(4):
        for c in range(7 * quarter, 7 * quarter + 7):
            for at, (_, _, vector0_ref, vector1_ref, _) in ((core, own), (1 - core, other)):
                part = slice(8 * c, 8 * c + 8)
                here = pl.ds(pl.multiple_of(c * GROUPS + 8 * at, 8), 8)
                control_ref[here, :] = ahead * vector0_ref[part, :] - back * vector1_ref[part, :]
        part = slice(7 * quarter * GROUPS, (7 * quarter + 7) * GROUPS)
        send(control_ref.at[part, :], control_hbm.at[part, :])
    for copy in copies:
        copy.wait()


def shape(*dims):
    return jax.ShapeDtypeStruct(dims, jnp.float32)


def scratch(*dims):
    return pltpu.VMEM(dims, jnp.float32)


def call(kernel, out_shape, scratch_shapes, in_specs, out_specs):
    return pl.pallas_call(
        kernel,
        out_shape=out_shape,
        in_specs=in_specs,
        out_specs=out_specs,
        scratch_shapes=scratch_shapes,
        compiler_params=pltpu.CompilerParams(vmem_limit_bytes=32 * 1024 * 1024),
    )


def columns(count):
    return (count, COLS, 8, LANES)


def pack_call(core, y, *args):
    return call(
        lambda *refs: pack(core(), y(), *refs),
        shape(DEVICES, LANES),
        [pltpu.VMEM((1, COLS, WIDTH), jnp.bfloat16)]
        + [scratch(COLS, WIDTH)] * 3
        + [scratch(ROWS, WIDTH), pltpu.SemaphoreType.DMA((4,))],
        [HBM] * 4,
        VMEM,
    )(*(pltpu.with_memory_space_constraint(value, pltpu.HBM) for value in args))


def own_call(core, received, other):
    first = call(
        lambda *refs: own_first(core(), *refs),
        (shape(COLS, 8, LANES), shape(*columns(4)), shape(2, NEAR + FAR, 8, LANES)),
        [scratch(2 * LANES, LANES)],
        [VMEM],
        (VMEM,) * 3,
    )(received)
    return call(
        lambda *refs: own_lines(core(), *refs),
        shape(DEVICES, LANES),
        [
            scratch(DEVICES, LANES),
            scratch(COLS, 8, LANES),
            scratch(*columns(3)),
            scratch(COLS, 2, 8, LANES),
            scratch(COLS, 2, 8, LANES),
        ],
        [VMEM] * 4,
        VMEM,
    )(other, *first)


BY_COLUMN = (COLS * 8, LANES)
RESULTS = ((COLS, HALF), (COLS, HALF), BY_COLUMN, BY_COLUMN, (8, CHIPS))
FACTORS = ((COLS, HALF), BY_COLUMN, BY_COLUMN, BY_COLUMN, BY_COLUMN)


def prepare_call(core, returned, *args):
    return call(
        lambda *refs: prepare(core(), *refs),
        tuple(shape(*dims) for dims in RESULTS + FACTORS),
        [scratch(*dims) for dims in FACTORS],
        [VMEM] * 5,
        (VMEM,) * 10,
    )(returned, *args)


def finish_call(core, other, prepared):
    return call(
        lambda *refs: finish(core(), *refs),
        (shape(COLS * GROUPS, LANES), shape(COLS, WIDTH)),
        [scratch(*dims) for dims in RESULTS]
        + [scratch(COLS * GROUPS, LANES), scratch(COLS, WIDTH), pltpu.SemaphoreType.DMA((5,))],
        [VMEM] * 11,
        (HBM, HBM),
    )(other, *prepared)


def on_device(ensemble, decay_rate, innovation, obs_weight):
    args = (ensemble, decay_rate, innovation, obs_weight)
    core, y = (lambda: lax.axis_index("core")), (lambda: lax.axis_index("y"))

    def among_chips(value):
        pieces = value.reshape(CHIPS, 2, LANES)
        return lax.all_to_all(pieces, ("y", "space"), 0, 0, tiled=True).reshape(DEVICES, LANES)

    def swap(value):
        return lax.ppermute(value, "core", [(0, 1), (1, 0)])

    received = among_chips(pack_call(core, y, *args))
    returned = among_chips(own_call(core, received, swap(received)))
    control, increment = finish_call(core, swap(returned), prepare_call(core, returned, *args))
    return control.reshape(1, COLS, WIDTH), increment


def solution(mesh):
    chips = jax.sharding.Mesh(mesh.devices.reshape(MEMBERS // 2, 2, TILES), ("y", "core", "space"))
    split = P(("y", "core"), "space", None)
    in_specs = (split, P("space", None), P("space", None), P("space", None))
    return jax.shard_map(
        on_device, mesh=chips, in_specs=in_specs, out_specs=(split, P("space", None)), check_vma=False
    )
```

```python
import jax
import jax.numpy as jnp
from jax import lax
from jax.experimental import pallas as pl
from jax.experimental.pallas import tpu as pltpu
from jax.sharding import PartitionSpec as P

MEMBERS, TILES, COLS, LINES = 16, 32, 28, 4
DEVICES = MEMBERS * TILES
ROWS = 32
LANES = 128
BLOCKS = DEVICES // LANES
GROUPS = LINES * BLOCKS
WIDTH = LINES * DEVICES
CHIPS, HALF = DEVICES // 2, WIDTH // 2
NEAR = 8
SEGMENT = 7
SEGMENTS = [range(start, start + SEGMENT) for start in range(0, COLS, SEGMENT)]
SCALARS = tuple(line * ROWS + COLS + 2 for line in range(LINES)) + (COLS + 3,)
VMEM = pl.BlockSpec(memory_space=pltpu.VMEM)
HBM = pl.BlockSpec(memory_space=pltpu.HBM)


def lane_block(line, block):
    start = (block // 2) * HALF + line * CHIPS + (block % 2) * LANES
    return slice(start, start + LANES)


def pack(place, ensemble_hbm, decay_hbm, innovation_hbm, weight_hbm, out_ref,
         ensemble_ref, decay_ref, innovation_ref, weight_ref, rows_ref, sems):
    quarter = lax.rem(place, 8)
    start = pl.multiple_of(8 * jnp.minimum(lax.div(quarter, 2), 2), 8)
    pairs = (
        (ensemble_hbm, ensemble_ref), (weight_hbm, weight_ref), (decay_hbm, decay_ref), (innovation_hbm, innovation_ref)
    )
    copies = [pltpu.make_async_copy(*pair, sems.at[i]) for i, pair in enumerate(pairs)]
    for copy in copies:
        copy.start()
    for copy in copies:
        copy.wait()
    rows_ref[:COLS, :] = ensemble_ref[0].astype(jnp.float32) * jnp.sqrt(weight_ref[...])

    def four(ref):
        eight = ref[pl.ds(start, 8), :]
        inner = jnp.where(lax.rem(quarter, 2) == 0, eight[:4], eight[4:])
        return jnp.where(quarter >= 6, ref[COLS - 4 :, :], inner)

    scaled = jnp.sqrt(four(weight_ref)) * four(innovation_ref)
    rows_ref[COLS:, :] = jnp.where(place < 8, four(decay_ref), scaled)
    for block in range(BLOCKS):
        piece = jnp.concatenate([rows_ref[:, lane_block(line, block)] for line in range(LINES)], axis=0)
        out_ref[block * LANES : (block + 1) * LANES, :] = piece.T


def balanced(join, terms):
    while len(terms) > 1:
        terms = [join(*terms[i : i + 2]) if i + 1 < len(terms) else terms[i] for i in range(0, len(terms), 2)]
    return terms[0]


def add(x, y):
    return x + y


def spread(piece, lane_group):
    turned = [piece] + [pltpu.roll(piece, 32 * k, 1) for k in (1, 2, 3)]
    out = []
    for source in range(4):
        value = turned[(3 - source) % 4]
        for group in (2, 1, 0):
            value = jnp.where(lane_group == group, turned[(group - source) % 4], value)
        out.append(value)
    return out


def own_lines(in_ref, out_ref, rows_ref, members_ref, fields_ref, state_ref, first_ref):
    for block in range(BLOCKS):
        piece = slice(block * LANES, (block + 1) * LANES)
        rows_ref[piece, :] = in_ref[piece, :].T

    lane = lax.broadcasted_iota(jnp.int32, (8, LANES), 1)
    sub = lax.broadcasted_iota(jnp.int32, (8, LANES), 0)
    tile, lane_group = lane % TILES, lane // TILES
    low = sub < 4
    zero = jnp.zeros((8, LANES), jnp.float32)

    for c in range(COLS):
        value = rows_ref[pl.ds(c, 16, stride=ROWS), :]
        members_ref[c, 0], members_ref[c, 1] = value[:8], value[8:]

    RATE, SQUARED, AFTER, UPTO, INNOV, Z0, Z1 = range(7)

    def field(kind, c):
        return fields_ref[kind, c]

    for j in range(4):
        given = rows_ref[pl.ds(COLS + j, 16, stride=ROWS), :]
        for kind, value in ((RATE, given[:8]), (INNOV, given[8:])):
            other = pltpu.roll(value, 4, 0)
            for half, both in enumerate((jnp.where(low, value, other), jnp.where(low, other, value))):
                for source, copied in enumerate(spread(both, lane_group)):
                    c = 16 * half + 4 * source + j
                    if c < COLS:
                        fields_ref[kind, c] = copied

    one = zero + 1.0
    parts = []
    for columns in SEGMENTS:
        upto, after = one, one
        for c in columns:
            rate = field(RATE, c)
            fields_ref[SQUARED, c] = (1.0 - rate) * (1.0 + rate)
            upto = upto * rate
            fields_ref[UPTO, c] = upto
        for c in reversed(columns):
            fields_ref[AFTER, c] = after
            after = after * field(RATE, c)
        parts.append(upto)
    upto = balanced(lambda x, y: x * y, parts)

    def turn(value, k, backward):
        return pltpu.roll(value, LANES - k if backward else k, 1)

    def inside(k, backward):
        return tile < TILES - k if backward else tile >= k

    def factors(backward):
        near, product = [], one
        for k in range(1, NEAR + 1):
            near.append((k, jnp.where(inside(k, backward), product, 0.0)))
            product = product * turn(upto, k, backward)
        stride = jnp.where(inside(NEAR, backward), product, 0.0)
        far, product = [(NEAR, stride)], stride
        for k in range(2 * NEAR, TILES, NEAR):
            product = stride * turn(product, NEAR, backward)
            far.append((k, jnp.where(inside(k, backward), product, 0.0)))
        return near, far

    chains = {backward: factors(backward) for backward in (True, False)}

    def entering(values, backward):
        near, far = chains[backward]
        out = []
        for value in values:
            value = balanced(add, [factor * turn(value, k, backward) for k, factor in near])
            out.append(balanced(add, [value] + [factor * turn(value, k, backward) for k, factor in far]))
        return out

    def through(ends, products, start):
        states = [start]
        for end, product in zip(ends, products):
            states.append(end if states[-1] is None else end + product * states[-1])
        return states

    def apply(source, target, on_state, on_field):
        ends = [[], []]
        for columns in reversed(SEGMENTS):
            carry = [None, None]
            for c in reversed(columns):
                rate, weight = field(RATE, c), field(source, c)
                for i in range(2):
                    summed = members_ref[c, i] * weight
                    summed = summed if carry[i] is None else summed + carry[i]
                    state_ref[c, i] = summed
                    carry[i] = rate * summed
            for i in range(2):
                ends[i].append(carry[i])
        from_right = entering([through(ends[i], parts[::-1], None)[-1] for i in range(2)], True)
        starts = [through(ends[i], parts[::-1], from_right[i])[:-1][::-1] for i in range(2)]
        ends = [[], []]
        for s, columns in enumerate(SEGMENTS):
            state = [None, None]
            for c in columns:
                rate, squared, after = field(RATE, c), field(SQUARED, c), field(AFTER, c)
                for i in range(2):
                    summed = state_ref[c, i] + after * starts[i][s]
                    driven = squared * summed
                    on_state(c, i, summed, driven)
                    state[i] = driven if state[i] is None else rate * state[i] + driven
                    state_ref[c, i] = state[i]
            for i in range(2):
                ends[i].append(state[i])
        from_left = entering([through(ends[i], parts, None)[-1] for i in range(2)], False)
        starts = [through(ends[i], parts, from_left[i])[:-1] for i in range(2)]
        for s, columns in reversed(list(enumerate(SEGMENTS))):
            for c in reversed(columns):
                upto = field(UPTO, c)
                total = add(*(members_ref[c, i] * (state_ref[c, i] + upto * starts[i][s]) for i in range(2)))
                total = total + pltpu.roll(total, 4, 0)
                total = total + pltpu.roll(total, 64, 1)
                total = total + pltpu.roll(total, 32, 1)
                fields_ref[target, c] = total
                on_field(c, total)
        return from_right

    def whole(value):
        return jnp.sum(jnp.sum(value, axis=0, keepdims=True), axis=1, keepdims=True)

    sums = {name: zero for name in ("alpha", "beta", "kappa", "energy", "cross")}

    def keep(c, i, summed, driven):
        first_ref[c, i] = summed
        sums["alpha"] += summed * driven

    def square(c, total):
        sums["beta"] += total * total

    right0 = apply(INNOV, Z0, keep, square)
    alpha = whole(sums["alpha"])
    beta = 0.125 * whole(sums["beta"])
    ratio = jnp.where(alpha > 0.0, beta / jnp.where(alpha > 0.0, alpha, 1.0), 0.0)
    ratio = jnp.broadcast_to(ratio, (8, LANES))

    def orthogonal(c, i, summed, driven):
        part = summed - ratio * first_ref[c, i]
        sums["kappa"] += field(SQUARED, c) * part * part

    def put(row, values):
        rows_ref[pl.ds(row, 16, stride=ROWS), :] = jnp.concatenate(values, axis=0)

    def compare(c, total):
        part = total - ratio * field(Z0, c)
        sums["energy"] += part * part
        sums["cross"] += part * field(Z0, c)
        put(c, [field(Z0, c), total])

    put(COLS, right0)
    put(COLS + 1, apply(Z0, Z1, orthogonal, compare))
    scalars = (alpha, beta, whole(sums["kappa"]), 0.125 * whole(sums["energy"]), 0.125 * whole(sums["cross"]))
    row = lax.broadcasted_iota(jnp.int32, (1, LANES), 1)
    last = jnp.zeros((1, LANES), jnp.float32)
    for place, value in zip(SCALARS, scalars):
        last = jnp.where(row == place, value, last)
    last = jnp.broadcast_to(last, (LANES, LANES))
    ours = lax.broadcasted_iota(jnp.int32, (LANES, LANES), 1) % ROWS >= COLS + 2
    for block in range(BLOCKS):
        piece = rows_ref[block * LANES : (block + 1) * LANES, :].T
        to = pl.ds((block % 2) * 2 * LANES + block // 2, LANES, stride=2)
        out_ref[to, :] = jnp.where(ours, last, piece)


def factors_of(at, ensemble_ref, decay_ref, innovation_ref, weight_ref, refs):
    inverse_ref, vector_ref, factor_ref, rate_ref, amplitude_ref, after_ref = refs
    for g in range(8):
        here = pl.ds(pl.multiple_of(at + g * LANES, LANES), LANES)
        group = pl.ds(g, COLS, stride=8)
        root = jnp.sqrt(weight_ref[:, here])
        inverse_ref[:, g * LANES : (g + 1) * LANES] = 1.0 / root
        factor = ensemble_ref[0, :, here].astype(jnp.float32) * root
        vector_ref[group, :] = factor * (root * innovation_ref[:, here])
        factor_ref[group, :] = factor
        rate = decay_ref[:, here]
        rate_ref[group, :] = rate
        amplitude_ref[group, :] = jnp.sqrt((1.0 - rate) * (1.0 + rate))
    for columns in SEGMENTS:
        after = jnp.ones((8, LANES), jnp.float32)
        for c in reversed(columns):
            part = slice(8 * c, 8 * c + 8)
            after_ref[part, :] = after
            after = after * rate_ref[part, :]


def one_half(core, in_ref, field0_ref, field1_ref, vector0_ref, vector1_ref, scalars_ref,
             inverse_ref, vector_ref, factor_ref, rate_ref, amplitude_ref, after_ref):
    rows = [None] * 8
    for j in range(2):
        pieces = [in_ref[pl.ds(2 * j * LANES + h, LANES, stride=2), :].T for h in range(2)]
        for line in range(LINES):
            g = 2 * line + j
            part = slice(g * LANES, (g + 1) * LANES)
            z0, z1 = (piece[line * ROWS : line * ROWS + COLS] for piece in pieces)
            inverse = inverse_ref[:, part]
            field0_ref[:, part] = inverse * z0
            field1_ref[:, part] = inverse * z1
            vector1_ref[pl.ds(g, COLS, stride=8), :] = z0
            states = [piece[line * ROWS + COLS : line * ROWS + COLS + 2] for piece in pieces]
            rows[g] = jnp.where(core == 0, *states)
        for i, place in enumerate(SCALARS):
            scalars_ref[i : i + 1, j * LANES : (j + 1) * LANES] = pieces[0][place : place + 1]
    entering = [jnp.concatenate([row[i : i + 1] for row in rows], axis=0) for i in range(2)]
    for columns in reversed(SEGMENTS):
        carry = [None, None]
        for c in reversed(columns):
            part = slice(8 * c, 8 * c + 8)
            for i, value in enumerate((vector_ref[part, :], factor_ref[part, :] * vector1_ref[part, :])):
                summed = value if carry[i] is None else value + carry[i]
                carry[i] = rate_ref[part, :] * summed
                (vector0_ref, vector1_ref)[i][part, :] = summed
        for c in columns:
            part = slice(8 * c, 8 * c + 8)
            for ref, state in zip((vector0_ref, vector1_ref), entering):
                ref[part, :] = amplitude_ref[part, :] * (ref[part, :] + after_ref[part, :] * state)
        first = slice(8 * columns[0], 8 * columns[0] + 8)
        product = rate_ref[first, :] * after_ref[first, :]
        entering = [end + product * state for end, state in zip(carry, entering)]


def prepare(core, in_ref, *refs):
    args, half, other, own = refs[:4], refs[4:9], refs[9:15], refs[15:]
    factors_of(core * HALF, *args, own)
    one_half(core, in_ref, *half, *own)
    factors_of((1 - core) * HALF, *args, other)


def finish(core, in_ref, *refs):
    own, factors = refs[:5], refs[5:11]
    control_hbm, increment_hbm = refs[11:13]
    other = refs[13:18]
    control_ref, increment_ref, sems = refs[18:]
    one_half(core, in_ref, *other, *factors)

    def whole(value):
        return jnp.sum(value, axis=1, keepdims=True)

    def both(i):
        return jnp.concatenate([ref[i : i + 1, :] for ref in (own[4], other[4])], axis=1)

    alphas, betas, kappas, energies, crosses = (both(i) for i in range(5))
    alpha, beta = whole(alphas), whole(betas)
    ratio = beta / alpha
    shift = jnp.where(alphas > 0.0, betas / jnp.where(alphas > 0.0, alphas, 1.0), 0.0) - ratio
    kappa = whole(kappas + alphas * shift * shift)
    energy = whole(energies + shift * (2.0 * crosses + shift * betas))
    step = alpha / (alpha + beta)
    curvature = kappa + energy - step * kappa * (kappa / alpha)
    back = jnp.where(curvature > 0.0, step * kappa / jnp.where(curvature > 0.0, curvature, 1.0), 0.0)
    ahead = step + back * (ratio + step * (kappa / alpha))

    copies = []

    def send(source, target):
        copies.append(pltpu.make_async_copy(source, target, sems.at[len(copies)]))
        copies[-1].start()

    for at, (field0_ref, field1_ref, *_) in ((core, own), (1 - core, other)):
        here = pl.ds(pl.multiple_of(at * HALF, HALF), HALF)
        increment_ref[:, here] = ahead * field0_ref[...] - back * field1_ref[...]
    send(increment_ref, increment_hbm)
    for quarter in range(4):
        for c in range(7 * quarter, 7 * quarter + 7):
            for at, (_, _, vector0_ref, vector1_ref, _) in ((core, own), (1 - core, other)):
                part = slice(8 * c, 8 * c + 8)
                here = pl.ds(pl.multiple_of(c * GROUPS + 8 * at, 8), 8)
                control_ref[here, :] = ahead * vector0_ref[part, :] - back * vector1_ref[part, :]
        part = slice(7 * quarter * GROUPS, (7 * quarter + 7) * GROUPS)
        send(control_ref.at[part, :], control_hbm.at[part, :])
    for copy in copies:
        copy.wait()


def shape(*dims):
    return jax.ShapeDtypeStruct(dims, jnp.float32)


def scratch(*dims):
    return pltpu.VMEM(dims, jnp.float32)


def call(kernel, out_shape, scratch_shapes, in_specs, out_specs):
    return pl.pallas_call(
        kernel,
        out_shape=out_shape,
        in_specs=in_specs,
        out_specs=out_specs,
        scratch_shapes=scratch_shapes,
        compiler_params=pltpu.CompilerParams(vmem_limit_bytes=32 * 1024 * 1024),
    )


def pack_call(place, *args):
    return call(
        lambda *refs: pack(place(), *refs),
        (shape(DEVICES, LANES),) + tuple(jax.ShapeDtypeStruct(value.shape, value.dtype) for value in args),
        [scratch(ROWS, WIDTH), pltpu.SemaphoreType.DMA((4,))],
        [HBM] * 4,
        (VMEM,) * 5,
    )(*(pltpu.with_memory_space_constraint(value, pltpu.HBM) for value in args))


def own_call(received):
    return call(
        own_lines,
        shape(DEVICES, LANES),
        [
            scratch(DEVICES, LANES),
            scratch(COLS, 2, 8, LANES),
            scratch(7, COLS, 8, LANES),
            scratch(COLS, 2, 8, LANES),
            scratch(COLS, 2, 8, LANES),
        ],
        [VMEM],
        VMEM,
    )(received)


BY_COLUMN = (COLS * 8, LANES)
RESULTS = ((COLS, HALF), (COLS, HALF), BY_COLUMN, BY_COLUMN, (8, CHIPS))
FACTORS = ((COLS, HALF), BY_COLUMN, BY_COLUMN, BY_COLUMN, BY_COLUMN, BY_COLUMN)


def prepare_call(core, returned, *args):
    return call(
        lambda *refs: prepare(core(), *refs),
        tuple(shape(*dims) for dims in RESULTS + FACTORS),
        [scratch(*dims) for dims in FACTORS],
        [VMEM] * 5,
        (VMEM,) * 11,
    )(returned, *args)


def finish_call(core, other, prepared):
    return call(
        lambda *refs: finish(core(), *refs),
        (shape(COLS * GROUPS, LANES), shape(COLS, WIDTH)),
        [scratch(*dims) for dims in RESULTS]
        + [scratch(COLS * GROUPS, LANES), scratch(COLS, WIDTH), pltpu.SemaphoreType.DMA((5,))],
        [VMEM] * 12,
        (HBM, HBM),
    )(other, *prepared)


def on_device(ensemble, decay_rate, innovation, obs_weight):
    args = (ensemble, decay_rate, innovation, obs_weight)
    core = lambda: lax.axis_index("core")
    sent, *args = pack_call(lambda: 8 * lax.axis_index("core") + lax.axis_index("y"), *args)
    received = lax.all_to_all(sent, ("core", "y", "space"), 0, 0, tiled=True)
    results = own_call(received).reshape(CHIPS, 2, LANES)
    returned = lax.all_to_all(results, ("y", "space"), 0, 0, tiled=True).reshape(DEVICES, LANES)
    other = lax.ppermute(returned, "core", [(0, 1), (1, 0)])
    control, increment = finish_call(core, other, prepare_call(core, returned, *args))
    return control.reshape(1, COLS, WIDTH), increment


def solution(mesh):
    chips = jax.sharding.Mesh(mesh.devices.reshape(MEMBERS // 2, 2, TILES), ("y", "core", "space"))
    split = P(("y", "core"), "space", None)
    in_specs = (split, P("space", None), P("space", None), P("space", None))
    return jax.shard_map(
        on_device, mesh=chips, in_specs=in_specs, out_specs=(split, P("space", None)), check_vma=False
    )
```

```python
import jax
import jax.numpy as jnp
from jax import lax
from jax.experimental import pallas as pl
from jax.experimental.pallas import tpu as pltpu
from jax.sharding import PartitionSpec as P

MEMBERS, TILES, COLS, LINES = 16, 32, 28, 4
DEVICES = MEMBERS * TILES
ROWS = 32
LANES = 128
BLOCKS = DEVICES // LANES
GROUPS = LINES * BLOCKS
WIDTH = LINES * DEVICES
CHIPS, HALF = DEVICES // 2, WIDTH // 2
SEGMENT = 7
SEGMENTS = [range(start, start + SEGMENT) for start in range(0, COLS, SEGMENT)]
SCALARS = tuple(line * ROWS + COLS + 2 for line in range(LINES)) + (COLS + 3,)
VMEM = pl.BlockSpec(memory_space=pltpu.VMEM)
HBM = pl.BlockSpec(memory_space=pltpu.HBM)


def lane_block(line, block):
    start = (block // 2) * HALF + line * CHIPS + (block % 2) * LANES
    return slice(start, start + LANES)


def pack(place, ensemble_hbm, decay_hbm, innovation_hbm, weight_hbm, out_ref,
         ensemble_ref, weight_ref, eight_ref, last_ref, rows_ref, sems):
    quarter = lax.rem(place, 8)
    start = pl.multiple_of(8 * jnp.minimum(lax.div(quarter, 2), 2), 8)
    pairs = [(ensemble_hbm, ensemble_ref), (weight_hbm, weight_ref)]
    for i, hbm in enumerate((decay_hbm, innovation_hbm)):
        pairs.append((hbm.at[pl.ds(start, 8), :], eight_ref.at[i]))
        pairs.append((hbm.at[COLS - 4 : COLS, :], last_ref.at[i]))
    copies = [pltpu.make_async_copy(*pair, sems.at[i]) for i, pair in enumerate(pairs)]
    for copy in copies:
        copy.start()
    for copy in copies:
        copy.wait()
    rows_ref[:COLS, :] = ensemble_ref[0].astype(jnp.float32) * jnp.sqrt(weight_ref[...])

    def four(eight, last):
        inner = jnp.where(lax.rem(quarter, 2) == 0, eight[:4], eight[4:])
        return jnp.where(quarter >= 6, last, inner)

    scaled = jnp.sqrt(four(weight_ref[pl.ds(start, 8), :], weight_ref[COLS - 4 :, :])) * four(eight_ref[1], last_ref[1])
    rows_ref[COLS:, :] = jnp.where(place < 8, four(eight_ref[0], last_ref[0]), scaled)
    for block in range(BLOCKS):
        piece = jnp.concatenate([rows_ref[:, lane_block(line, block)] for line in range(LINES)], axis=0)
        out_ref[block * LANES : (block + 1) * LANES, :] = piece.T


def balanced(join, terms):
    while len(terms) > 1:
        terms = [join(*terms[i : i + 2]) if i + 1 < len(terms) else terms[i] for i in range(0, len(terms), 2)]
    return terms[0]


def add(x, y):
    return x + y


def spread(piece, lane_group):
    turned = [piece] + [pltpu.roll(piece, 32 * k, 1) for k in (1, 2, 3)]
    out = []
    for source in range(4):
        value = turned[(3 - source) % 4]
        for group in (2, 1, 0):
            value = jnp.where(lane_group == group, turned[(group - source) % 4], value)
        out.append(value)
    return out


def own_lines(in_ref, out_ref, rows_ref, members_ref, fields_ref, state_ref, first_ref):
    for block in range(BLOCKS):
        piece = slice(block * LANES, (block + 1) * LANES)
        rows_ref[piece, :] = in_ref[piece, :].T

    lane = lax.broadcasted_iota(jnp.int32, (8, LANES), 1)
    sub = lax.broadcasted_iota(jnp.int32, (8, LANES), 0)
    tile, lane_group = lane % TILES, lane // TILES
    low = sub < 4
    zero = jnp.zeros((8, LANES), jnp.float32)

    for c in range(COLS):
        value = rows_ref[pl.ds(c, 16, stride=ROWS), :]
        members_ref[c, 0], members_ref[c, 1] = value[:8], value[8:]

    RATE, SQUARED, AFTER, UPTO, INNOV, Z0, Z1 = range(7)

    def field(kind, c):
        return fields_ref[kind, c]

    for j in range(4):
        given = rows_ref[pl.ds(COLS + j, 16, stride=ROWS), :]
        for kind, value in ((RATE, given[:8]), (INNOV, given[8:])):
            other = pltpu.roll(value, 4, 0)
            for half, both in enumerate((jnp.where(low, value, other), jnp.where(low, other, value))):
                for source, copied in enumerate(spread(both, lane_group)):
                    c = 16 * half + 4 * source + j
                    if c < COLS:
                        fields_ref[kind, c] = copied

    one = zero + 1.0
    parts = []
    for columns in SEGMENTS:
        upto, after = one, one
        for c in columns:
            rate = field(RATE, c)
            fields_ref[SQUARED, c] = (1.0 - rate) * (1.0 + rate)
            upto = upto * rate
            fields_ref[UPTO, c] = upto
        for c in reversed(columns):
            fields_ref[AFTER, c] = after
            after = after * field(RATE, c)
        parts.append(upto)
    upto = balanced(lambda x, y: x * y, parts)

    def turn(value, k, backward):
        return pltpu.roll(value, LANES - k if backward else k, 1)

    def inside(k, backward):
        return tile < TILES - k if backward else tile >= k

    def factors(backward):
        out, product = [], one
        for k in range(1, TILES):
            out.append((k, jnp.where(inside(k, backward), product, 0.0)))
            product = product * turn(upto, k, backward)
        return out

    chains = {backward: factors(backward) for backward in (True, False)}

    def entering(values, backward):
        return [
            balanced(add, [factor * turn(value, k, backward) for k, factor in chains[backward]]) for value in values
        ]

    def through(ends, products, start):
        states = [start]
        for end, product in zip(ends, products):
            states.append(end if states[-1] is None else end + product * states[-1])
        return states

    def apply(source, target, on_state, on_field):
        ends = [[], []]
        for columns in reversed(SEGMENTS):
            carry = [None, None]
            for c in reversed(columns):
                rate, weight = field(RATE, c), field(source, c)
                for i in range(2):
                    summed = members_ref[c, i] * weight
                    summed = summed if carry[i] is None else summed + carry[i]
                    state_ref[c, i] = summed
                    carry[i] = rate * summed
            for i in range(2):
                ends[i].append(carry[i])
        from_right = entering([through(ends[i], parts[::-1], None)[-1] for i in range(2)], True)
        starts = [through(ends[i], parts[::-1], from_right[i])[:-1][::-1] for i in range(2)]
        ends = [[], []]
        for s, columns in enumerate(SEGMENTS):
            state = [None, None]
            for c in columns:
                rate, squared, after = field(RATE, c), field(SQUARED, c), field(AFTER, c)
                for i in range(2):
                    summed = state_ref[c, i] + after * starts[i][s]
                    driven = squared * summed
                    on_state(c, i, summed, driven)
                    state[i] = driven if state[i] is None else rate * state[i] + driven
                    state_ref[c, i] = state[i]
            for i in range(2):
                ends[i].append(state[i])
        from_left = entering([through(ends[i], parts, None)[-1] for i in range(2)], False)
        starts = [through(ends[i], parts, from_left[i])[:-1] for i in range(2)]
        for s, columns in reversed(list(enumerate(SEGMENTS))):
            for c in reversed(columns):
                upto = field(UPTO, c)
                total = add(*(members_ref[c, i] * (state_ref[c, i] + upto * starts[i][s]) for i in range(2)))
                total = total + pltpu.roll(total, 4, 0)
                total = total + pltpu.roll(total, 64, 1)
                total = total + pltpu.roll(total, 32, 1)
                fields_ref[target, c] = total
                on_field(c, total)
        return from_right

    def whole(value):
        return jnp.sum(jnp.sum(value, axis=0, keepdims=True), axis=1, keepdims=True)

    sums = {name: zero for name in ("alpha", "beta", "kappa", "energy", "cross")}

    def keep(c, i, summed, driven):
        first_ref[c, i] = summed
        sums["alpha"] += summed * driven

    def square(c, total):
        sums["beta"] += total * total

    right0 = apply(INNOV, Z0, keep, square)
    alpha = whole(sums["alpha"])
    beta = 0.125 * whole(sums["beta"])
    ratio = jnp.where(alpha > 0.0, beta / jnp.where(alpha > 0.0, alpha, 1.0), 0.0)
    ratio = jnp.broadcast_to(ratio, (8, LANES))

    def orthogonal(c, i, summed, driven):
        part = summed - ratio * first_ref[c, i]
        sums["kappa"] += field(SQUARED, c) * part * part

    def put(row, values):
        rows_ref[pl.ds(row, 16, stride=ROWS), :] = jnp.concatenate(values, axis=0)

    def compare(c, total):
        part = total - ratio * field(Z0, c)
        sums["energy"] += part * part
        sums["cross"] += part * field(Z0, c)
        put(c, [field(Z0, c), total])

    put(COLS, right0)
    put(COLS + 1, apply(Z0, Z1, orthogonal, compare))
    scalars = (alpha, beta, whole(sums["kappa"]), 0.125 * whole(sums["energy"]), 0.125 * whole(sums["cross"]))
    row = lax.broadcasted_iota(jnp.int32, (1, LANES), 1)
    last = jnp.zeros((1, LANES), jnp.float32)
    for place, value in zip(SCALARS, scalars):
        last = jnp.where(row == place, value, last)
    last = jnp.broadcast_to(last, (LANES, LANES))
    ours = lax.broadcasted_iota(jnp.int32, (LANES, LANES), 1) % ROWS >= COLS + 2
    for block in range(BLOCKS):
        piece = rows_ref[block * LANES : (block + 1) * LANES, :].T
        to = pl.ds((block % 2) * 2 * LANES + block // 2, LANES, stride=2)
        out_ref[to, :] = jnp.where(ours, last, piece)


def factors_of(at, ensemble_ref, decay_ref, innovation_ref, weight_ref, refs):
    inverse_ref, vector_ref, factor_ref, rate_ref, amplitude_ref, after_ref = refs
    for g in range(8):
        here = pl.ds(pl.multiple_of(at + g * LANES, LANES), LANES)
        group = pl.ds(g, COLS, stride=8)
        root = jnp.sqrt(weight_ref[:, here])
        inverse_ref[:, g * LANES : (g + 1) * LANES] = 1.0 / root
        factor = ensemble_ref[0, :, here].astype(jnp.float32) * root
        vector_ref[group, :] = factor * (root * innovation_ref[:, here])
        factor_ref[group, :] = factor
        rate = decay_ref[:, here]
        rate_ref[group, :] = rate
        amplitude_ref[group, :] = jnp.sqrt((1.0 - rate) * (1.0 + rate))
    for columns in SEGMENTS:
        after = jnp.ones((8, LANES), jnp.float32)
        for c in reversed(columns):
            part = slice(8 * c, 8 * c + 8)
            after_ref[part, :] = after
            after = after * rate_ref[part, :]


def one_half(core, in_ref, field0_ref, field1_ref, vector0_ref, vector1_ref, scalars_ref,
             inverse_ref, vector_ref, factor_ref, rate_ref, amplitude_ref, after_ref):
    rows = [None] * 8
    for j in range(2):
        pieces = [in_ref[pl.ds(2 * j * LANES + h, LANES, stride=2), :].T for h in range(2)]
        for line in range(LINES):
            g = 2 * line + j
            part = slice(g * LANES, (g + 1) * LANES)
            z0, z1 = (piece[line * ROWS : line * ROWS + COLS] for piece in pieces)
            inverse = inverse_ref[:, part]
            field0_ref[:, part] = inverse * z0
            field1_ref[:, part] = inverse * z1
            vector1_ref[pl.ds(g, COLS, stride=8), :] = z0
            states = [piece[line * ROWS + COLS : line * ROWS + COLS + 2] for piece in pieces]
            rows[g] = jnp.where(core == 0, *states)
        for i, place in enumerate(SCALARS):
            scalars_ref[i : i + 1, j * LANES : (j + 1) * LANES] = pieces[0][place : place + 1]
    entering = [jnp.concatenate([row[i : i + 1] for row in rows], axis=0) for i in range(2)]
    for columns in reversed(SEGMENTS):
        carry = [None, None]
        for c in reversed(columns):
            part = slice(8 * c, 8 * c + 8)
            for i, value in enumerate((vector_ref[part, :], factor_ref[part, :] * vector1_ref[part, :])):
                summed = value if carry[i] is None else value + carry[i]
                carry[i] = rate_ref[part, :] * summed
                (vector0_ref, vector1_ref)[i][part, :] = summed
        for c in columns:
            part = slice(8 * c, 8 * c + 8)
            for ref, state in zip((vector0_ref, vector1_ref), entering):
                ref[part, :] = amplitude_ref[part, :] * (ref[part, :] + after_ref[part, :] * state)
        first = slice(8 * columns[0], 8 * columns[0] + 8)
        product = rate_ref[first, :] * after_ref[first, :]
        entering = [end + product * state for end, state in zip(carry, entering)]


def prepare(core, in_ref, *refs):
    args, half, other, own = refs[:4], refs[4:9], refs[9:15], refs[15:]
    factors_of(core * HALF, *args, own)
    one_half(core, in_ref, *half, *own)
    factors_of((1 - core) * HALF, *args, other)


def finish(core, in_ref, *refs):
    own, factors = refs[:5], refs[5:11]
    control_hbm, increment_hbm = refs[11:13]
    other = refs[13:18]
    control_ref, increment_ref, sems = refs[18:]
    one_half(core, in_ref, *other, *factors)

    def whole(value):
        return jnp.sum(value, axis=1, keepdims=True)

    def both(i):
        return jnp.concatenate([ref[i : i + 1, :] for ref in (own[4], other[4])], axis=1)

    alphas, betas, kappas, energies, crosses = (both(i) for i in range(5))
    alpha, beta = whole(alphas), whole(betas)
    ratio = beta / alpha
    shift = jnp.where(alphas > 0.0, betas / jnp.where(alphas > 0.0, alphas, 1.0), 0.0) - ratio
    kappa = whole(kappas + alphas * shift * shift)
    energy = whole(energies + shift * (2.0 * crosses + shift * betas))
    step = alpha / (alpha + beta)
    curvature = kappa + energy - step * kappa * (kappa / alpha)
    back = jnp.where(curvature > 0.0, step * kappa / jnp.where(curvature > 0.0, curvature, 1.0), 0.0)
    ahead = step + back * (ratio + step * (kappa / alpha))

    copies = []

    def send(source, target):
        copies.append(pltpu.make_async_copy(source, target, sems.at[len(copies)]))
        copies[-1].start()

    for at, (field0_ref, field1_ref, *_) in ((core, own), (1 - core, other)):
        here = pl.ds(pl.multiple_of(at * HALF, HALF), HALF)
        increment_ref[:, here] = ahead * field0_ref[...] - back * field1_ref[...]
    send(increment_ref, increment_hbm)
    for quarter in range(4):
        for c in range(7 * quarter, 7 * quarter + 7):
            for at, (_, _, vector0_ref, vector1_ref, _) in ((core, own), (1 - core, other)):
                part = slice(8 * c, 8 * c + 8)
                here = pl.ds(pl.multiple_of(c * GROUPS + 8 * at, 8), 8)
                control_ref[here, :] = ahead * vector0_ref[part, :] - back * vector1_ref[part, :]
        part = slice(7 * quarter * GROUPS, (7 * quarter + 7) * GROUPS)
        send(control_ref.at[part, :], control_hbm.at[part, :])
    for copy in copies:
        copy.wait()


def shape(*dims):
    return jax.ShapeDtypeStruct(dims, jnp.float32)


def scratch(*dims):
    return pltpu.VMEM(dims, jnp.float32)


def call(kernel, out_shape, scratch_shapes, in_specs, out_specs):
    return pl.pallas_call(
        kernel,
        out_shape=out_shape,
        in_specs=in_specs,
        out_specs=out_specs,
        scratch_shapes=scratch_shapes,
        compiler_params=pltpu.CompilerParams(vmem_limit_bytes=32 * 1024 * 1024),
    )


def pack_call(place, *args):
    return call(
        lambda *refs: pack(place(), *refs),
        shape(DEVICES, LANES),
        [pltpu.VMEM((1, COLS, WIDTH), jnp.bfloat16)]
        + [scratch(COLS, WIDTH), scratch(2, 8, WIDTH), scratch(2, 4, WIDTH)]
        + [scratch(ROWS, WIDTH), pltpu.SemaphoreType.DMA((6,))],
        [HBM] * 4,
        VMEM,
    )(*(pltpu.with_memory_space_constraint(value, pltpu.HBM) for value in args))


def own_call(received):
    return call(
        own_lines,
        shape(DEVICES, LANES),
        [
            scratch(DEVICES, LANES),
            scratch(COLS, 2, 8, LANES),
            scratch(7, COLS, 8, LANES),
            scratch(COLS, 2, 8, LANES),
            scratch(COLS, 2, 8, LANES),
        ],
        [VMEM],
        VMEM,
    )(received)


BY_COLUMN = (COLS * 8, LANES)
RESULTS = ((COLS, HALF), (COLS, HALF), BY_COLUMN, BY_COLUMN, (8, CHIPS))
FACTORS = ((COLS, HALF), BY_COLUMN, BY_COLUMN, BY_COLUMN, BY_COLUMN, BY_COLUMN)


def prepare_call(core, returned, *args):
    return call(
        lambda *refs: prepare(core(), *refs),
        tuple(shape(*dims) for dims in RESULTS + FACTORS),
        [scratch(*dims) for dims in FACTORS],
        [VMEM] * 5,
        (VMEM,) * 11,
    )(returned, *args)


def finish_call(core, other, prepared):
    return call(
        lambda *refs: finish(core(), *refs),
        (shape(COLS * GROUPS, LANES), shape(COLS, WIDTH)),
        [scratch(*dims) for dims in RESULTS]
        + [scratch(COLS * GROUPS, LANES), scratch(COLS, WIDTH), pltpu.SemaphoreType.DMA((5,))],
        [VMEM] * 12,
        (HBM, HBM),
    )(other, *prepared)


def on_device(ensemble, decay_rate, innovation, obs_weight):
    args = (ensemble, decay_rate, innovation, obs_weight)
    core = lambda: lax.axis_index("core")
    sent = pack_call(lambda: 8 * lax.axis_index("core") + lax.axis_index("y"), *args)
    received = lax.all_to_all(sent, ("core", "y", "space"), 0, 0, tiled=True)
    results = own_call(received).reshape(CHIPS, 2 * LANES)
    returned = lax.all_to_all(results, ("y", "space"), 0, 0, tiled=True).reshape(DEVICES, LANES)
    other = lax.ppermute(returned, "core", [(0, 1), (1, 0)])
    control, increment = finish_call(core, other, prepare_call(core, returned, *args))
    return control.reshape(1, COLS, WIDTH), increment


def solution(mesh):
    chips = jax.sharding.Mesh(mesh.devices.reshape(MEMBERS // 2, 2, TILES), ("y", "core", "space"))
    split = P(("y", "core"), "space", None)
    in_specs = (split, P("space", None), P("space", None), P("space", None))
    return jax.shard_map(
        on_device, mesh=chips, in_specs=in_specs, out_specs=(split, P("space", None)), check_vma=False
    )
```

```python
import jax
import jax.numpy as jnp
from jax import lax
from jax.experimental import pallas as pl
from jax.experimental.pallas import tpu as pltpu
from jax.sharding import PartitionSpec as P

MEMBERS, TILES, COLS, LINES = 16, 32, 28, 4
DEVICES = MEMBERS * TILES
ROWS = 32
LANES = 128
BLOCKS = DEVICES // LANES
GROUPS = LINES * BLOCKS
WIDTH = LINES * DEVICES
CHIPS, HALF = DEVICES // 2, WIDTH // 2
SEGMENT = 7
SEGMENTS = [range(start, start + SEGMENT) for start in range(0, COLS, SEGMENT)]
SCALARS = tuple(line * ROWS + COLS + 2 for line in range(LINES)) + (COLS + 3,)
VMEM = pl.BlockSpec(memory_space=pltpu.VMEM)
HBM = pl.BlockSpec(memory_space=pltpu.HBM)


def lane_block(line, block):
    start = (block // 2) * HALF + line * CHIPS + (block % 2) * LANES
    return slice(start, start + LANES)


def pack(place, ensemble_hbm, decay_hbm, innovation_hbm, weight_hbm, out_ref,
         ensemble_ref, weight_ref, eight_ref, last_ref, rows_ref, sems):
    quarter = lax.rem(place, 8)
    start = pl.multiple_of(8 * jnp.minimum(lax.div(quarter, 2), 2), 8)
    pairs = [(ensemble_hbm, ensemble_ref), (weight_hbm, weight_ref)]
    for i, hbm in enumerate((decay_hbm, innovation_hbm)):
        pairs.append((hbm.at[pl.ds(start, 8), :], eight_ref.at[i]))
        pairs.append((hbm.at[COLS - 4 : COLS, :], last_ref.at[i]))
    copies = [pltpu.make_async_copy(*pair, sems.at[i]) for i, pair in enumerate(pairs)]
    for copy in copies:
        copy.start()
    for copy in copies:
        copy.wait()
    rows_ref[:COLS, :] = ensemble_ref[0].astype(jnp.float32) * jnp.sqrt(weight_ref[...])

    def four(eight, last):
        inner = jnp.where(lax.rem(quarter, 2) == 0, eight[:4], eight[4:])
        return jnp.where(quarter >= 6, last, inner)

    scaled = jnp.sqrt(four(weight_ref[pl.ds(start, 8), :], weight_ref[COLS - 4 :, :])) * four(eight_ref[1], last_ref[1])
    rows_ref[COLS:, :] = jnp.where(place < 8, four(eight_ref[0], last_ref[0]), scaled)
    for block in range(BLOCKS):
        piece = jnp.concatenate([rows_ref[:, lane_block(line, block)] for line in range(LINES)], axis=0)
        out_ref[block * LANES : (block + 1) * LANES, :] = piece.T


def balanced(join, terms):
    while len(terms) > 1:
        terms = [join(*terms[i : i + 2]) if i + 1 < len(terms) else terms[i] for i in range(0, len(terms), 2)]
    return terms[0]


def add(x, y):
    return x + y


def spread(piece, lane_group):
    turned = [piece] + [pltpu.roll(piece, 32 * k, 1) for k in (1, 2, 3)]
    out = []
    for source in range(4):
        value = turned[(3 - source) % 4]
        for group in (2, 1, 0):
            value = jnp.where(lane_group == group, turned[(group - source) % 4], value)
        out.append(value)
    return out


def own_lines(in_ref, out_ref, rows_ref, members_ref, fields_ref, state_ref, first_ref):
    for block in range(BLOCKS):
        piece = slice(block * LANES, (block + 1) * LANES)
        rows_ref[piece, :] = in_ref[piece, :].T

    lane = lax.broadcasted_iota(jnp.int32, (8, LANES), 1)
    sub = lax.broadcasted_iota(jnp.int32, (8, LANES), 0)
    tile, lane_group = lane % TILES, lane // TILES
    low = sub < 4
    zero = jnp.zeros((8, LANES), jnp.float32)

    for c in range(COLS):
        value = rows_ref[pl.ds(c, 16, stride=ROWS), :]
        members_ref[c, 0], members_ref[c, 1] = value[:8], value[8:]

    RATE, SQUARED, AFTER, UPTO, INNOV, Z0, Z1 = range(7)

    def field(kind, c):
        return fields_ref[kind, c]

    for j in range(4):
        given = rows_ref[pl.ds(COLS + j, 16, stride=ROWS), :]
        for kind, value in ((RATE, given[:8]), (INNOV, given[8:])):
            other = pltpu.roll(value, 4, 0)
            for half, both in enumerate((jnp.where(low, value, other), jnp.where(low, other, value))):
                for source, copied in enumerate(spread(both, lane_group)):
                    c = 16 * half + 4 * source + j
                    if c < COLS:
                        fields_ref[kind, c] = copied

    one = zero + 1.0
    parts = []
    for columns in SEGMENTS:
        upto, after = one, one
        for c in columns:
            rate = field(RATE, c)
            fields_ref[SQUARED, c] = (1.0 - rate) * (1.0 + rate)
            upto = upto * rate
            fields_ref[UPTO, c] = upto
        for c in reversed(columns):
            fields_ref[AFTER, c] = after
            after = after * field(RATE, c)
        parts.append(upto)
    upto = balanced(lambda x, y: x * y, parts)

    def turn(value, k, backward):
        return pltpu.roll(value, LANES - k if backward else k, 1)

    def inside(k, backward):
        return tile < TILES - k if backward else tile >= k

    def factors(backward):
        out, product = [], one
        for k in range(1, TILES):
            out.append((k, jnp.where(inside(k, backward), product, 0.0)))
            product = product * turn(upto, k, backward)
        return out

    chains = {backward: factors(backward) for backward in (True, False)}

    def entering(values, backward):
        return [
            balanced(add, [factor * turn(value, k, backward) for k, factor in chains[backward]]) for value in values
        ]

    def through(ends, products, start):
        states = [start]
        for end, product in zip(ends, products):
            states.append(end if states[-1] is None else end + product * states[-1])
        return states

    def apply(source, target, on_state, on_field):
        ends = [[], []]
        for columns in reversed(SEGMENTS):
            carry = [None, None]
            for c in reversed(columns):
                rate, weight = field(RATE, c), field(source, c)
                for i in range(2):
                    summed = members_ref[c, i] * weight
                    summed = summed if carry[i] is None else summed + carry[i]
                    state_ref[c, i] = summed
                    carry[i] = rate * summed
            for i in range(2):
                ends[i].append(carry[i])
        from_right = entering([through(ends[i], parts[::-1], None)[-1] for i in range(2)], True)
        starts = [through(ends[i], parts[::-1], from_right[i])[:-1][::-1] for i in range(2)]
        ends = [[], []]
        for s, columns in enumerate(SEGMENTS):
            state = [None, None]
            for c in columns:
                rate, squared, after = field(RATE, c), field(SQUARED, c), field(AFTER, c)
                for i in range(2):
                    summed = state_ref[c, i] + after * starts[i][s]
                    driven = squared * summed
                    on_state(c, i, summed, driven)
                    state[i] = driven if state[i] is None else rate * state[i] + driven
                    state_ref[c, i] = state[i]
            for i in range(2):
                ends[i].append(state[i])
        from_left = entering([through(ends[i], parts, None)[-1] for i in range(2)], False)
        starts = [through(ends[i], parts, from_left[i])[:-1] for i in range(2)]
        for s, columns in reversed(list(enumerate(SEGMENTS))):
            for c in reversed(columns):
                upto = field(UPTO, c)
                total = add(*(members_ref[c, i] * (state_ref[c, i] + upto * starts[i][s]) for i in range(2)))
                total = total + pltpu.roll(total, 4, 0)
                total = total + pltpu.roll(total, 64, 1)
                total = total + pltpu.roll(total, 32, 1)
                fields_ref[target, c] = total
                on_field(c, total)
        return from_right

    def whole(value):
        return jnp.sum(jnp.sum(value, axis=0, keepdims=True), axis=1, keepdims=True)

    sums = {name: zero for name in ("alpha", "beta", "kappa", "energy", "cross")}

    def keep(c, i, summed, driven):
        first_ref[c, i] = summed
        sums["alpha"] += summed * driven

    def square(c, total):
        sums["beta"] += total * total

    right0 = apply(INNOV, Z0, keep, square)
    alpha = whole(sums["alpha"])
    beta = 0.125 * whole(sums["beta"])
    ratio = jnp.where(alpha > 0.0, beta / jnp.where(alpha > 0.0, alpha, 1.0), 0.0)
    ratio = jnp.broadcast_to(ratio, (8, LANES))

    def orthogonal(c, i, summed, driven):
        part = summed - ratio * first_ref[c, i]
        sums["kappa"] += field(SQUARED, c) * part * part

    def put(row, values):
        rows_ref[pl.ds(row, 16, stride=ROWS), :] = jnp.concatenate(values, axis=0)

    def compare(c, total):
        part = total - ratio * field(Z0, c)
        sums["energy"] += part * part
        sums["cross"] += part * field(Z0, c)
        put(c, [field(Z0, c), total])

    put(COLS, right0)
    put(COLS + 1, apply(Z0, Z1, orthogonal, compare))
    scalars = (alpha, beta, whole(sums["kappa"]), 0.125 * whole(sums["energy"]), 0.125 * whole(sums["cross"]))
    row = lax.broadcasted_iota(jnp.int32, (1, LANES), 1)
    last = jnp.zeros((1, LANES), jnp.float32)
    for place, value in zip(SCALARS, scalars):
        last = jnp.where(row == place, value, last)
    last = jnp.broadcast_to(last, (LANES, LANES))
    ours = lax.broadcasted_iota(jnp.int32, (LANES, LANES), 1) % ROWS >= COLS + 2
    for block in range(BLOCKS):
        piece = rows_ref[block * LANES : (block + 1) * LANES, :].T
        to = pl.ds((block % 2) * 2 * LANES + block // 2, LANES, stride=2)
        out_ref[to, :] = jnp.where(ours, last, piece)


def factors_of(at, ensemble_ref, decay_ref, innovation_ref, weight_ref, refs):
    inverse_ref, vector_ref, factor_ref, rate_ref, amplitude_ref, after_ref = refs
    for g in range(8):
        here = pl.ds(pl.multiple_of(at + g * LANES, LANES), LANES)
        group = pl.ds(g, COLS, stride=8)
        root = jnp.sqrt(weight_ref[:, here])
        inverse_ref[:COLS, g * LANES : (g + 1) * LANES] = 1.0 / root
        factor = ensemble_ref[0, :, here].astype(jnp.float32) * root
        vector_ref[group, :] = factor * (root * innovation_ref[:, here])
        factor_ref[group, :] = factor
        rate = decay_ref[:, here]
        rate_ref[group, :] = rate
        amplitude_ref[group, :] = jnp.sqrt((1.0 - rate) * (1.0 + rate))
    for columns in SEGMENTS:
        after = jnp.ones((8, LANES), jnp.float32)
        for c in reversed(columns):
            part = slice(8 * c, 8 * c + 8)
            after_ref[part, :] = after
            after = after * rate_ref[part, :]


def one_half(core, in_ref, field0_ref, field1_ref, vector0_ref, vector1_ref, scalars_ref,
             inverse_ref, vector_ref, factor_ref, rate_ref, amplitude_ref, after_ref):
    rows = [None] * 8
    for j in range(2):
        pieces = [in_ref[pl.ds(2 * j * LANES + h, LANES, stride=2), :].T for h in range(2)]
        for line in range(LINES):
            g = 2 * line + j
            part = slice(g * LANES, (g + 1) * LANES)
            z0, z1 = (piece[line * ROWS : line * ROWS + COLS] for piece in pieces)
            inverse = inverse_ref[:COLS, part]
            field0_ref[:COLS, part] = inverse * z0
            field1_ref[:COLS, part] = inverse * z1
            vector1_ref[pl.ds(g, COLS, stride=8), :] = z0
            states = [piece[line * ROWS + COLS : line * ROWS + COLS + 2] for piece in pieces]
            rows[g] = jnp.where(core == 0, *states)
        for i, place in enumerate(SCALARS):
            scalars_ref[i : i + 1, j * LANES : (j + 1) * LANES] = pieces[0][place : place + 1]
    entering = [jnp.concatenate([row[i : i + 1] for row in rows], axis=0) for i in range(2)]
    for columns in reversed(SEGMENTS):
        carry = [None, None]
        for c in reversed(columns):
            part = slice(8 * c, 8 * c + 8)
            for i, value in enumerate((vector_ref[part, :], factor_ref[part, :] * vector1_ref[part, :])):
                summed = value if carry[i] is None else value + carry[i]
                carry[i] = rate_ref[part, :] * summed
                (vector0_ref, vector1_ref)[i][part, :] = summed
        for c in columns:
            part = slice(8 * c, 8 * c + 8)
            for ref, state in zip((vector0_ref, vector1_ref), entering):
                ref[part, :] = amplitude_ref[part, :] * (ref[part, :] + after_ref[part, :] * state)
        first = slice(8 * columns[0], 8 * columns[0] + 8)
        product = rate_ref[first, :] * after_ref[first, :]
        entering = [end + product * state for end, state in zip(carry, entering)]


def prepare(core, in_ref, *refs):
    args, half, other, own = refs[:4], refs[4:9], refs[9:15], refs[15:]
    factors_of(core * HALF, *args, own)
    one_half(core, in_ref, *half, *own)
    factors_of((1 - core) * HALF, *args, other)


def finish(core, in_ref, *refs):
    own, factors = refs[:5], refs[5:11]
    control_hbm, increment_hbm = refs[11:13]
    other = refs[13:18]
    control_ref, increment_ref, sems = refs[18:]
    one_half(core, in_ref, *other, *factors)

    def whole(value):
        return jnp.sum(value, axis=1, keepdims=True)

    def both(i):
        return jnp.concatenate([ref[i : i + 1, :] for ref in (own[4], other[4])], axis=1)

    alphas, betas, kappas, energies, crosses = (both(i) for i in range(5))
    alpha, beta = whole(alphas), whole(betas)
    ratio = beta / alpha
    shift = jnp.where(alphas > 0.0, betas / jnp.where(alphas > 0.0, alphas, 1.0), 0.0) - ratio
    kappa = whole(kappas + alphas * shift * shift)
    energy = whole(energies + shift * (2.0 * crosses + shift * betas))
    step = alpha / (alpha + beta)
    curvature = kappa + energy - step * kappa * (kappa / alpha)
    back = jnp.where(curvature > 0.0, step * kappa / jnp.where(curvature > 0.0, curvature, 1.0), 0.0)
    ahead = step + back * (ratio + step * (kappa / alpha))

    copies = []

    def send(source, target):
        copies.append(pltpu.make_async_copy(source, target, sems.at[len(copies)]))
        copies[-1].start()

    for at, (field0_ref, field1_ref, *_) in ((core, own), (1 - core, other)):
        here = pl.ds(pl.multiple_of(at * HALF, HALF), HALF)
        increment_ref[:, here] = ahead * field0_ref[:COLS, :] - back * field1_ref[:COLS, :]
    send(increment_ref, increment_hbm)
    for quarter in range(4):
        for c in range(7 * quarter, 7 * quarter + 7):
            for at, (_, _, vector0_ref, vector1_ref, _) in ((core, own), (1 - core, other)):
                part = slice(8 * c, 8 * c + 8)
                here = pl.ds(pl.multiple_of(c * GROUPS + 8 * at, 8), 8)
                control_ref[here, :] = ahead * vector0_ref[part, :] - back * vector1_ref[part, :]
        part = slice(7 * quarter * GROUPS, (7 * quarter + 7) * GROUPS)
        send(control_ref.at[part, :], control_hbm.at[part, :])
    for copy in copies:
        copy.wait()


def shape(*dims):
    return jax.ShapeDtypeStruct(dims, jnp.float32)


def scratch(*dims):
    return pltpu.VMEM(dims, jnp.float32)


def call(kernel, out_shape, scratch_shapes, in_specs, out_specs):
    return pl.pallas_call(
        kernel,
        out_shape=out_shape,
        in_specs=in_specs,
        out_specs=out_specs,
        scratch_shapes=scratch_shapes,
        compiler_params=pltpu.CompilerParams(vmem_limit_bytes=32 * 1024 * 1024),
    )


def pack_call(place, *args):
    return call(
        lambda *refs: pack(place(), *refs),
        shape(DEVICES, LANES),
        [pltpu.VMEM((1, COLS, WIDTH), jnp.bfloat16)]
        + [scratch(COLS, WIDTH), scratch(2, 8, WIDTH), scratch(2, 4, WIDTH)]
        + [scratch(ROWS, WIDTH), pltpu.SemaphoreType.DMA((6,))],
        [HBM] * 4,
        VMEM,
    )(*(pltpu.with_memory_space_constraint(value, pltpu.HBM) for value in args))


def own_call(received):
    return call(
        own_lines,
        shape(DEVICES, LANES),
        [
            scratch(DEVICES, LANES),
            scratch(COLS, 2, 8, LANES),
            scratch(7, COLS, 8, LANES),
            scratch(COLS, 2, 8, LANES),
            scratch(COLS, 2, 8, LANES),
        ],
        [VMEM],
        VMEM,
    )(received)


BY_COLUMN = (ROWS * 8, LANES)
RESULTS = ((ROWS, HALF), (ROWS, HALF), BY_COLUMN, BY_COLUMN, (8, CHIPS))
FACTORS = ((ROWS, HALF), BY_COLUMN, BY_COLUMN, BY_COLUMN, BY_COLUMN, BY_COLUMN)


def prepare_call(core, returned, *args):
    return call(
        lambda *refs: prepare(core(), *refs),
        tuple(shape(*dims) for dims in RESULTS + FACTORS),
        [scratch(*dims) for dims in FACTORS],
        [VMEM] * 5,
        (VMEM,) * 11,
    )(returned, *args)


def finish_call(core, other, prepared):
    return call(
        lambda *refs: finish(core(), *refs),
        (shape(COLS * GROUPS, LANES), shape(COLS, WIDTH)),
        [scratch(*dims) for dims in RESULTS]
        + [scratch(COLS * GROUPS, LANES), scratch(COLS, WIDTH), pltpu.SemaphoreType.DMA((5,))],
        [VMEM] * 12,
        (HBM, HBM),
    )(other, *prepared)


def on_device(ensemble, decay_rate, innovation, obs_weight):
    args = (ensemble, decay_rate, innovation, obs_weight)
    core = lambda: lax.axis_index("core")
    sent = pack_call(lambda: 8 * lax.axis_index("core") + lax.axis_index("y"), *args)
    received = lax.all_to_all(sent, ("core", "y", "space"), 0, 0, tiled=True)
    results = own_call(received).reshape(CHIPS, 2 * LANES)
    returned = lax.all_to_all(results, ("y", "space"), 0, 0, tiled=True).reshape(DEVICES, LANES)
    other = lax.ppermute(returned, "core", [(0, 1), (1, 0)])
    control, increment = finish_call(core, other, prepare_call(core, returned, *args))
    return control.reshape(1, COLS, WIDTH), increment


def solution(mesh):
    chips = jax.sharding.Mesh(mesh.devices.reshape(MEMBERS // 2, 2, TILES), ("y", "core", "space"))
    split = P(("y", "core"), "space", None)
    in_specs = (split, P("space", None), P("space", None), P("space", None))
    return jax.shard_map(
        on_device, mesh=chips, in_specs=in_specs, out_specs=(split, P("space", None)), check_vma=False
    )
```

```python
import jax
import jax.numpy as jnp
from jax import lax
from jax.experimental import pallas as pl
from jax.experimental.pallas import tpu as pltpu
from jax.sharding import PartitionSpec as P

MEMBERS, TILES, COLS, LINES = 16, 32, 28, 4
XS, ZS = 4, 8
DEVICES = MEMBERS * TILES
ROWS = 32
LANES = 128
BLOCKS = DEVICES // LANES
GROUPS = LINES * BLOCKS
WIDTH = LINES * DEVICES
CHIPS, HALF = DEVICES // 2, WIDTH // 2
SEGMENT = 7
SEGMENTS = [range(start, start + SEGMENT) for start in range(0, COLS, SEGMENT)]
SCALARS = tuple(line * ROWS + COLS + 2 for line in range(LINES)) + (COLS + 3,)
VMEM = pl.BlockSpec(memory_space=pltpu.VMEM)
HBM = pl.BlockSpec(memory_space=pltpu.HBM)


def lane_block(line, block):
    start = (block // 2) * HALF + line * CHIPS + (block % 2) * LANES
    return slice(start, start + LANES)


def pack(place, ensemble_hbm, decay_hbm, innovation_hbm, weight_hbm, out_ref,
         ensemble_ref, weight_ref, eight_ref, last_ref, rows_ref, sems):
    quarter = lax.rem(place, 8)
    start = pl.multiple_of(8 * jnp.minimum(lax.div(quarter, 2), 2), 8)
    pairs = [(ensemble_hbm, ensemble_ref), (weight_hbm, weight_ref)]
    for i, hbm in enumerate((decay_hbm, innovation_hbm)):
        pairs.append((hbm.at[pl.ds(start, 8), :], eight_ref.at[i]))
        pairs.append((hbm.at[COLS - 4 : COLS, :], last_ref.at[i]))
    copies = [pltpu.make_async_copy(*pair, sems.at[i]) for i, pair in enumerate(pairs)]
    for copy in copies:
        copy.start()
    for copy in copies:
        copy.wait()
    rows_ref[:COLS, :] = ensemble_ref[0].astype(jnp.float32) * jnp.sqrt(weight_ref[...])

    def four(eight, last):
        inner = jnp.where(lax.rem(quarter, 2) == 0, eight[:4], eight[4:])
        return jnp.where(quarter >= 6, last, inner)

    scaled = jnp.sqrt(four(weight_ref[pl.ds(start, 8), :], weight_ref[COLS - 4 :, :])) * four(eight_ref[1], last_ref[1])
    rows_ref[COLS:, :] = jnp.where(place < 8, four(eight_ref[0], last_ref[0]), scaled)
    for block in range(BLOCKS):
        piece = jnp.concatenate([rows_ref[:, lane_block(line, block)] for line in range(LINES)], axis=0).T
        for half in range(2):
            x = 2 * (block % 2) + half
            to = pl.ds((block // 2) * CHIPS + x, CHIPS // XS, stride=XS)
            out_ref[to, :] = piece[half * CHIPS // XS : (half + 1) * CHIPS // XS]


def balanced(join, terms):
    while len(terms) > 1:
        terms = [join(*terms[i : i + 2]) if i + 1 < len(terms) else terms[i] for i in range(0, len(terms), 2)]
    return terms[0]


def add(x, y):
    return x + y


def spread(piece, lane_group):
    turned = [piece] + [pltpu.roll(piece, 32 * k, 1) for k in (1, 2, 3)]
    out = []
    for source in range(4):
        value = turned[(3 - source) % 4]
        for group in (2, 1, 0):
            value = jnp.where(lane_group == group, turned[(group - source) % 4], value)
        out.append(value)
    return out


def own_lines(in_ref, out_ref, rows_ref, members_ref, fields_ref, state_ref, first_ref):
    for block in range(BLOCKS):
        piece = slice(block * LANES, (block + 1) * LANES)
        rows_ref[piece, :] = in_ref[piece, :].T

    lane = lax.broadcasted_iota(jnp.int32, (8, LANES), 1)
    sub = lax.broadcasted_iota(jnp.int32, (8, LANES), 0)
    tile, lane_group = lane % TILES, lane // TILES
    low = sub < 4
    zero = jnp.zeros((8, LANES), jnp.float32)

    for c in range(COLS):
        value = rows_ref[pl.ds(c, 16, stride=ROWS), :]
        members_ref[c, 0], members_ref[c, 1] = value[:8], value[8:]

    RATE, SQUARED, AFTER, UPTO, INNOV, Z0, Z1 = range(7)

    def field(kind, c):
        return fields_ref[kind, c]

    for j in range(4):
        given = rows_ref[pl.ds(COLS + j, 16, stride=ROWS), :]
        for kind, value in ((RATE, given[:8]), (INNOV, given[8:])):
            other = pltpu.roll(value, 4, 0)
            for half, both in enumerate((jnp.where(low, value, other), jnp.where(low, other, value))):
                for source, copied in enumerate(spread(both, lane_group)):
                    c = 16 * half + 4 * source + j
                    if c < COLS:
                        fields_ref[kind, c] = copied

    one = zero + 1.0
    parts = []
    for columns in SEGMENTS:
        upto, after = one, one
        for c in columns:
            rate = field(RATE, c)
            fields_ref[SQUARED, c] = (1.0 - rate) * (1.0 + rate)
            upto = upto * rate
            fields_ref[UPTO, c] = upto
        for c in reversed(columns):
            fields_ref[AFTER, c] = after
            after = after * field(RATE, c)
        parts.append(upto)
    upto = balanced(lambda x, y: x * y, parts)

    def turn(value, k, backward):
        return pltpu.roll(value, LANES - k if backward else k, 1)

    def inside(k, backward):
        return tile < TILES - k if backward else tile >= k

    def factors(backward):
        out, product = [], one
        for k in range(1, TILES):
            out.append((k, jnp.where(inside(k, backward), product, 0.0)))
            product = product * turn(upto, k, backward)
        return out

    chains = {backward: factors(backward) for backward in (True, False)}

    def entering(values, backward):
        return [
            balanced(add, [factor * turn(value, k, backward) for k, factor in chains[backward]]) for value in values
        ]

    def through(ends, products, start):
        states = [start]
        for end, product in zip(ends, products):
            states.append(end if states[-1] is None else end + product * states[-1])
        return states

    def apply(source, target, on_state, on_field):
        ends = [[], []]
        for columns in reversed(SEGMENTS):
            carry = [None, None]
            for c in reversed(columns):
                rate, weight = field(RATE, c), field(source, c)
                for i in range(2):
                    summed = members_ref[c, i] * weight
                    summed = summed if carry[i] is None else summed + carry[i]
                    state_ref[c, i] = summed
                    carry[i] = rate * summed
            for i in range(2):
                ends[i].append(carry[i])
        from_right = entering([through(ends[i], parts[::-1], None)[-1] for i in range(2)], True)
        starts = [through(ends[i], parts[::-1], from_right[i])[:-1][::-1] for i in range(2)]
        ends = [[], []]
        for s, columns in enumerate(SEGMENTS):
            state = [None, None]
            for c in columns:
                rate, squared, after = field(RATE, c), field(SQUARED, c), field(AFTER, c)
                for i in range(2):
                    summed = state_ref[c, i] + after * starts[i][s]
                    driven = squared * summed
                    on_state(c, i, summed, driven)
                    state[i] = driven if state[i] is None else rate * state[i] + driven
                    state_ref[c, i] = state[i]
            for i in range(2):
                ends[i].append(state[i])
        from_left = entering([through(ends[i], parts, None)[-1] for i in range(2)], False)
        starts = [through(ends[i], parts, from_left[i])[:-1] for i in range(2)]
        for s, columns in reversed(list(enumerate(SEGMENTS))):
            for c in reversed(columns):
                upto = field(UPTO, c)
                total = add(*(members_ref[c, i] * (state_ref[c, i] + upto * starts[i][s]) for i in range(2)))
                total = total + pltpu.roll(total, 4, 0)
                total = total + pltpu.roll(total, 64, 1)
                total = total + pltpu.roll(total, 32, 1)
                fields_ref[target, c] = total
                on_field(c, total)
        return from_right

    def whole(value):
        return jnp.sum(jnp.sum(value, axis=0, keepdims=True), axis=1, keepdims=True)

    sums = {name: zero for name in ("alpha", "beta", "kappa", "energy", "cross")}

    def keep(c, i, summed, driven):
        first_ref[c, i] = summed
        sums["alpha"] += summed * driven

    def square(c, total):
        sums["beta"] += total * total

    right0 = apply(INNOV, Z0, keep, square)
    alpha = whole(sums["alpha"])
    beta = 0.125 * whole(sums["beta"])
    ratio = jnp.where(alpha > 0.0, beta / jnp.where(alpha > 0.0, alpha, 1.0), 0.0)
    ratio = jnp.broadcast_to(ratio, (8, LANES))

    def orthogonal(c, i, summed, driven):
        part = summed - ratio * first_ref[c, i]
        sums["kappa"] += field(SQUARED, c) * part * part

    def put(row, values):
        rows_ref[pl.ds(row, 16, stride=ROWS), :] = jnp.concatenate(values, axis=0)

    def compare(c, total):
        part = total - ratio * field(Z0, c)
        sums["energy"] += part * part
        sums["cross"] += part * field(Z0, c)
        put(c, [field(Z0, c), total])

    put(COLS, right0)
    put(COLS + 1, apply(Z0, Z1, orthogonal, compare))
    scalars = (alpha, beta, whole(sums["kappa"]), 0.125 * whole(sums["energy"]), 0.125 * whole(sums["cross"]))
    row = lax.broadcasted_iota(jnp.int32, (1, LANES), 1)
    last = jnp.zeros((1, LANES), jnp.float32)
    for place, value in zip(SCALARS, scalars):
        last = jnp.where(row == place, value, last)
    last = jnp.broadcast_to(last, (LANES, LANES))
    ours = lax.broadcasted_iota(jnp.int32, (LANES, LANES), 1) % ROWS >= COLS + 2
    for block in range(BLOCKS):
        piece = rows_ref[block * LANES : (block + 1) * LANES, :].T
        here = slice(block * LANES, (block + 1) * LANES)
        rows_ref[here, :] = jnp.where(ours, last, piece)
        for x in range(XS):
            from_x = rows_ref[pl.ds(block * LANES + x, LANES // XS, stride=XS), :]
            to = pl.ds(2 * (x * CHIPS // XS + (block % 2) * LANES // XS) + block // 2, LANES // XS, stride=2)
            out_ref[to, :] = from_x


def factors_of(at, ensemble_ref, decay_ref, innovation_ref, weight_ref, refs):
    inverse_ref, vector_ref, factor_ref, rate_ref, amplitude_ref, after_ref = refs
    for g in range(8):
        here = pl.ds(pl.multiple_of(at + g * LANES, LANES), LANES)
        group = pl.ds(g, COLS, stride=8)
        root = jnp.sqrt(weight_ref[:, here])
        inverse_ref[:COLS, g * LANES : (g + 1) * LANES] = 1.0 / root
        factor = ensemble_ref[0, :, here].astype(jnp.float32) * root
        vector_ref[group, :] = factor * (root * innovation_ref[:, here])
        factor_ref[group, :] = factor
        rate = decay_ref[:, here]
        rate_ref[group, :] = rate
        amplitude_ref[group, :] = jnp.sqrt((1.0 - rate) * (1.0 + rate))
    for columns in SEGMENTS:
        after = jnp.ones((8, LANES), jnp.float32)
        for c in reversed(columns):
            part = slice(8 * c, 8 * c + 8)
            after_ref[part, :] = after
            after = after * rate_ref[part, :]


def one_half(core, in_ref, field0_ref, field1_ref, vector0_ref, vector1_ref, scalars_ref,
             inverse_ref, vector_ref, factor_ref, rate_ref, amplitude_ref, after_ref):
    rows = [None] * 8
    for j in range(2):
        pieces = [in_ref[pl.ds(2 * j * LANES + h, LANES, stride=2), :].T for h in range(2)]
        for line in range(LINES):
            g = 2 * line + j
            part = slice(g * LANES, (g + 1) * LANES)
            z0, z1 = (piece[line * ROWS : line * ROWS + COLS] for piece in pieces)
            inverse = inverse_ref[:COLS, part]
            field0_ref[:COLS, part] = inverse * z0
            field1_ref[:COLS, part] = inverse * z1
            vector1_ref[pl.ds(g, COLS, stride=8), :] = z0
            states = [piece[line * ROWS + COLS : line * ROWS + COLS + 2] for piece in pieces]
            rows[g] = jnp.where(core == 0, *states)
        for i, place in enumerate(SCALARS):
            scalars_ref[i : i + 1, j * LANES : (j + 1) * LANES] = pieces[0][place : place + 1]
    entering = [jnp.concatenate([row[i : i + 1] for row in rows], axis=0) for i in range(2)]
    for columns in reversed(SEGMENTS):
        carry = [None, None]
        for c in reversed(columns):
            part = slice(8 * c, 8 * c + 8)
            for i, value in enumerate((vector_ref[part, :], factor_ref[part, :] * vector1_ref[part, :])):
                summed = value if carry[i] is None else value + carry[i]
                carry[i] = rate_ref[part, :] * summed
                (vector0_ref, vector1_ref)[i][part, :] = summed
        for c in columns:
            part = slice(8 * c, 8 * c + 8)
            for ref, state in zip((vector0_ref, vector1_ref), entering):
                ref[part, :] = amplitude_ref[part, :] * (ref[part, :] + after_ref[part, :] * state)
        first = slice(8 * columns[0], 8 * columns[0] + 8)
        product = rate_ref[first, :] * after_ref[first, :]
        entering = [end + product * state for end, state in zip(carry, entering)]


def prepare(core, in_ref, *refs):
    args, half, other, own = refs[:4], refs[4:9], refs[9:15], refs[15:]
    factors_of(core * HALF, *args, own)
    one_half(core, in_ref, *half, *own)
    factors_of((1 - core) * HALF, *args, other)


def finish(core, in_ref, *refs):
    own, factors = refs[:5], refs[5:11]
    control_hbm, increment_hbm = refs[11:13]
    other = refs[13:18]
    control_ref, increment_ref, sems = refs[18:]
    one_half(core, in_ref, *other, *factors)

    def whole(value):
        return jnp.sum(value, axis=1, keepdims=True)

    def both(i):
        return jnp.concatenate([ref[i : i + 1, :] for ref in (own[4], other[4])], axis=1)

    alphas, betas, kappas, energies, crosses = (both(i) for i in range(5))
    alpha, beta = whole(alphas), whole(betas)
    ratio = beta / alpha
    shift = jnp.where(alphas > 0.0, betas / jnp.where(alphas > 0.0, alphas, 1.0), 0.0) - ratio
    kappa = whole(kappas + alphas * shift * shift)
    energy = whole(energies + shift * (2.0 * crosses + shift * betas))
    step = alpha / (alpha + beta)
    curvature = kappa + energy - step * kappa * (kappa / alpha)
    back = jnp.where(curvature > 0.0, step * kappa / jnp.where(curvature > 0.0, curvature, 1.0), 0.0)
    ahead = step + back * (ratio + step * (kappa / alpha))

    copies = []

    def send(source, target):
        copies.append(pltpu.make_async_copy(source, target, sems.at[len(copies)]))
        copies[-1].start()

    for at, (field0_ref, field1_ref, *_) in ((core, own), (1 - core, other)):
        here = pl.ds(pl.multiple_of(at * HALF, HALF), HALF)
        increment_ref[:, here] = ahead * field0_ref[:COLS, :] - back * field1_ref[:COLS, :]
    send(increment_ref, increment_hbm)
    for quarter in range(4):
        for c in range(7 * quarter, 7 * quarter + 7):
            for at, (_, _, vector0_ref, vector1_ref, _) in ((core, own), (1 - core, other)):
                part = slice(8 * c, 8 * c + 8)
                here = pl.ds(pl.multiple_of(c * GROUPS + 8 * at, 8), 8)
                control_ref[here, :] = ahead * vector0_ref[part, :] - back * vector1_ref[part, :]
        part = slice(7 * quarter * GROUPS, (7 * quarter + 7) * GROUPS)
        send(control_ref.at[part, :], control_hbm.at[part, :])
    for copy in copies:
        copy.wait()


def shape(*dims):
    return jax.ShapeDtypeStruct(dims, jnp.float32)


def scratch(*dims):
    return pltpu.VMEM(dims, jnp.float32)


def call(kernel, out_shape, scratch_shapes, in_specs, out_specs):
    return pl.pallas_call(
        kernel,
        out_shape=out_shape,
        in_specs=in_specs,
        out_specs=out_specs,
        scratch_shapes=scratch_shapes,
        compiler_params=pltpu.CompilerParams(vmem_limit_bytes=32 * 1024 * 1024),
    )


def pack_call(place, *args):
    return call(
        lambda *refs: pack(place(), *refs),
        shape(DEVICES, LANES),
        [pltpu.VMEM((1, COLS, WIDTH), jnp.bfloat16)]
        + [scratch(COLS, WIDTH), scratch(2, 8, WIDTH), scratch(2, 4, WIDTH)]
        + [scratch(ROWS, WIDTH), pltpu.SemaphoreType.DMA((6,))],
        [HBM] * 4,
        VMEM,
    )(*(pltpu.with_memory_space_constraint(value, pltpu.HBM) for value in args))


def own_call(received):
    return call(
        own_lines,
        shape(DEVICES, LANES),
        [
            scratch(DEVICES, LANES),
            scratch(COLS, 2, 8, LANES),
            scratch(7, COLS, 8, LANES),
            scratch(COLS, 2, 8, LANES),
            scratch(COLS, 2, 8, LANES),
        ],
        [VMEM],
        VMEM,
    )(received)


BY_COLUMN = (ROWS * 8, LANES)
RESULTS = ((ROWS, HALF), (ROWS, HALF), BY_COLUMN, BY_COLUMN, (8, CHIPS))
FACTORS = ((ROWS, HALF), BY_COLUMN, BY_COLUMN, BY_COLUMN, BY_COLUMN, BY_COLUMN)


def prepare_call(core, returned, *args):
    return call(
        lambda *refs: prepare(core(), *refs),
        tuple(shape(*dims) for dims in RESULTS + FACTORS),
        [scratch(*dims) for dims in FACTORS],
        [VMEM] * 5,
        (VMEM,) * 11,
    )(returned, *args)


def finish_call(core, other, prepared):
    return call(
        lambda *refs: finish(core(), *refs),
        (shape(COLS * GROUPS, LANES), shape(COLS, WIDTH)),
        [scratch(*dims) for dims in RESULTS]
        + [scratch(COLS * GROUPS, LANES), scratch(COLS, WIDTH), pltpu.SemaphoreType.DMA((5,))],
        [VMEM] * 12,
        (HBM, HBM),
    )(other, *prepared)


def on_device(ensemble, decay_rate, innovation, obs_weight):
    args = (ensemble, decay_rate, innovation, obs_weight)
    core = lambda: lax.axis_index("core")
    sent = pack_call(lambda: 8 * lax.axis_index("core") + lax.axis_index("y"), *args)
    received = lax.all_to_all(sent, ("core", "y", "z", "x"), 0, 0, tiled=True)
    results = own_call(received).reshape(CHIPS, 2 * LANES)
    returned = lax.all_to_all(results, ("x", "y", "z"), 0, 0, tiled=True).reshape(DEVICES, LANES)
    other = lax.ppermute(returned, "core", [(0, 1), (1, 0)])
    control, increment = finish_call(core, other, prepare_call(core, returned, *args))
    return control.reshape(1, COLS, WIDTH), increment


def solution(mesh):
    chips = jax.sharding.Mesh(mesh.devices.reshape(MEMBERS // 2, 2, ZS, XS), ("y", "core", "z", "x"))
    whole, field = P(("y", "core"), ("z", "x"), None), P(("z", "x"), None)
    return jax.shard_map(
        on_device, mesh=chips, in_specs=(whole, field, field, field), out_specs=(whole, field), check_vma=False
    )
```

```python
import jax
import jax.numpy as jnp
from jax import lax
from jax.experimental import pallas as pl
from jax.experimental.pallas import tpu as pltpu
from jax.sharding import PartitionSpec as P

MEMBERS, TILES, COLS, LINES = 16, 32, 28, 4
XS, YS, ZS = 4, 8, 8
DEVICES = MEMBERS * TILES
ROWS = 32
LANES = 128
BLOCKS = DEVICES // LANES
GROUPS = LINES * BLOCKS
WIDTH = LINES * DEVICES
CHIPS, HALF = DEVICES // 2, WIDTH // 2
SEGMENT = 7
SEGMENTS = [range(start, start + SEGMENT) for start in range(0, COLS, SEGMENT)]
SCALARS = tuple(line * ROWS + COLS + 2 for line in range(LINES)) + (COLS + 3,)
VMEM = pl.BlockSpec(memory_space=pltpu.VMEM)
HBM = pl.BlockSpec(memory_space=pltpu.HBM)


def lane_block(line, block):
    start = (block // 2) * HALF + line * CHIPS + (block % 2) * LANES
    return slice(start, start + LANES)


def pack(place, ensemble_hbm, decay_hbm, innovation_hbm, weight_hbm, out_ref,
         ensemble_ref, weight_ref, eight_ref, last_ref, rows_ref, sems):
    quarter = lax.rem(place, 8)
    start = pl.multiple_of(8 * jnp.minimum(lax.div(quarter, 2), 2), 8)
    pairs = [(ensemble_hbm, ensemble_ref), (weight_hbm, weight_ref)]
    for i, hbm in enumerate((decay_hbm, innovation_hbm)):
        pairs.append((hbm.at[pl.ds(start, 8), :], eight_ref.at[i]))
        pairs.append((hbm.at[COLS - 4 : COLS, :], last_ref.at[i]))
    copies = [pltpu.make_async_copy(*pair, sems.at[i]) for i, pair in enumerate(pairs)]
    for copy in copies:
        copy.start()
    for copy in copies:
        copy.wait()
    rows_ref[:COLS, :] = ensemble_ref[0].astype(jnp.float32) * jnp.sqrt(weight_ref[...])

    def four(eight, last):
        inner = jnp.where(lax.rem(quarter, 2) == 0, eight[:4], eight[4:])
        return jnp.where(quarter >= 6, last, inner)

    scaled = jnp.sqrt(four(weight_ref[pl.ds(start, 8), :], weight_ref[COLS - 4 :, :])) * four(eight_ref[1], last_ref[1])
    rows_ref[COLS:, :] = jnp.where(place < 8, four(eight_ref[0], last_ref[0]), scaled)
    for block in range(BLOCKS):
        piece = jnp.concatenate([rows_ref[:, lane_block(line, block)] for line in range(LINES)], axis=0).T
        for half in range(2):
            x = 2 * (block % 2) + half
            for y in range(YS):
                to = pl.ds(x * LANES + 2 * y + block // 2, ZS, stride=2 * YS)
                start = half * YS * ZS + y * ZS
                out_ref[to, :] = piece[start : start + ZS]


def balanced(join, terms):
    while len(terms) > 1:
        terms = [join(*terms[i : i + 2]) if i + 1 < len(terms) else terms[i] for i in range(0, len(terms), 2)]
    return terms[0]


def add(x, y):
    return x + y


def spread(piece, lane_group):
    turned = [piece] + [pltpu.roll(piece, 32 * k, 1) for k in (1, 2, 3)]
    out = []
    for source in range(4):
        value = turned[(3 - source) % 4]
        for group in (2, 1, 0):
            value = jnp.where(lane_group == group, turned[(group - source) % 4], value)
        out.append(value)
    return out


def own_lines(in_ref, out_ref, rows_ref, members_ref, fields_ref, state_ref, first_ref):
    for block in range(BLOCKS):
        for i in range(YS // 2):
            for x in range(XS):
                given = in_ref[pl.ds(x * LANES + (block % 2) * YS + 2 * i + block // 2, ZS, stride=2 * YS), :]
                rows_ref[pl.ds(block * LANES + i * TILES + x, ZS, stride=XS), :] = given
        piece = slice(block * LANES, (block + 1) * LANES)
        rows_ref[piece, :] = rows_ref[piece, :].T

    lane = lax.broadcasted_iota(jnp.int32, (8, LANES), 1)
    sub = lax.broadcasted_iota(jnp.int32, (8, LANES), 0)
    tile, lane_group = lane % TILES, lane // TILES
    low = sub < 4
    zero = jnp.zeros((8, LANES), jnp.float32)

    for c in range(COLS):
        value = rows_ref[pl.ds(c, 16, stride=ROWS), :]
        members_ref[c, 0], members_ref[c, 1] = value[:8], value[8:]

    RATE, SQUARED, AFTER, UPTO, INNOV, Z0, Z1 = range(7)

    def field(kind, c):
        return fields_ref[kind, c]

    for j in range(4):
        given = rows_ref[pl.ds(COLS + j, 16, stride=ROWS), :]
        for kind, value in ((RATE, given[:8]), (INNOV, given[8:])):
            other = pltpu.roll(value, 4, 0)
            for half, both in enumerate((jnp.where(low, value, other), jnp.where(low, other, value))):
                for source, copied in enumerate(spread(both, lane_group)):
                    c = 16 * half + 4 * source + j
                    if c < COLS:
                        fields_ref[kind, c] = copied

    one = zero + 1.0
    parts = []
    for columns in SEGMENTS:
        upto, after = one, one
        for c in columns:
            rate = field(RATE, c)
            fields_ref[SQUARED, c] = (1.0 - rate) * (1.0 + rate)
            upto = upto * rate
            fields_ref[UPTO, c] = upto
        for c in reversed(columns):
            fields_ref[AFTER, c] = after
            after = after * field(RATE, c)
        parts.append(upto)
    upto = balanced(lambda x, y: x * y, parts)

    def turn(value, k, backward):
        return pltpu.roll(value, LANES - k if backward else k, 1)

    def inside(k, backward):
        return tile < TILES - k if backward else tile >= k

    def factors(backward):
        out, product = [], one
        for k in range(1, TILES):
            out.append((k, jnp.where(inside(k, backward), product, 0.0)))
            product = product * turn(upto, k, backward)
        return out

    chains = {backward: factors(backward) for backward in (True, False)}

    def entering(values, backward):
        return [
            balanced(add, [factor * turn(value, k, backward) for k, factor in chains[backward]]) for value in values
        ]

    def through(ends, products, start):
        states = [start]
        for end, product in zip(ends, products):
            states.append(end if states[-1] is None else end + product * states[-1])
        return states

    def apply(source, target, on_state, on_field):
        ends = [[], []]
        for columns in reversed(SEGMENTS):
            carry = [None, None]
            for c in reversed(columns):
                rate, weight = field(RATE, c), field(source, c)
                for i in range(2):
                    summed = members_ref[c, i] * weight
                    summed = summed if carry[i] is None else summed + carry[i]
                    state_ref[c, i] = summed
                    carry[i] = rate * summed
            for i in range(2):
                ends[i].append(carry[i])
        from_right = entering([through(ends[i], parts[::-1], None)[-1] for i in range(2)], True)
        starts = [through(ends[i], parts[::-1], from_right[i])[:-1][::-1] for i in range(2)]
        ends = [[], []]
        for s, columns in enumerate(SEGMENTS):
            state = [None, None]
            for c in columns:
                rate, squared, after = field(RATE, c), field(SQUARED, c), field(AFTER, c)
                for i in range(2):
                    summed = state_ref[c, i] + after * starts[i][s]
                    driven = squared * summed
                    on_state(c, i, summed, driven)
                    state[i] = driven if state[i] is None else rate * state[i] + driven
                    state_ref[c, i] = state[i]
            for i in range(2):
                ends[i].append(state[i])
        from_left = entering([through(ends[i], parts, None)[-1] for i in range(2)], False)
        starts = [through(ends[i], parts, from_left[i])[:-1] for i in range(2)]
        for s, columns in reversed(list(enumerate(SEGMENTS))):
            for c in reversed(columns):
                upto = field(UPTO, c)
                total = add(*(members_ref[c, i] * (state_ref[c, i] + upto * starts[i][s]) for i in range(2)))
                total = total + pltpu.roll(total, 4, 0)
                total = total + pltpu.roll(total, 64, 1)
                total = total + pltpu.roll(total, 32, 1)
                fields_ref[target, c] = total
                on_field(c, total)
        return from_right

    def whole(value):
        return jnp.sum(jnp.sum(value, axis=0, keepdims=True), axis=1, keepdims=True)

    sums = {name: zero for name in ("alpha", "beta", "kappa", "energy", "cross")}

    def keep(c, i, summed, driven):
        first_ref[c, i] = summed
        sums["alpha"] += summed * driven

    def square(c, total):
        sums["beta"] += total * total

    right0 = apply(INNOV, Z0, keep, square)
    alpha = whole(sums["alpha"])
    beta = 0.125 * whole(sums["beta"])
    ratio = jnp.where(alpha > 0.0, beta / jnp.where(alpha > 0.0, alpha, 1.0), 0.0)
    ratio = jnp.broadcast_to(ratio, (8, LANES))

    def orthogonal(c, i, summed, driven):
        part = summed - ratio * first_ref[c, i]
        sums["kappa"] += field(SQUARED, c) * part * part

    def put(row, values):
        rows_ref[pl.ds(row, 16, stride=ROWS), :] = jnp.concatenate(values, axis=0)

    def compare(c, total):
        part = total - ratio * field(Z0, c)
        sums["energy"] += part * part
        sums["cross"] += part * field(Z0, c)
        put(c, [field(Z0, c), total])

    put(COLS, right0)
    put(COLS + 1, apply(Z0, Z1, orthogonal, compare))
    scalars = (alpha, beta, whole(sums["kappa"]), 0.125 * whole(sums["energy"]), 0.125 * whole(sums["cross"]))
    row = lax.broadcasted_iota(jnp.int32, (1, LANES), 1)
    last = jnp.zeros((1, LANES), jnp.float32)
    for place, value in zip(SCALARS, scalars):
        last = jnp.where(row == place, value, last)
    last = jnp.broadcast_to(last, (LANES, LANES))
    ours = lax.broadcasted_iota(jnp.int32, (LANES, LANES), 1) % ROWS >= COLS + 2
    for block in range(BLOCKS):
        piece = rows_ref[block * LANES : (block + 1) * LANES, :].T
        here = slice(block * LANES, (block + 1) * LANES)
        rows_ref[here, :] = jnp.where(ours, last, piece)
        for x in range(XS):
            from_x = rows_ref[pl.ds(block * LANES + x, LANES // XS, stride=XS), :]
            to = pl.ds(2 * (x * CHIPS // XS + (block % 2) * LANES // XS) + block // 2, LANES // XS, stride=2)
            out_ref[to, :] = from_x


def factors_of(at, ensemble_ref, decay_ref, innovation_ref, weight_ref, refs):
    inverse_ref, vector_ref, factor_ref, rate_ref, amplitude_ref, after_ref = refs
    for g in range(8):
        here = pl.ds(pl.multiple_of(at + g * LANES, LANES), LANES)
        group = pl.ds(g, COLS, stride=8)
        root = jnp.sqrt(weight_ref[:, here])
        inverse_ref[:COLS, g * LANES : (g + 1) * LANES] = 1.0 / root
        factor = ensemble_ref[0, :, here].astype(jnp.float32) * root
        vector_ref[group, :] = factor * (root * innovation_ref[:, here])
        factor_ref[group, :] = factor
        rate = decay_ref[:, here]
        rate_ref[group, :] = rate
        amplitude_ref[group, :] = jnp.sqrt((1.0 - rate) * (1.0 + rate))
    for columns in SEGMENTS:
        after = jnp.ones((8, LANES), jnp.float32)
        for c in reversed(columns):
            part = slice(8 * c, 8 * c + 8)
            after_ref[part, :] = after
            after = after * rate_ref[part, :]


def one_half(core, in_ref, field0_ref, field1_ref, vector0_ref, vector1_ref, scalars_ref,
             inverse_ref, vector_ref, factor_ref, rate_ref, amplitude_ref, after_ref):
    rows = [None] * 8
    for j in range(2):
        pieces = [in_ref[pl.ds(2 * j * LANES + h, LANES, stride=2), :].T for h in range(2)]
        for line in range(LINES):
            g = 2 * line + j
            part = slice(g * LANES, (g + 1) * LANES)
            z0, z1 = (piece[line * ROWS : line * ROWS + COLS] for piece in pieces)
            inverse = inverse_ref[:COLS, part]
            field0_ref[:COLS, part] = inverse * z0
            field1_ref[:COLS, part] = inverse * z1
            vector1_ref[pl.ds(g, COLS, stride=8), :] = z0
            states = [piece[line * ROWS + COLS : line * ROWS + COLS + 2] for piece in pieces]
            rows[g] = jnp.where(core == 0, *states)
        for i, place in enumerate(SCALARS):
            scalars_ref[i : i + 1, j * LANES : (j + 1) * LANES] = pieces[0][place : place + 1]
    entering = [jnp.concatenate([row[i : i + 1] for row in rows], axis=0) for i in range(2)]
    for columns in reversed(SEGMENTS):
        carry = [None, None]
        for c in reversed(columns):
            part = slice(8 * c, 8 * c + 8)
            for i, value in enumerate((vector_ref[part, :], factor_ref[part, :] * vector1_ref[part, :])):
                summed = value if carry[i] is None else value + carry[i]
                carry[i] = rate_ref[part, :] * summed
                (vector0_ref, vector1_ref)[i][part, :] = summed
        for c in columns:
            part = slice(8 * c, 8 * c + 8)
            for ref, state in zip((vector0_ref, vector1_ref), entering):
                ref[part, :] = amplitude_ref[part, :] * (ref[part, :] + after_ref[part, :] * state)
        first = slice(8 * columns[0], 8 * columns[0] + 8)
        product = rate_ref[first, :] * after_ref[first, :]
        entering = [end + product * state for end, state in zip(carry, entering)]


def prepare(core, in_ref, *refs):
    args, half, other, own = refs[:4], refs[4:9], refs[9:15], refs[15:]
    factors_of(core * HALF, *args, own)
    one_half(core, in_ref, *half, *own)
    factors_of((1 - core) * HALF, *args, other)


def finish(core, in_ref, *refs):
    own, factors = refs[:5], refs[5:11]
    control_hbm, increment_hbm = refs[11:13]
    other = refs[13:18]
    control_ref, increment_ref, sems = refs[18:]
    one_half(core, in_ref, *other, *factors)

    def whole(value):
        return jnp.sum(value, axis=1, keepdims=True)

    def both(i):
        return jnp.concatenate([ref[i : i + 1, :] for ref in (own[4], other[4])], axis=1)

    alphas, betas, kappas, energies, crosses = (both(i) for i in range(5))
    alpha, beta = whole(alphas), whole(betas)
    ratio = beta / alpha
    shift = jnp.where(alphas > 0.0, betas / jnp.where(alphas > 0.0, alphas, 1.0), 0.0) - ratio
    kappa = whole(kappas + alphas * shift * shift)
    energy = whole(energies + shift * (2.0 * crosses + shift * betas))
    step = alpha / (alpha + beta)
    curvature = kappa + energy - step * kappa * (kappa / alpha)
    back = jnp.where(curvature > 0.0, step * kappa / jnp.where(curvature > 0.0, curvature, 1.0), 0.0)
    ahead = step + back * (ratio + step * (kappa / alpha))

    copies = []

    def send(source, target):
        copies.append(pltpu.make_async_copy(source, target, sems.at[len(copies)]))
        copies[-1].start()

    for at, (field0_ref, field1_ref, *_) in ((core, own), (1 - core, other)):
        here = pl.ds(pl.multiple_of(at * HALF, HALF), HALF)
        increment_ref[:, here] = ahead * field0_ref[:COLS, :] - back * field1_ref[:COLS, :]
    send(increment_ref, increment_hbm)
    for quarter in range(4):
        for c in range(7 * quarter, 7 * quarter + 7):
            for at, (_, _, vector0_ref, vector1_ref, _) in ((core, own), (1 - core, other)):
                part = slice(8 * c, 8 * c + 8)
                here = pl.ds(pl.multiple_of(c * GROUPS + 8 * at, 8), 8)
                control_ref[here, :] = ahead * vector0_ref[part, :] - back * vector1_ref[part, :]
        part = slice(7 * quarter * GROUPS, (7 * quarter + 7) * GROUPS)
        send(control_ref.at[part, :], control_hbm.at[part, :])
    for copy in copies:
        copy.wait()


def shape(*dims):
    return jax.ShapeDtypeStruct(dims, jnp.float32)


def scratch(*dims):
    return pltpu.VMEM(dims, jnp.float32)


def call(kernel, out_shape, scratch_shapes, in_specs, out_specs):
    return pl.pallas_call(
        kernel,
        out_shape=out_shape,
        in_specs=in_specs,
        out_specs=out_specs,
        scratch_shapes=scratch_shapes,
        compiler_params=pltpu.CompilerParams(vmem_limit_bytes=32 * 1024 * 1024),
    )


def pack_call(place, *args):
    return call(
        lambda *refs: pack(place(), *refs),
        shape(DEVICES, LANES),
        [pltpu.VMEM((1, COLS, WIDTH), jnp.bfloat16)]
        + [scratch(COLS, WIDTH), scratch(2, 8, WIDTH), scratch(2, 4, WIDTH)]
        + [scratch(ROWS, WIDTH), pltpu.SemaphoreType.DMA((6,))],
        [HBM] * 4,
        VMEM,
    )(*(pltpu.with_memory_space_constraint(value, pltpu.HBM) for value in args))


def own_call(received):
    return call(
        own_lines,
        shape(DEVICES, LANES),
        [
            scratch(DEVICES, LANES),
            scratch(COLS, 2, 8, LANES),
            scratch(7, COLS, 8, LANES),
            scratch(COLS, 2, 8, LANES),
            scratch(COLS, 2, 8, LANES),
        ],
        [VMEM],
        VMEM,
    )(received)


BY_COLUMN = (ROWS * 8, LANES)
RESULTS = ((ROWS, HALF), (ROWS, HALF), BY_COLUMN, BY_COLUMN, (8, CHIPS))
FACTORS = ((ROWS, HALF), BY_COLUMN, BY_COLUMN, BY_COLUMN, BY_COLUMN, BY_COLUMN)


def prepare_call(core, returned, *args):
    return call(
        lambda *refs: prepare(core(), *refs),
        tuple(shape(*dims) for dims in RESULTS + FACTORS),
        [scratch(*dims) for dims in FACTORS],
        [VMEM] * 5,
        (VMEM,) * 11,
    )(returned, *args)


def finish_call(core, other, prepared):
    return call(
        lambda *refs: finish(core(), *refs),
        (shape(COLS * GROUPS, LANES), shape(COLS, WIDTH)),
        [scratch(*dims) for dims in RESULTS]
        + [scratch(COLS * GROUPS, LANES), scratch(COLS, WIDTH), pltpu.SemaphoreType.DMA((5,))],
        [VMEM] * 12,
        (HBM, HBM),
    )(other, *prepared)


def on_device(ensemble, decay_rate, innovation, obs_weight):
    args = (ensemble, decay_rate, innovation, obs_weight)
    core = lambda: lax.axis_index("core")
    sent = pack_call(lambda: 8 * lax.axis_index("core") + lax.axis_index("y"), *args)
    received = lax.all_to_all(sent, ("x", "z", "y", "core"), 0, 0, tiled=True)
    results = own_call(received).reshape(CHIPS, 2 * LANES)
    returned = lax.all_to_all(results, ("x", "y", "z"), 0, 0, tiled=True).reshape(DEVICES, LANES)
    other = lax.ppermute(returned, "core", [(0, 1), (1, 0)])
    control, increment = finish_call(core, other, prepare_call(core, returned, *args))
    return control.reshape(1, COLS, WIDTH), increment


def solution(mesh):
    chips = jax.sharding.Mesh(mesh.devices.reshape(MEMBERS // 2, 2, ZS, XS), ("y", "core", "z", "x"))
    whole, field = P(("y", "core"), ("z", "x"), None), P(("z", "x"), None)
    return jax.shard_map(
        on_device, mesh=chips, in_specs=(whole, field, field, field), out_specs=(whole, field), check_vma=False
    )
```

```python
import jax
import jax.numpy as jnp
from jax import lax
from jax.experimental import pallas as pl
from jax.experimental.pallas import tpu as pltpu
from jax.sharding import PartitionSpec as P

MEMBERS, TILES, COLS, LINES = 16, 32, 28, 4
XS, ZS = 4, 8
DEVICES = MEMBERS * TILES
ROWS = 32
LANES = 128
BLOCKS = DEVICES // LANES
GROUPS = LINES * BLOCKS
WIDTH = LINES * DEVICES
CHIPS, HALF = DEVICES // 2, WIDTH // 2
SEGMENT = 4
SEGMENTS = [range(start, start + SEGMENT) for start in range(0, COLS, SEGMENT)]
SCALARS = tuple(line * ROWS + COLS + 2 for line in range(LINES)) + (COLS + 3,)
VMEM = pl.BlockSpec(memory_space=pltpu.VMEM)
HBM = pl.BlockSpec(memory_space=pltpu.HBM)


def lane_block(line, block):
    start = (block // 2) * HALF + line * CHIPS + (block % 2) * LANES
    return slice(start, start + LANES)


def pack(place, ensemble_hbm, decay_hbm, innovation_hbm, weight_hbm, out_ref,
         ensemble_ref, weight_ref, eight_ref, last_ref, rows_ref, sems):
    quarter = lax.rem(place, 8)
    start = pl.multiple_of(8 * jnp.minimum(lax.div(quarter, 2), 2), 8)
    pairs = [(ensemble_hbm, ensemble_ref), (weight_hbm, weight_ref)]
    for i, hbm in enumerate((decay_hbm, innovation_hbm)):
        pairs.append((hbm.at[pl.ds(start, 8), :], eight_ref.at[i]))
        pairs.append((hbm.at[COLS - 4 : COLS, :], last_ref.at[i]))
    copies = [pltpu.make_async_copy(*pair, sems.at[i]) for i, pair in enumerate(pairs)]
    for copy in copies:
        copy.start()
    for copy in copies:
        copy.wait()
    rows_ref[:COLS, :] = ensemble_ref[0].astype(jnp.float32) * jnp.sqrt(weight_ref[...])

    def four(eight, last):
        inner = jnp.where(lax.rem(quarter, 2) == 0, eight[:4], eight[4:])
        return jnp.where(quarter >= 6, last, inner)

    scaled = jnp.sqrt(four(weight_ref[pl.ds(start, 8), :], weight_ref[COLS - 4 :, :])) * four(eight_ref[1], last_ref[1])
    rows_ref[COLS:, :] = jnp.where(place < 8, four(eight_ref[0], last_ref[0]), scaled)
    for block in range(BLOCKS):
        piece = jnp.concatenate([rows_ref[:, lane_block(line, block)] for line in range(LINES)], axis=0).T
        for half in range(2):
            x = 2 * (block % 2) + half
            to = pl.ds((block // 2) * CHIPS + x, CHIPS // XS, stride=XS)
            out_ref[to, :] = piece[half * CHIPS // XS : (half + 1) * CHIPS // XS]


def balanced(join, terms):
    while len(terms) > 1:
        terms = [join(*terms[i : i + 2]) if i + 1 < len(terms) else terms[i] for i in range(0, len(terms), 2)]
    return terms[0]


def add(x, y):
    return x + y


def spread(piece, lane_group):
    turned = [piece] + [pltpu.roll(piece, 32 * k, 1) for k in (1, 2, 3)]
    out = []
    for source in range(4):
        value = turned[(3 - source) % 4]
        for group in (2, 1, 0):
            value = jnp.where(lane_group == group, turned[(group - source) % 4], value)
        out.append(value)
    return out


def own_lines(in_ref, out_ref, rows_ref, members_ref, fields_ref, state_ref, first_ref):
    for block in range(BLOCKS):
        piece = slice(block * LANES, (block + 1) * LANES)
        rows_ref[piece, :] = in_ref[piece, :].T

    lane = lax.broadcasted_iota(jnp.int32, (8, LANES), 1)
    sub = lax.broadcasted_iota(jnp.int32, (8, LANES), 0)
    tile, lane_group = lane % TILES, lane // TILES
    low = sub < 4
    zero = jnp.zeros((8, LANES), jnp.float32)

    for c in range(COLS):
        value = rows_ref[pl.ds(c, 16, stride=ROWS), :]
        members_ref[c, 0], members_ref[c, 1] = value[:8], value[8:]

    RATE, SQUARED, AFTER, UPTO, INNOV, Z0, Z1 = range(7)

    def field(kind, c):
        return fields_ref[kind, c]

    for j in range(4):
        given = rows_ref[pl.ds(COLS + j, 16, stride=ROWS), :]
        for kind, value in ((RATE, given[:8]), (INNOV, given[8:])):
            other = pltpu.roll(value, 4, 0)
            for half, both in enumerate((jnp.where(low, value, other), jnp.where(low, other, value))):
                for source, copied in enumerate(spread(both, lane_group)):
                    c = 16 * half + 4 * source + j
                    if c < COLS:
                        fields_ref[kind, c] = copied

    one = zero + 1.0
    parts = []
    for columns in SEGMENTS:
        upto, after = one, one
        for c in columns:
            rate = field(RATE, c)
            fields_ref[SQUARED, c] = (1.0 - rate) * (1.0 + rate)
            upto = upto * rate
            fields_ref[UPTO, c] = upto
        for c in reversed(columns):
            fields_ref[AFTER, c] = after
            after = after * field(RATE, c)
        parts.append(upto)
    upto = balanced(lambda x, y: x * y, parts)

    def turn(value, k, backward):
        return pltpu.roll(value, LANES - k if backward else k, 1)

    def inside(k, backward):
        return tile < TILES - k if backward else tile >= k

    def factors(backward):
        out, product = [], one
        for k in range(1, TILES):
            out.append((k, jnp.where(inside(k, backward), product, 0.0)))
            product = product * turn(upto, k, backward)
        return out

    chains = {backward: factors(backward) for backward in (True, False)}

    def entering(values, backward):
        return [
            balanced(add, [factor * turn(value, k, backward) for k, factor in chains[backward]]) for value in values
        ]

    def through(ends, products, start):
        states = [start]
        for end, product in zip(ends, products):
            states.append(end if states[-1] is None else end + product * states[-1])
        return states

    def apply(source, target, on_state, on_field):
        ends = [[], []]
        for columns in reversed(SEGMENTS):
            carry = [None, None]
            for c in reversed(columns):
                rate, weight = field(RATE, c), field(source, c)
                for i in range(2):
                    summed = members_ref[c, i] * weight
                    summed = summed if carry[i] is None else summed + carry[i]
                    state_ref[c, i] = summed
                    carry[i] = rate * summed
            for i in range(2):
                ends[i].append(carry[i])
        from_right = entering([through(ends[i], parts[::-1], None)[-1] for i in range(2)], True)
        starts = [through(ends[i], parts[::-1], from_right[i])[:-1][::-1] for i in range(2)]
        ends = [[], []]
        for s, columns in enumerate(SEGMENTS):
            state = [None, None]
            for c in columns:
                rate, squared, after = field(RATE, c), field(SQUARED, c), field(AFTER, c)
                for i in range(2):
                    summed = state_ref[c, i] + after * starts[i][s]
                    driven = squared * summed
                    on_state(c, i, summed, driven)
                    state[i] = driven if state[i] is None else rate * state[i] + driven
                    state_ref[c, i] = state[i]
            for i in range(2):
                ends[i].append(state[i])
        from_left = entering([through(ends[i], parts, None)[-1] for i in range(2)], False)
        starts = [through(ends[i], parts, from_left[i])[:-1] for i in range(2)]
        for s, columns in reversed(list(enumerate(SEGMENTS))):
            for c in reversed(columns):
                upto = field(UPTO, c)
                total = add(*(members_ref[c, i] * (state_ref[c, i] + upto * starts[i][s]) for i in range(2)))
                total = total + pltpu.roll(total, 4, 0)
                total = total + pltpu.roll(total, 64, 1)
                total = total + pltpu.roll(total, 32, 1)
                fields_ref[target, c] = total
                on_field(c, total)
        return from_right

    def whole(value):
        return jnp.sum(jnp.sum(value, axis=0, keepdims=True), axis=1, keepdims=True)

    sums = {name: zero for name in ("alpha", "beta", "kappa", "energy", "cross")}

    def keep(c, i, summed, driven):
        first_ref[c, i] = summed
        sums["alpha"] += summed * driven

    def square(c, total):
        sums["beta"] += total * total

    right0 = apply(INNOV, Z0, keep, square)
    alpha = whole(sums["alpha"])
    beta = 0.125 * whole(sums["beta"])
    ratio = jnp.where(alpha > 0.0, beta / jnp.where(alpha > 0.0, alpha, 1.0), 0.0)
    ratio = jnp.broadcast_to(ratio, (8, LANES))

    def orthogonal(c, i, summed, driven):
        part = summed - ratio * first_ref[c, i]
        sums["kappa"] += field(SQUARED, c) * part * part

    def put(row, values):
        rows_ref[pl.ds(row, 16, stride=ROWS), :] = jnp.concatenate(values, axis=0)

    def compare(c, total):
        part = total - ratio * field(Z0, c)
        sums["energy"] += part * part
        sums["cross"] += part * field(Z0, c)
        put(c, [field(Z0, c), total])

    put(COLS, right0)
    put(COLS + 1, apply(Z0, Z1, orthogonal, compare))
    scalars = (alpha, ratio[:1, :1], whole(sums["kappa"]), 0.125 * whole(sums["energy"]), 0.125 * whole(sums["cross"]))
    row = lax.broadcasted_iota(jnp.int32, (1, LANES), 1)
    last = jnp.zeros((1, LANES), jnp.float32)
    for place, value in zip(SCALARS, scalars):
        last = jnp.where(row == place, value, last)
    last = jnp.broadcast_to(last, (LANES, LANES))
    ours = lax.broadcasted_iota(jnp.int32, (LANES, LANES), 1) % ROWS >= COLS + 2
    for block in range(BLOCKS):
        piece = rows_ref[block * LANES : (block + 1) * LANES, :].T
        here = slice(block * LANES, (block + 1) * LANES)
        rows_ref[here, :] = jnp.where(ours, last, piece)
        for x in range(XS):
            from_x = rows_ref[pl.ds(block * LANES + x, LANES // XS, stride=XS), :]
            to = pl.ds(2 * (x * CHIPS // XS + (block % 2) * LANES // XS) + block // 2, LANES // XS, stride=2)
            out_ref[to, :] = from_x


def factors_of(at, ensemble_ref, decay_ref, innovation_ref, weight_ref, refs):
    inverse_ref, vector_ref, factor_ref, rate_ref, amplitude_ref, after_ref = refs
    for g in range(8):
        here = pl.ds(pl.multiple_of(at + g * LANES, LANES), LANES)
        group = pl.ds(g, COLS, stride=8)
        root = jnp.sqrt(weight_ref[:, here])
        inverse_ref[:COLS, g * LANES : (g + 1) * LANES] = 1.0 / root
        factor = ensemble_ref[0, :, here].astype(jnp.float32) * root
        vector_ref[group, :] = factor * (root * innovation_ref[:, here])
        factor_ref[group, :] = factor
        rate = decay_ref[:, here]
        rate_ref[group, :] = rate
        amplitude_ref[group, :] = jnp.sqrt((1.0 - rate) * (1.0 + rate))
    for columns in SEGMENTS:
        after = jnp.ones((8, LANES), jnp.float32)
        for c in reversed(columns):
            part = slice(8 * c, 8 * c + 8)
            after_ref[part, :] = after
            after = after * rate_ref[part, :]


def one_half(core, in_ref, field0_ref, field1_ref, vector0_ref, vector1_ref, scalars_ref,
             inverse_ref, vector_ref, factor_ref, rate_ref, amplitude_ref, after_ref):
    rows = [None] * 8
    for j in range(2):
        pieces = [in_ref[pl.ds(2 * j * LANES + h, LANES, stride=2), :].T for h in range(2)]
        for line in range(LINES):
            g = 2 * line + j
            part = slice(g * LANES, (g + 1) * LANES)
            z0, z1 = (piece[line * ROWS : line * ROWS + COLS] for piece in pieces)
            inverse = inverse_ref[:COLS, part]
            field0_ref[:COLS, part] = inverse * z0
            field1_ref[:COLS, part] = inverse * z1
            vector1_ref[pl.ds(g, COLS, stride=8), :] = z0
            states = [piece[line * ROWS + COLS : line * ROWS + COLS + 2] for piece in pieces]
            rows[g] = jnp.where(core == 0, *states)
        for i, place in enumerate(SCALARS):
            scalars_ref[i : i + 1, j * LANES : (j + 1) * LANES] = pieces[0][place : place + 1]
    entering = [jnp.concatenate([row[i : i + 1] for row in rows], axis=0) for i in range(2)]
    for columns in reversed(SEGMENTS):
        carry = [None, None]
        for c in reversed(columns):
            part = slice(8 * c, 8 * c + 8)
            for i, value in enumerate((vector_ref[part, :], factor_ref[part, :] * vector1_ref[part, :])):
                summed = value if carry[i] is None else value + carry[i]
                carry[i] = rate_ref[part, :] * summed
                (vector0_ref, vector1_ref)[i][part, :] = summed
        for c in columns:
            part = slice(8 * c, 8 * c + 8)
            for ref, state in zip((vector0_ref, vector1_ref), entering):
                ref[part, :] = amplitude_ref[part, :] * (ref[part, :] + after_ref[part, :] * state)
        first = slice(8 * columns[0], 8 * columns[0] + 8)
        product = rate_ref[first, :] * after_ref[first, :]
        entering = [end + product * state for end, state in zip(carry, entering)]


def prepare(core, in_ref, *refs):
    args, half, other, own = refs[:4], refs[4:9], refs[9:15], refs[15:]
    factors_of(core * HALF, *args, own)
    one_half(core, in_ref, *half, *own)
    factors_of((1 - core) * HALF, *args, other)


def finish(core, in_ref, *refs):
    own, factors = refs[:5], refs[5:11]
    control_hbm, increment_hbm = refs[11:13]
    other = refs[13:18]
    control_ref, increment_ref, sems = refs[18:]
    one_half(core, in_ref, *other, *factors)

    def whole(value):
        return jnp.sum(value, axis=1, keepdims=True)

    def both(i):
        return jnp.concatenate([ref[i : i + 1, :] for ref in (own[4], other[4])], axis=1)

    alphas, ratios, kappas, energies, crosses = (both(i) for i in range(5))
    betas = alphas * ratios
    alpha, beta = whole(alphas), whole(betas)
    ratio = beta / alpha
    shift = ratios - ratio
    kappa = whole(kappas + alphas * shift * shift)
    energy = whole(energies + shift * (2.0 * crosses + shift * betas))
    step = alpha / (alpha + beta)
    turned = step * (kappa / alpha)
    curvature = kappa + energy - turned * kappa
    back = jnp.where(curvature > 0.0, step * kappa / jnp.where(curvature > 0.0, curvature, 1.0), 0.0)
    ahead = step + back * (ratio + turned)

    copies = []

    def send(source, target):
        copies.append(pltpu.make_async_copy(source, target, sems.at[len(copies)]))
        copies[-1].start()

    for at, (field0_ref, field1_ref, *_) in ((core, own), (1 - core, other)):
        here = pl.ds(pl.multiple_of(at * HALF, HALF), HALF)
        increment_ref[:, here] = ahead * field0_ref[:COLS, :] - back * field1_ref[:COLS, :]
    send(increment_ref, increment_hbm)
    for quarter in range(4):
        for c in range(7 * quarter, 7 * quarter + 7):
            for at, (_, _, vector0_ref, vector1_ref, _) in ((core, own), (1 - core, other)):
                part = slice(8 * c, 8 * c + 8)
                here = pl.ds(pl.multiple_of(c * GROUPS + 8 * at, 8), 8)
                control_ref[here, :] = ahead * vector0_ref[part, :] - back * vector1_ref[part, :]
        part = slice(7 * quarter * GROUPS, (7 * quarter + 7) * GROUPS)
        send(control_ref.at[part, :], control_hbm.at[part, :])
    for copy in copies:
        copy.wait()


def shape(*dims):
    return jax.ShapeDtypeStruct(dims, jnp.float32)


def scratch(*dims):
    return pltpu.VMEM(dims, jnp.float32)


def call(kernel, out_shape, scratch_shapes, in_specs, out_specs):
    return pl.pallas_call(
        kernel,
        out_shape=out_shape,
        in_specs=in_specs,
        out_specs=out_specs,
        scratch_shapes=scratch_shapes,
        compiler_params=pltpu.CompilerParams(vmem_limit_bytes=32 * 1024 * 1024),
    )


def pack_call(place, *args):
    return call(
        lambda *refs: pack(place(), *refs),
        shape(DEVICES, LANES),
        [pltpu.VMEM((1, COLS, WIDTH), jnp.bfloat16)]
        + [scratch(COLS, WIDTH), scratch(2, 8, WIDTH), scratch(2, 4, WIDTH)]
        + [scratch(ROWS, WIDTH), pltpu.SemaphoreType.DMA((6,))],
        [HBM] * 4,
        VMEM,
    )(*(pltpu.with_memory_space_constraint(value, pltpu.HBM) for value in args))


def own_call(received):
    return call(
        own_lines,
        shape(DEVICES, LANES),
        [
            scratch(DEVICES, LANES),
            scratch(COLS, 2, 8, LANES),
            scratch(7, COLS, 8, LANES),
            scratch(COLS, 2, 8, LANES),
            scratch(COLS, 2, 8, LANES),
        ],
        [VMEM],
        VMEM,
    )(received)


BY_COLUMN = (ROWS * 8, LANES)
RESULTS = ((ROWS, HALF), (ROWS, HALF), BY_COLUMN, BY_COLUMN, (8, CHIPS))
FACTORS = ((ROWS, HALF), BY_COLUMN, BY_COLUMN, BY_COLUMN, BY_COLUMN, BY_COLUMN)


def prepare_call(core, returned, *args):
    return call(
        lambda *refs: prepare(core(), *refs),
        tuple(shape(*dims) for dims in RESULTS + FACTORS),
        [scratch(*dims) for dims in FACTORS],
        [VMEM] * 5,
        (VMEM,) * 11,
    )(returned, *args)


def finish_call(core, other, prepared):
    return call(
        lambda *refs: finish(core(), *refs),
        (shape(COLS * GROUPS, LANES), shape(COLS, WIDTH)),
        [scratch(*dims) for dims in RESULTS]
        + [scratch(COLS * GROUPS, LANES), scratch(COLS, WIDTH), pltpu.SemaphoreType.DMA((5,))],
        [VMEM] * 12,
        (HBM, HBM),
    )(other, *prepared)


def on_device(ensemble, decay_rate, innovation, obs_weight):
    args = (ensemble, decay_rate, innovation, obs_weight)
    core = lambda: lax.axis_index("core")
    sent = pack_call(lambda: 8 * lax.axis_index("core") + lax.axis_index("y"), *args)
    received = lax.all_to_all(sent, ("core", "y", "z", "x"), 0, 0, tiled=True)
    results = own_call(received).reshape(CHIPS, 2 * LANES)
    returned = lax.all_to_all(results, ("x", "y", "z"), 0, 0, tiled=True).reshape(DEVICES, LANES)
    other = lax.ppermute(returned, "core", [(0, 1), (1, 0)])
    control, increment = finish_call(core, other, prepare_call(core, returned, *args))
    return control.reshape(1, COLS, WIDTH), increment


def solution(mesh):
    chips = jax.sharding.Mesh(mesh.devices.reshape(MEMBERS // 2, 2, ZS, XS), ("y", "core", "z", "x"))
    whole, field = P(("y", "core"), ("z", "x"), None), P(("z", "x"), None)
    return jax.shard_map(
        on_device, mesh=chips, in_specs=(whole, field, field, field), out_specs=(whole, field), check_vma=False
    )
```

```python
import jax
import jax.numpy as jnp
from jax import lax
from jax.experimental import pallas as pl
from jax.experimental.pallas import tpu as pltpu
from jax.sharding import PartitionSpec as P

MEMBERS, TILES, COLS, LINES = 16, 32, 28, 4
XS, ZS = 4, 8
DEVICES = MEMBERS * TILES
ROWS = 32
LANES = 128
BLOCKS = DEVICES // LANES
GROUPS = LINES * BLOCKS
WIDTH = LINES * DEVICES
CHIPS, HALF = DEVICES // 2, WIDTH // 2
SEGMENT = 7
SEGMENTS = [range(start, start + SEGMENT) for start in range(0, COLS, SEGMENT)]
SCALARS = tuple(line * ROWS + COLS + 2 for line in range(LINES)) + (COLS + 3,)
VMEM = pl.BlockSpec(memory_space=pltpu.VMEM)
HBM = pl.BlockSpec(memory_space=pltpu.HBM)


def lane_block(line, block):
    start = (block // 2) * HALF + line * CHIPS + (block % 2) * LANES
    return slice(start, start + LANES)


def pack(place, ensemble_hbm, decay_hbm, innovation_hbm, weight_hbm, out_ref,
         ensemble_ref, weight_ref, eight_ref, last_ref, rows_ref, sems):
    quarter = lax.rem(place, 8)
    start = pl.multiple_of(8 * jnp.minimum(lax.div(quarter, 2), 2), 8)
    pairs = [(ensemble_hbm, ensemble_ref), (weight_hbm, weight_ref)]
    for i, hbm in enumerate((decay_hbm, innovation_hbm)):
        pairs.append((hbm.at[pl.ds(start, 8), :], eight_ref.at[i]))
        pairs.append((hbm.at[COLS - 4 : COLS, :], last_ref.at[i]))
    copies = [pltpu.make_async_copy(*pair, sems.at[i]) for i, pair in enumerate(pairs)]
    for copy in copies:
        copy.start()
    for copy in copies:
        copy.wait()
    rows_ref[:COLS, :] = ensemble_ref[0].astype(jnp.float32) * jnp.sqrt(weight_ref[...])

    def four(eight, last):
        inner = jnp.where(lax.rem(quarter, 2) == 0, eight[:4], eight[4:])
        return jnp.where(quarter >= 6, last, inner)

    scaled = jnp.sqrt(four(weight_ref[pl.ds(start, 8), :], weight_ref[COLS - 4 :, :])) * four(eight_ref[1], last_ref[1])
    rows_ref[COLS:, :] = jnp.where(place < 8, four(eight_ref[0], last_ref[0]), scaled)
    for block in range(BLOCKS):
        piece = jnp.concatenate([rows_ref[:, lane_block(line, block)] for line in range(LINES)], axis=0).T
        for half in range(2):
            x = 2 * (block % 2) + half
            to = pl.ds((block // 2) * CHIPS + x, CHIPS // XS, stride=XS)
            out_ref[to, :] = piece[half * CHIPS // XS : (half + 1) * CHIPS // XS]


def balanced(join, terms):
    while len(terms) > 1:
        terms = [join(*terms[i : i + 2]) if i + 1 < len(terms) else terms[i] for i in range(0, len(terms), 2)]
    return terms[0]


def add(x, y):
    return x + y


def spread(piece, lane_group):
    turned = [piece] + [pltpu.roll(piece, 32 * k, 1) for k in (1, 2, 3)]
    out = []
    for source in range(4):
        value = turned[(3 - source) % 4]
        for group in (2, 1, 0):
            value = jnp.where(lane_group == group, turned[(group - source) % 4], value)
        out.append(value)
    return out


def own_lines(in_ref, out_ref, rows_ref, members_ref, fields_ref, state_ref, first_ref):
    for block in range(BLOCKS):
        piece = slice(block * LANES, (block + 1) * LANES)
        rows_ref[piece, :] = in_ref[piece, :].T

    lane = lax.broadcasted_iota(jnp.int32, (8, LANES), 1)
    sub = lax.broadcasted_iota(jnp.int32, (8, LANES), 0)
    tile, lane_group = lane % TILES, lane // TILES
    low = sub < 4
    zero = jnp.zeros((8, LANES), jnp.float32)

    for c in range(COLS):
        value = rows_ref[pl.ds(c, 16, stride=ROWS), :]
        members_ref[c, 0], members_ref[c, 1] = value[:8], value[8:]

    RATE, SQUARED, AFTER, UPTO, INNOV, Z0, Z1 = range(7)

    def field(kind, c):
        return fields_ref[kind, c]

    for j in range(4):
        given = rows_ref[pl.ds(COLS + j, 16, stride=ROWS), :]
        for kind, value in ((RATE, given[:8]), (INNOV, given[8:])):
            other = pltpu.roll(value, 4, 0)
            for half, both in enumerate((jnp.where(low, value, other), jnp.where(low, other, value))):
                for source, copied in enumerate(spread(both, lane_group)):
                    c = 16 * half + 4 * source + j
                    if c < COLS:
                        fields_ref[kind, c] = copied

    one = zero + 1.0
    parts = []
    for columns in SEGMENTS:
        upto, after = one, one
        for c in columns:
            rate = field(RATE, c)
            fields_ref[SQUARED, c] = (1.0 - rate) * (1.0 + rate)
            upto = upto * rate
            fields_ref[UPTO, c] = upto
        for c in reversed(columns):
            fields_ref[AFTER, c] = after
            after = after * field(RATE, c)
        parts.append(upto)
    upto = balanced(lambda x, y: x * y, parts)

    def turn(value, k, backward):
        return pltpu.roll(value, LANES - k if backward else k, 1)

    def inside(k, backward):
        return tile < TILES - k if backward else tile >= k

    def factors(backward):
        out, product = [], one
        for k in range(1, TILES):
            out.append((k, jnp.where(inside(k, backward), product, 0.0)))
            product = product * turn(upto, k, backward)
        return out

    chains = {backward: factors(backward) for backward in (True, False)}

    def entering(values, backward):
        return [
            balanced(add, [factor * turn(value, k, backward) for k, factor in chains[backward]]) for value in values
        ]

    def through(ends, products, start):
        states = [start]
        for end, product in zip(ends, products):
            states.append(end if states[-1] is None else end + product * states[-1])
        return states

    def apply(source, target, on_state, on_field):
        ends = [[], []]
        for columns in reversed(SEGMENTS):
            carry = [None, None]
            for c in reversed(columns):
                rate, weight = field(RATE, c), field(source, c)
                for i in range(2):
                    summed = members_ref[c, i] * weight
                    summed = summed if carry[i] is None else summed + carry[i]
                    state_ref[c, i] = summed
                    carry[i] = rate * summed
            for i in range(2):
                ends[i].append(carry[i])
        from_right = entering([through(ends[i], parts[::-1], None)[-1] for i in range(2)], True)
        starts = [through(ends[i], parts[::-1], from_right[i])[:-1][::-1] for i in range(2)]
        ends = [[], []]
        for s, columns in enumerate(SEGMENTS):
            state = [None, None]
            for c in columns:
                rate, squared, after = field(RATE, c), field(SQUARED, c), field(AFTER, c)
                for i in range(2):
                    summed = state_ref[c, i] + after * starts[i][s]
                    driven = squared * summed
                    on_state(c, i, summed, driven)
                    state[i] = driven if state[i] is None else rate * state[i] + driven
                    state_ref[c, i] = state[i]
            for i in range(2):
                ends[i].append(state[i])
        from_left = entering([through(ends[i], parts, None)[-1] for i in range(2)], False)
        starts = [through(ends[i], parts, from_left[i])[:-1] for i in range(2)]
        for s, columns in reversed(list(enumerate(SEGMENTS))):
            for c in reversed(columns):
                upto = field(UPTO, c)
                total = add(*(members_ref[c, i] * (state_ref[c, i] + upto * starts[i][s]) for i in range(2)))
                total = total + pltpu.roll(total, 4, 0)
                total = total + pltpu.roll(total, 64, 1)
                total = total + pltpu.roll(total, 32, 1)
                fields_ref[target, c] = total
                on_field(c, total)
        return from_right

    def whole(value):
        return jnp.sum(jnp.sum(value, axis=0, keepdims=True), axis=1, keepdims=True)

    sums = {name: zero for name in ("alpha", "beta", "kappa", "energy", "cross")}

    def keep(c, i, summed, driven):
        first_ref[c, i] = summed
        sums["alpha"] += summed * driven

    def square(c, total):
        sums["beta"] += total * total

    right0 = apply(INNOV, Z0, keep, square)
    alpha = whole(sums["alpha"])
    beta = 0.125 * whole(sums["beta"])
    ratio = jnp.where(alpha > 0.0, beta / jnp.where(alpha > 0.0, alpha, 1.0), 0.0)
    ratio = jnp.broadcast_to(ratio, (8, LANES))

    def orthogonal(c, i, summed, driven):
        part = summed - ratio * first_ref[c, i]
        sums["kappa"] += field(SQUARED, c) * part * part

    def put(row, values):
        rows_ref[pl.ds(row, 16, stride=ROWS), :] = jnp.concatenate(values, axis=0)

    def compare(c, total):
        part = total - ratio * field(Z0, c)
        sums["energy"] += part * part
        sums["cross"] += part * field(Z0, c)
        put(c, [field(Z0, c), total])

    put(COLS, right0)
    put(COLS + 1, apply(Z0, Z1, orthogonal, compare))
    scalars = (alpha, beta, whole(sums["kappa"]), 0.125 * whole(sums["energy"]), 0.125 * whole(sums["cross"]))
    row = lax.broadcasted_iota(jnp.int32, (1, LANES), 1)
    last = jnp.zeros((1, LANES), jnp.float32)
    for place, value in zip(SCALARS, scalars):
        last = jnp.where(row == place, value, last)
    last = jnp.broadcast_to(last, (LANES, LANES))
    ours = lax.broadcasted_iota(jnp.int32, (LANES, LANES), 1) % ROWS >= COLS + 2
    for block in range(BLOCKS):
        piece = rows_ref[block * LANES : (block + 1) * LANES, :].T
        here = slice(block * LANES, (block + 1) * LANES)
        rows_ref[here, :] = jnp.where(ours, last, piece)
        for x in range(XS):
            from_x = rows_ref[pl.ds(block * LANES + x, LANES // XS, stride=XS), :]
            to = pl.ds(2 * (x * CHIPS // XS + (block % 2) * LANES // XS) + block // 2, LANES // XS, stride=2)
            out_ref[to, :] = from_x


def factors_of(at, ensemble_ref, decay_ref, innovation_ref, weight_ref, refs):
    inverse_ref, vector_ref, factor_ref, rate_ref, amplitude_ref, after_ref = refs
    for g in range(8):
        here = pl.ds(pl.multiple_of(at + g * LANES, LANES), LANES)
        group = pl.ds(g, COLS, stride=8)
        root = jnp.sqrt(weight_ref[:, here])
        inverse_ref[:COLS, g * LANES : (g + 1) * LANES] = 1.0 / root
        factor = ensemble_ref[0, :, here].astype(jnp.float32) * root
        vector_ref[group, :] = factor * (root * innovation_ref[:, here])
        factor_ref[group, :] = factor
        rate = decay_ref[:, here]
        rate_ref[group, :] = rate
        amplitude_ref[group, :] = jnp.sqrt((1.0 - rate) * (1.0 + rate))
    for columns in SEGMENTS:
        after = jnp.ones((8, LANES), jnp.float32)
        for c in reversed(columns):
            part = slice(8 * c, 8 * c + 8)
            after_ref[part, :] = after
            after = after * rate_ref[part, :]


def one_half(core, in_ref, field0_ref, field1_ref, vector0_ref, vector1_ref, scalars_ref,
             inverse_ref, vector_ref, factor_ref, rate_ref, amplitude_ref, after_ref):
    rows = [None] * 8
    for j in range(2):
        pieces = [in_ref[pl.ds(2 * j * LANES + h, LANES, stride=2), :].T for h in range(2)]
        for line in range(LINES):
            g = 2 * line + j
            part = slice(g * LANES, (g + 1) * LANES)
            z0, z1 = (piece[line * ROWS : line * ROWS + COLS] for piece in pieces)
            inverse = inverse_ref[:COLS, part]
            field0_ref[:COLS, part] = inverse * z0
            field1_ref[:COLS, part] = inverse * z1
            vector1_ref[pl.ds(g, COLS, stride=8), :] = z0
            states = [piece[line * ROWS + COLS : line * ROWS + COLS + 2] for piece in pieces]
            rows[g] = jnp.where(core == 0, *states)
        for i, place in enumerate(SCALARS):
            scalars_ref[i : i + 1, j * LANES : (j + 1) * LANES] = pieces[0][place : place + 1]
    entering = [jnp.concatenate([row[i : i + 1] for row in rows], axis=0) for i in range(2)]
    for columns in reversed(SEGMENTS):
        carry = [None, None]
        for c in reversed(columns):
            part = slice(8 * c, 8 * c + 8)
            for i, value in enumerate((vector_ref[part, :], factor_ref[part, :] * vector1_ref[part, :])):
                summed = value if carry[i] is None else value + carry[i]
                carry[i] = rate_ref[part, :] * summed
                (vector0_ref, vector1_ref)[i][part, :] = summed
        for c in columns:
            part = slice(8 * c, 8 * c + 8)
            for ref, state in zip((vector0_ref, vector1_ref), entering):
                ref[part, :] = amplitude_ref[part, :] * (ref[part, :] + after_ref[part, :] * state)
        first = slice(8 * columns[0], 8 * columns[0] + 8)
        product = rate_ref[first, :] * after_ref[first, :]
        entering = [end + product * state for end, state in zip(carry, entering)]


def prepare(core, in_ref, *refs):
    args, half, other, own = refs[:4], refs[4:9], refs[9:15], refs[15:]
    factors_of(core * HALF, *args, own)
    one_half(core, in_ref, *half, *own)
    factors_of((1 - core) * HALF, *args, other)


def finish(core, in_ref, *refs):
    own, factors = refs[:5], refs[5:11]
    control_hbm, increment_hbm = refs[11:13]
    other = refs[13:18]
    control_ref, increment_ref, sems = refs[18:]
    one_half(core, in_ref, *other, *factors)

    def whole(value):
        return jnp.sum(value, axis=1, keepdims=True)

    def both(i):
        return jnp.concatenate([ref[i : i + 1, :] for ref in (own[4], other[4])], axis=1)

    alphas, betas, kappas, energies, crosses = (both(i) for i in range(5))
    alpha, beta = whole(alphas), whole(betas)
    ratio = beta / alpha
    shift = jnp.where(alphas > 0.0, betas / jnp.where(alphas > 0.0, alphas, 1.0), 0.0) - ratio
    kappa = whole(kappas + alphas * shift * shift)
    energy = whole(energies + shift * (2.0 * crosses + shift * betas))
    step = alpha / (alpha + beta)
    curvature = kappa + energy - step * kappa * (kappa / alpha)
    back = jnp.where(curvature > 0.0, step * kappa / jnp.where(curvature > 0.0, curvature, 1.0), 0.0)
    ahead = step + back * (ratio + step * (kappa / alpha))

    copies = []

    def send(source, target):
        copies.append(pltpu.make_async_copy(source, target, sems.at[len(copies)]))
        copies[-1].start()

    for quarter in range(4):
        for c in range(7 * quarter, 7 * quarter + 7):
            for at, (_, _, vector0_ref, vector1_ref, _) in ((core, own), (1 - core, other)):
                part = slice(8 * c, 8 * c + 8)
                here = pl.ds(pl.multiple_of(c * GROUPS + 8 * at, 8), 8)
                control_ref[here, :] = ahead * vector0_ref[part, :] - back * vector1_ref[part, :]
        part = slice(7 * quarter * GROUPS, (7 * quarter + 7) * GROUPS)
        send(control_ref.at[part, :], control_hbm.at[part, :])
    for at, (field0_ref, field1_ref, *_) in ((core, own), (1 - core, other)):
        here = pl.ds(pl.multiple_of(at * HALF, HALF), HALF)
        increment_ref[:, here] = ahead * field0_ref[:COLS, :] - back * field1_ref[:COLS, :]
    send(increment_ref, increment_hbm)
    for copy in copies:
        copy.wait()


def shape(*dims):
    return jax.ShapeDtypeStruct(dims, jnp.float32)


def scratch(*dims):
    return pltpu.VMEM(dims, jnp.float32)


def call(kernel, out_shape, scratch_shapes, in_specs, out_specs):
    return pl.pallas_call(
        kernel,
        out_shape=out_shape,
        in_specs=in_specs,
        out_specs=out_specs,
        scratch_shapes=scratch_shapes,
        compiler_params=pltpu.CompilerParams(vmem_limit_bytes=32 * 1024 * 1024),
    )


def pack_call(place, *args):
    return call(
        lambda *refs: pack(place(), *refs),
        shape(DEVICES, LANES),
        [pltpu.VMEM((1, COLS, WIDTH), jnp.bfloat16)]
        + [scratch(COLS, WIDTH), scratch(2, 8, WIDTH), scratch(2, 4, WIDTH)]
        + [scratch(ROWS, WIDTH), pltpu.SemaphoreType.DMA((6,))],
        [HBM] * 4,
        VMEM,
    )(*(pltpu.with_memory_space_constraint(value, pltpu.HBM) for value in args))


def own_call(received):
    return call(
        own_lines,
        shape(DEVICES, LANES),
        [
            scratch(DEVICES, LANES),
            scratch(COLS, 2, 8, LANES),
            scratch(7, COLS, 8, LANES),
            scratch(COLS, 2, 8, LANES),
            scratch(COLS, 2, 8, LANES),
        ],
        [VMEM],
        VMEM,
    )(received)


BY_COLUMN = (ROWS * 8, LANES)
RESULTS = ((ROWS, HALF), (ROWS, HALF), BY_COLUMN, BY_COLUMN, (8, CHIPS))
FACTORS = ((ROWS, HALF), BY_COLUMN, BY_COLUMN, BY_COLUMN, BY_COLUMN, BY_COLUMN)


def prepare_call(core, returned, *args):
    return call(
        lambda *refs: prepare(core(), *refs),
        tuple(shape(*dims) for dims in RESULTS + FACTORS),
        [scratch(*dims) for dims in FACTORS],
        [VMEM] * 5,
        (VMEM,) * 11,
    )(returned, *args)


def finish_call(core, other, prepared):
    return call(
        lambda *refs: finish(core(), *refs),
        (shape(COLS * GROUPS, LANES), shape(COLS, WIDTH)),
        [scratch(*dims) for dims in RESULTS]
        + [scratch(COLS * GROUPS, LANES), scratch(COLS, WIDTH), pltpu.SemaphoreType.DMA((5,))],
        [VMEM] * 12,
        (HBM, HBM),
    )(other, *prepared)


def on_device(ensemble, decay_rate, innovation, obs_weight):
    args = (ensemble, decay_rate, innovation, obs_weight)
    core = lambda: lax.axis_index("core")
    sent = pack_call(lambda: 8 * lax.axis_index("core") + lax.axis_index("y"), *args)
    received = lax.all_to_all(sent, ("core", "y", "z", "x"), 0, 0, tiled=True)
    results = own_call(received).reshape(CHIPS, 2 * LANES)
    returned = lax.all_to_all(results, ("x", "y", "z"), 0, 0, tiled=True).reshape(DEVICES, LANES)
    other = lax.ppermute(returned, "core", [(0, 1), (1, 0)])
    control, increment = finish_call(core, other, prepare_call(core, returned, *args))
    return control.reshape(1, COLS, WIDTH), increment


def solution(mesh):
    chips = jax.sharding.Mesh(mesh.devices.reshape(MEMBERS // 2, 2, ZS, XS), ("y", "core", "z", "x"))
    whole, field = P(("y", "core"), ("z", "x"), None), P(("z", "x"), None)
    return jax.shard_map(
        on_device, mesh=chips, in_specs=(whole, field, field, field), out_specs=(whole, field), check_vma=False
    )
```
